128 devices in a mesh: gx: 16 (over z, x), gy: 8 (over y, core).
Axes of the slice: x: 4, y: 4, z: 4, core: 2. Of those that a mesh axis runs over, the one named last changes fastest.
Arguments:
- pressure: float32 [262144, 512], P(('gx', 'gy')), may hold values from -3 to -0.05
- soil_class: int32 [262144], P(('gx', 'gy')), may hold values from 0 to 11
- levels: int32 [262144], P(('gx', 'gy')), may hold values from 0 to 2
- neighbors: int32 [262144, 6], P(('gx', 'gy')), may hold values from -1 to 262143, as said below
- neighbor_levels: int32 [262144, 6], P(('gx', 'gy')), may hold values from 0 to 2, as said below
- patch_of_block: int32 [262144], P(('gx', 'gy')), may hold values from -1 to 65535, as said below
- soil_params: float32 [5, 12], replicated, as said below
- water_depth: float32 [2048, 2048], P('gx', 'gy'), may hold values from 0.0001 to 0.3
- bed_height: float32 [2048, 2048], P('gx', 'gy'), may hold values from -1 to 1
- roughness: float32 [2048, 2048], P('gx', 'gy'), may hold values from 0.02 to 0.2
Outputs:
- new_pressure: float32 [262144, 512], P(('gx', 'gy'))
- new_depth: float32 [2048, 2048], P('gx', 'gy')
The draws below stay inside these ranges and needn't reach their ends.
Inputs may be any that keep to these rules, and one draw needn't show every extreme that they name: `patch_of_block`: every surface patch lies over exactly one block. The blocks under the patches of device d belong to the devices d - 8 to d + 16 / 2 - 1 (flat index gx index * 8 + gy index, modulo the device count). Among the blocks of one device at most 64 lie under the patches of any one device, and every device has exactly 64 patches over the blocks of some one device. `neighbors`: symmetric face relation (b's +x neighbour has b as its -x neighbour, likewise y and z); neighbour numbers differ from the block's by at most 256, and by exactly 256 for some; neighbours' levels differ by at most one; blocks with a patch have no +z neighbour. `neighbor_levels`: the level of the neighbour across each face, 0 where there is none. `soil_params`: 0.02 <= theta_r <= 0.1, 0.35 <= theta_s <= 0.5, 0.5 <= alpha <= 5, 1.3 <= n <= 2.8, 0.02 <= Ks <= 1.
All inputs are finite; a program needn't handle non-finite values.
Results may differ from the reference program's by a relative error of at most 0.0003.
Values sent between devices are 32-bit elements; how exact they have to be, the bound alone decides.
No kernel may reach another device: no remote copies, remote signals or barrier semaphores. Data moves between devices by JAX's collectives and lax.ppermute only.
A program may use at most 192 MiB of HBM per device.

```python
import math
import jax
import jax.numpy as jnp
from jax import lax

NSOIL = 12
HB = 256
NPIECE = 16
BLK_DEV = 2048
SX = 128
SY = 256
P_DEV = 512
CAP = 64
NBLK = 262144
NSX = 2048
NSY = 2048
N_GX = 16
N_GY = 8
DEVICES = 128


def octree_layout(key):
    key = jax.random.fold_in(key, 101)
    key_list = jax.random.split(key, 5)
    half_pieces = NPIECE // 2
    first_sizes = jax.random.randint(key_list[0], (DEVICES, half_pieces), 0, CAP + 1)
    first_sizes = first_sizes.at[:, 0].set(CAP)
    piece_sizes = jnp.stack([first_sizes, CAP - first_sizes], axis=-1).reshape(DEVICES, NPIECE)
    piece_starts = jnp.cumsum(piece_sizes, axis=1) - piece_sizes
    patch_order = jax.vmap(lambda k: jax.random.permutation(k, P_DEV))(jax.random.split(key_list[1], DEVICES))
    block_order = jax.vmap(lambda k: jax.random.permutation(k, BLK_DEV))(jax.random.split(key_list[2], DEVICES))
    target = jnp.arange(DEVICES)[:, None]
    piece_index = jnp.arange(NPIECE)[None, :]
    source = (target + piece_index - half_pieces) % DEVICES
    source_target = (target - piece_index + half_pieces) % DEVICES
    source_sizes = piece_sizes[source_target, piece_index]
    source_starts = jnp.cumsum(source_sizes, axis=1) - source_sizes
    within = jnp.arange(CAP)[None, None, :]
    is_valid = within < piece_sizes[:, :, None]
    patch_local = patch_order[target[:, :, None], jnp.minimum(piece_starts[:, :, None] + within, P_DEV - 1)]
    patch_global = target[:, :, None] * P_DEV + patch_local
    position = jnp.minimum(source_starts[source, piece_index][:, :, None] + within, BLK_DEV - 1)
    block_global = source[:, :, None] * BLK_DEV + block_order[source[:, :, None], position]
    top_patch = jnp.full((NBLK,), -1, jnp.int32).at[jnp.where(is_valid, block_global, NBLK).reshape(-1)].set(patch_global.reshape(-1).astype(jnp.int32), mode='drop')
    levels = jax.random.randint(key_list[3], (NBLK,), 0, 3)
    blocks = jnp.arange(NBLK)
    neighbors = jnp.full((NBLK, 6), -1, jnp.int32)
    for axis_number, reach_size in enumerate((max(2, HB // 8), max(2, HB // 2), HB)):
        window = reach_size + 1
        windows = -(-NBLK // window)
        window_keys = jax.random.split(jax.random.fold_in(key_list[4], axis_number), windows)
        middle = jax.vmap(lambda k: jax.random.permutation(k, reach_size - 1))(window_keys) + 1
        pair_count = (reach_size - 1) // 2
        low_end = middle[:, 0:2 * pair_count:2]
        high_end = middle[:, 1:2 * pair_count:2]
        partner = jnp.full((windows, window), -1, jnp.int32)
        partner = partner.at[:, 0].set(reach_size).at[:, reach_size].set(0)
        window_rows = jnp.arange(windows)[:, None]
        partner = partner.at[window_rows, low_end].set(high_end).at[window_rows, high_end].set(low_end)
        window_base = jnp.arange(windows)[:, None] * window
        partner = jnp.where(partner >= 0, partner + window_base, -1).reshape(-1)[:NBLK]
        partner = jnp.where(partner < NBLK, partner, -1)
        safe_index = jnp.clip(partner, 0, NBLK - 1)
        keep_pair = (partner >= 0) & (jnp.abs(levels - levels[safe_index]) <= 1)
        if axis_number == 2:
            keep_pair = keep_pair & (top_patch[jnp.minimum(blocks, safe_index)] < 0)
        neighbors = neighbors.at[:, 2 * axis_number].set(jnp.where(keep_pair & (partner < blocks), partner, -1))
        neighbors = neighbors.at[:, 2 * axis_number + 1].set(jnp.where(keep_pair & (partner > blocks), partner, -1))
    neighbor_levels = jnp.where(neighbors >= 0, levels[jnp.clip(neighbors, 0, NBLK - 1)], 0)
    return (top_patch, levels.astype(jnp.int32), neighbors.astype(jnp.int32), neighbor_levels.astype(jnp.int32))


def draw_patch_of_block(key, part):
    shared = octree_layout(key)
    return shared[0]


def draw_levels(key, part):
    shared = octree_layout(key)
    return shared[1]


def draw_neighbors(key, part):
    shared = octree_layout(key)
    return shared[2]


def draw_neighbor_levels(key, part):
    shared = octree_layout(key)
    return shared[3]


def draw_soil_params(key, part):
    key = jax.random.fold_in(key, 7)
    unit_draw = jax.random.uniform(key, (5, NSOIL), jnp.float32)
    residual_water = 0.02 + 0.08 * unit_draw[0]
    saturated_water = 0.35 + 0.15 * unit_draw[1]
    air_entry = 0.5 * jnp.exp(unit_draw[2] * jnp.log(10.0))
    shape_power = 1.3 + 1.5 * unit_draw[3]
    saturated_cond = 0.02 * jnp.exp(unit_draw[4] * jnp.log(50.0))
    return jnp.stack([residual_water, saturated_water, air_entry, shape_power, saturated_cond]).astype(jnp.float32)


def plant(drawn, rng, least, top_value):
    extent = drawn.shape
    index_at = [jax.random.randint(jax.random.fold_in(rng, axis), (), 0, extent[axis]) for axis in range(len(extent))]
    drawn = drawn.at[tuple(index_at)].set(least)
    longest = extent.index(max(extent))
    index_at[longest] = (index_at[longest] + 1) % extent[longest]
    return drawn.at[tuple(index_at)].set(top_value)


def block_scale(rng, dims, cuts, smallest, top_value):
    factor_of, own = 1.0, jax.random.fold_in(rng, 6)
    for dim, blocks in cuts:
        steps = jnp.exp(jax.random.uniform(jax.random.fold_in(own, dim), (blocks,), jnp.float32, smallest / len(cuts), top_value / len(cuts)))
        factor_of = factor_of * jnp.repeat(steps, dims[dim] // blocks).reshape([-1 if axis == dim else 1 for axis in range(len(dims))])
    return factor_of


def centred(rng, dims, scale, bound, shards=(), kind=jnp.bfloat16):
    loudness = block_scale(rng, dims, shards, -0.22, 0.18) if shards else 1.0
    values = jax.random.normal(rng, dims, jnp.float32) * scale * loudness
    return jnp.minimum(jnp.maximum(values, -bound), bound).astype(kind)


def setup_inputs(seed: int = 0) -> dict:
    keys = jax.random.split(jax.random.key(seed), 11)
    return {
        "pressure": jnp.clip(-3.0 + 2.95 * jax.random.uniform(keys[0], (NBLK, 512), jnp.float32) ** block_scale(keys[0], (NBLK, 512), ((0, 128),), -0.2, 0.2), -3.0, -0.05),
        "soil_class": plant(jax.random.randint(keys[1], (NBLK,), 0, NSOIL), jax.random.fold_in(keys[1], 1), 0, NSOIL - 1).astype(jnp.int32),
        "levels": draw_levels(jax.random.fold_in(keys[10], 71), 0),
        "neighbors": draw_neighbors(jax.random.fold_in(keys[10], 71), 0),
        "neighbor_levels": draw_neighbor_levels(jax.random.fold_in(keys[10], 71), 0),
        "patch_of_block": draw_patch_of_block(jax.random.fold_in(keys[10], 71), 0),
        "soil_params": draw_soil_params(jax.random.fold_in(keys[10], 71), 0),
        "water_depth": jnp.clip(jnp.exp(math.log(0.3) - 8.006368 * jax.random.uniform(keys[7], (NSX, NSY), jnp.float32) ** block_scale(keys[7], (NSX, NSY), ((0, 16), (1, 8)), -0.2, 0.2)), 0.0001, 0.3),
        "bed_height": centred(keys[8], (NSX, NSY), 0.2, 1.0, ((0, 16), (1, 8)), jnp.float32),
        "roughness": jnp.clip(jnp.exp(math.log(0.2) - 2.3025851 * jax.random.uniform(keys[9], (NSX, NSY), jnp.float32) ** block_scale(keys[9], (NSX, NSY), ((0, 16), (1, 8)), -0.2, 0.2)), 0.02, 0.2),
    }


CELL_BASE = 0.25
STORAGE = 0.05
SUB_STEP = 0.02
SURF_STEP = 0.003
SURF_CELL = 1.0
SLOPE_FLOOR = 0.01
OPPOSITE = (1, 0, 3, 2, 5, 4)
GRAVITY = (0.0, 0.0, 0.0, 0.0, -1.0, 1.0)

def van_genuchten(pressure, params):
    residual_water = params[:, 0:1]
    saturated_water = params[:, 1:2]
    air_entry = params[:, 2:3]
    shape_power = params[:, 3:4]
    saturated_cond = params[:, 4:5]
    exponent = 1.0 - 1.0 / shape_power
    suction = air_entry * jnp.maximum(-pressure, 0.0)
    powered = jnp.power(suction, shape_power)
    window_base = 1.0 + powered
    saturation = jnp.power(window_base, -exponent)
    pore_ratio = powered / window_base
    conductivity = saturated_cond * jnp.sqrt(saturation) * jnp.square(1.0 - jnp.power(pore_ratio, exponent))
    capacity = (saturated_water - residual_water) * air_entry * exponent * shape_power * jnp.power(suction, shape_power - 1.0) * jnp.power(window_base, -exponent - 1.0) + STORAGE
    return (conductivity, capacity)

def pack_faces(pressure, conductivity):
    block_count = pressure.shape[0]

    def faces_of(field):
        field_cube = field.reshape(block_count, 8, 8, 8)
        sides = (field_cube[:, :, :, 0], field_cube[:, :, :, 7], field_cube[:, :, 0, :], field_cube[:, :, 7, :], field_cube[:, 0], field_cube[:, 7])
        return jnp.stack([side.reshape(block_count, 64) for side in sides], axis=1)
    return jnp.stack([faces_of(pressure), faces_of(conductivity)], axis=2).reshape(block_count, 768)

def richards_update(pressure, conductivity, capacity, spacing, neighbors, neighbor_levels, top_flux, own_faces, far_faces):
    block_count = pressure.shape[0]
    head_cube = pressure.reshape(block_count, 8, 8, 8)
    cond_cube = conductivity.reshape(block_count, 8, 8, 8)
    cell_width = spacing[:, None, None, None]
    flux_i = 0.5 * (cond_cube[..., 1:] + cond_cube[..., :-1]) * (head_cube[..., 1:] - head_cube[..., :-1]) / cell_width
    flux_j = 0.5 * (cond_cube[:, :, 1:] + cond_cube[:, :, :-1]) * (head_cube[:, :, 1:] - head_cube[:, :, :-1]) / cell_width
    flux_k = 0.5 * (cond_cube[:, 1:] + cond_cube[:, :-1]) * ((head_cube[:, 1:] - head_cube[:, :-1]) / cell_width + 1.0)
    inflow = jnp.pad(flux_i, ((0, 0), (0, 0), (0, 0), (0, 1))) - jnp.pad(flux_i, ((0, 0), (0, 0), (0, 0), (1, 0))) + jnp.pad(flux_j, ((0, 0), (0, 0), (0, 1), (0, 0))) - jnp.pad(flux_j, ((0, 0), (0, 0), (1, 0), (0, 0))) + jnp.pad(flux_k, ((0, 0), (0, 1), (0, 0), (0, 0))) - jnp.pad(flux_k, ((0, 0), (1, 0), (0, 0), (0, 0)))
    own_split = own_faces.reshape(block_count, 6, 2, 64)
    far_width = CELL_BASE * jnp.exp2(neighbor_levels.astype(jnp.float32))
    face_gap = 0.5 * (spacing[:, None] + far_width)
    gravity = jnp.array(GRAVITY, jnp.float32)
    across = 0.5 * (own_split[:, :, 1] + far_faces[:, :, 64:]) * ((far_faces[:, :, :64] - own_split[:, :, 0]) / face_gap[:, :, None] + gravity[None, :, None])
    across = jnp.where((neighbors >= 0)[:, :, None], across, 0.0)
    across = across.at[:, 5].add(top_flux)
    face_sheet = across.reshape(block_count, 6, 8, 8)
    inflow = inflow.at[:, :, :, 0].add(face_sheet[:, 0]).at[:, :, :, 7].add(face_sheet[:, 1])
    inflow = inflow.at[:, :, 0, :].add(face_sheet[:, 2]).at[:, :, 7, :].add(face_sheet[:, 3])
    inflow = inflow.at[:, 0].add(face_sheet[:, 4]).at[:, 7].add(face_sheet[:, 5])
    return pressure + SUB_STEP * inflow.reshape(block_count, 512) / (spacing[:, None] * capacity)

def overland_sweep(head_ext, bed_ext, rough_ext, source, row_start, col_start, rows_total, cols_total):
    row_count, col_count = head_ext.shape
    wet_depth = jnp.maximum(head_ext, 0.0)
    section = head_ext + bed_ext

    def face_flux(wet_a, wet_b, section_a, section_b, rough_a, rough_b):
        surface_slope = (section_b - section_a) / SURF_CELL
        mean_depth = 0.5 * (wet_a + wet_b)
        return jnp.power(mean_depth, 5.0 / 3.0) / (0.5 * (rough_a + rough_b)) * surface_slope / jnp.sqrt(jnp.abs(surface_slope) + SLOPE_FLOOR)
    row_flux = face_flux(wet_depth[:-1], wet_depth[1:], section[:-1], section[1:], rough_ext[:-1], rough_ext[1:])
    row_ids = row_start + jnp.arange(row_count - 1)
    inside = (row_ids >= 0) & (row_ids + 1 < rows_total)
    row_flux = jnp.where(inside[:, None], row_flux, 0.0)
    col_flux = face_flux(wet_depth[:, :-1], wet_depth[:, 1:], section[:, :-1], section[:, 1:], rough_ext[:, :-1], rough_ext[:, 1:])
    col_ids = col_start + jnp.arange(col_count - 1)
    inside_cols = (col_ids >= 0) & (col_ids + 1 < cols_total)
    col_flux = jnp.where(inside_cols[None, :], col_flux, 0.0)
    net_inflow = row_flux[1:, 1:-1] - row_flux[:-1, 1:-1] + col_flux[1:-1, 1:] - col_flux[1:-1, :-1]
    return head_ext[1:-1, 1:-1] + SURF_STEP * (net_inflow / SURF_CELL - source)

def reference(pressure, soil_class, levels, neighbors, neighbor_levels, patch_of_block, soil_params, water_depth, bed_height, roughness):
    groups = N_GX * N_GY
    block_total = groups * BLK_DEV
    params = jnp.transpose(soil_params[:, soil_class])
    spacing = CELL_BASE * jnp.exp2(levels.astype(jnp.float32))

    def grouped(array):
        return array.reshape((groups, BLK_DEV) + array.shape[1:])
    conductivity, capacity = lax.map(lambda pair_items: van_genuchten(pair_items[0], pair_items[1]), (grouped(pressure), grouped(params)))
    conductivity = conductivity.reshape(block_total, 512)
    capacity = capacity.reshape(block_total, 512)
    face_table = lax.map(lambda pair_items: pack_faces(pair_items[0], pair_items[1]), (grouped(pressure), grouped(conductivity))).reshape(block_total, 768)
    half_cell = 0.5 * spacing[:, None]
    payload = jnp.concatenate([conductivity[:, 448:] / half_cell, pressure[:, 448:] - half_cell], axis=1)
    patch_total = groups * P_DEV
    is_top = patch_of_block >= 0
    patch_grid = jnp.zeros((patch_total, 128), jnp.float32).at[jnp.where(is_top, patch_of_block, patch_total)].set(payload, mode='drop')

    def to_surface(patch_part):
        return patch_part.reshape(N_GX, N_GY, SX // 8, SY // 8, 8, 8).transpose(0, 2, 4, 1, 3, 5).reshape(NSX, NSY)
    conductance = to_surface(patch_grid[:, :64])
    offset = to_surface(patch_grid[:, 64:])
    infiltration = jnp.minimum(conductance * (water_depth - offset), water_depth / (3.0 * SURF_STEP))
    surface_head = water_depth
    bed_padded = jnp.pad(bed_height, 1)
    rough_padded = jnp.pad(roughness, 1)
    for sweep_step in range(3):
        surface_head = overland_sweep(jnp.pad(surface_head, 1), bed_padded, rough_padded, infiltration, -1, -1, NSX, NSY)
    per_patch = infiltration.reshape(N_GX, SX // 8, 8, N_GY, SY // 8, 8).transpose(0, 3, 1, 4, 2, 5).reshape(patch_total, 64)
    top_flux = jnp.where(is_top[:, None], per_patch[jnp.clip(patch_of_block, 0, patch_total - 1)], 0.0)
    far_rows = (jnp.clip(neighbors, 0, block_total - 1) * 6 + jnp.array(OPPOSITE, jnp.int32)[None, :]).astype(jnp.int32)
    flat_faces = face_table.reshape(block_total * 6, 128)

    def update_group(block_items):
        return richards_update(block_items[0], block_items[1], block_items[2], block_items[3], block_items[4], block_items[5], block_items[6], block_items[7], flat_faces[block_items[8]])
    new_pressure = lax.map(update_group, tuple((grouped(array) for array in (pressure, conductivity, capacity, spacing, neighbors, neighbor_levels, top_flux, face_table, far_rows)))).reshape(block_total, 512)
    return (new_pressure, surface_head)
```

```python
import jax
import jax.numpy as jnp
from jax import lax
from jax.experimental import pallas as pl
from jax.experimental.pallas import tpu as pltpu
from jax.sharding import PartitionSpec as P

F32 = jnp.float32
BF16 = jnp.bfloat16
I32 = jnp.int32

HB = 256
TILE = 256
SLOTS = 64
GROUPS = 16
STORAGE = 0.05
SUB_STEP = 0.02
SURF_STEP = 0.003
SLOPE_FLOOR = 0.01
OPPOSITE = (1, 0, 3, 2, 5, 4)
GRAVITY = (0.0, 0.0, 0.0, 0.0, -1.0, 1.0)
MIB = 1024 * 1024

VMEM = pl.BlockSpec(memory_space=pltpu.VMEM)
SMEM = pl.BlockSpec(memory_space=pltpu.SMEM)


def split(value):
    high = value.astype(BF16)
    low = (value - high.astype(F32)).astype(BF16)
    return high, low


def iota(shape, dim):
    return lax.broadcasted_iota(I32, shape, dim)


def as_bf16(mask):
    return jnp.where(mask, 1.0, 0.0).astype(BF16)


def cell_width(levels):
    return jnp.where(levels == 0, 0.25, jnp.where(levels == 1, 0.5, 1.0)).astype(F32)


def soil_rows(soil_ref, classes):
    rows = []
    for row in range(5):
        value = jnp.full(classes.shape, soil_ref[row, 0], F32)
        for cls in range(1, soil_ref.shape[1]):
            value = jnp.where(classes == cls, soil_ref[row, cls], value)
        rows.append(value)
    residual, saturated, alpha, power, cond = rows
    exponent = 1.0 - 1.0 / power
    return alpha, power - 1.0, -0.5 * exponent, cond, (saturated - residual) * alpha * (exponent * power)


def curve(pressure, soil):
    alpha, lesser, half, _, _ = soil
    suction = alpha * jnp.maximum(-pressure, 0.0)
    powered = jnp.exp2(lesser * jnp.log2(suction))
    base = 1.0 + powered * suction
    root = jnp.exp2(half * jnp.log2(base))
    ratio = powered * (root * root)
    rest = 1.0 - ratio
    conductivity = soil[3] * root * (rest * rest)
    return conductivity, base, ratio


def face_rows(ref, half, face):
    if face < 2:
        return ref[half, pl.ds(7 * face, 64, stride=8), :]
    if face < 4:
        start = 56 * (face - 2)
        return jnp.concatenate([ref[half, 64 * k + start : 64 * k + start + 8, :] for k in range(8)], axis=0)
    start = 448 * (face - 4)
    return ref[half, start : start + 64, :]


def write_faces(head_ref, cond_ref, half, put):
    for face in range(6):
        head_high, head_low = split(face_rows(head_ref, half, face))
        cond_high, cond_low = split(face_rows(cond_ref, half, face))
        for part, value in enumerate((head_high, head_low, cond_high, cond_low)):
            put(256 * face + 64 * part, half, value)


def route_kernel(place_ref, meta_ref, top_ref, depth_ref, bed_ref, rough_ref,
                 send_ref, slot_ref, rows_ref, turned, packed, edges):
    own, gy = place_ref[0], place_ref[2]
    devices, width = place_ref[3], place_ref[4]
    blocks = meta_ref.shape[1]
    patch = meta_ref[2:3, :]
    is_top = patch >= 0
    safe = jnp.where(is_top, patch, 0)
    offset = lax.rem(lax.shift_right_logical(safe, 9) - own + (GROUPS // 2 - 1) + devices, devices) - (GROUPS // 2 - 1)
    column = gy + offset
    moved = (column < 0) | (column >= width)
    group = 2 * lax.rem(column + width, width) + moved.astype(I32)
    upper = as_bf16(iota((TILE, TILE), 0) < iota((TILE, TILE), 1))
    carry = jnp.zeros((GROUPS, 1), F32)
    for part in range(blocks // TILE):
        lanes = slice(part * TILE, (part + 1) * TILE)
        member = jnp.where(
            (iota((GROUPS, TILE), 0) == group[:, lanes]) & is_top[:, lanes], 1.0, 0.0
        )
        before = jnp.dot(member.astype(BF16), upper, preferred_element_type=F32) + carry
        rank = jnp.sum(member * before, axis=0, keepdims=True)
        carry = carry + jnp.sum(member, axis=1, keepdims=True)
        slot_ref[:, lanes] = jnp.where(
            is_top[:, lanes], group[:, lanes] * SLOTS + rank.astype(I32), -1
        )
        for half in (2 * part, 2 * part + 1):
            turned[half] = top_ref[128 * half : 128 * half + 128, :].T
    for half in range(blocks // 128):
        lanes = slice(128 * half, 128 * half + 128)
        heads = jnp.concatenate(
            [turned[half, pl.ds(64 + i, 8, stride=8), :] for i in range(8)], axis=0
        )
        high, low = split(heads)
        packed[0:64, lanes] = high
        packed[64:128, lanes] = low
    place = jnp.bitwise_and(safe, 511)
    row = iota((16, blocks), 0)
    tags = jnp.where(row == 0, jnp.bitwise_and(place, 255), 0)
    tags = jnp.where(row == 1, lax.shift_right_logical(place, 8), tags)
    tags = jnp.where(row == 2, 1, tags)
    tags = jnp.where(row == 3, meta_ref[0:1, :], tags)
    tags = jnp.where(row == 4, meta_ref[1:2, :], tags)
    packed[128:144, :] = tags.astype(F32).astype(BF16)
    for number, field in enumerate((depth_ref, bed_ref, rough_ref)):
        edges[0, 3 * number : 3 * number + 3, :] = field[:, 0:128].T[0:3, :]
        edges[1, 3 * number : 3 * number + 3, :] = field[:, 128:256].T[125:128, :]
        for half in range(2):
            at = 3 * (2 * number + half)
            lanes = slice(128 * half, 128 * half + 128)
            rows_ref[0, at : at + 3, :] = field[0:3, lanes]
            rows_ref[1, at : at + 3, :] = field[125:128, lanes]
    low_lane = iota((32, 128), 1) < 64
    slot = slot_ref[...]

    def chunk(number, _):
        wanted = as_bf16(iota((128, blocks), 0) + 128 * number == slot)
        out = lax.dot_general(packed[...], wanted, (((1,), (1,)), ((), ())), preferred_element_type=F32)
        first = out[0:32] + out[64:96]
        second = out[32:64] + out[96:128]
        send_ref[number, 0:32, :] = jnp.where(low_lane, first, pltpu.roll(second, 64, 1))
        send_ref[number, 32:64, :] = jnp.where(low_lane, pltpu.roll(first, 64, 1), second)
        label = out[130:131] * (out[128:129] + 256.0 * out[129:130] + 1.0) - 1.0
        row = iota((8, 128), 0)
        send_ref[number, 64:72, :] = jnp.where(
            row == 0, label, jnp.where(row == 1, out[131:132], out[132:133])
        )
        send_ref[number, 72:88, :] = jnp.where(number == gy + 1, edges[1], edges[0])
        return 0

    lax.fori_loop(0, send_ref.shape[0], chunk, 0)


def route(place, meta, pressure, water_depth, bed_height, roughness, width):
    blocks = meta.shape[1]
    return pl.pallas_call(
        route_kernel,
        grid=(1,),
        in_specs=[
            SMEM,
            pl.BlockSpec(meta.shape, lambda t: (0, 0)),
            pl.BlockSpec((blocks, 128), lambda t: (0, 3)),
            pl.BlockSpec(water_depth.shape, lambda t: (0, 0)),
            pl.BlockSpec(water_depth.shape, lambda t: (0, 0)),
            pl.BlockSpec(water_depth.shape, lambda t: (0, 0)),
        ],
        out_specs=[
            pl.BlockSpec((width, 88, 128), lambda t: (0, 0, 0)),
            pl.BlockSpec((1, blocks), lambda t: (0, 0)),
            pl.BlockSpec((2, 24, 128), lambda t: (0, 0, 0)),
        ],
        out_shape=[
            jax.ShapeDtypeStruct((width, 88, 128), F32),
            jax.ShapeDtypeStruct((1, blocks), I32),
            jax.ShapeDtypeStruct((2, 24, 128), F32),
        ],
        scratch_shapes=[
            pltpu.VMEM((blocks // 128, 128, 128), F32),
            pltpu.VMEM((144, blocks), BF16),
            pltpu.VMEM((2, 16, 128), F32),
        ],
        compiler_params=pltpu.CompilerParams(vmem_limit_bytes=40 * MIB),
        name="route",
    )(place, meta, pressure, water_depth, bed_height, roughness)


def surface_kernel(place_ref, soil_ref, got_ref, up_ref, down_ref, depth_ref,
                   stay_ref, back_ref, tile_ref, cols_ref, packed, labels, match):
    gy = place_ref[2]
    low_lane = iota((32, 128), 1) < 64
    tag_low = iota((8, 128), 1) < 64
    width = got_ref.shape[0]
    slots = width * 128
    patches = match.shape[0]
    for source in range(width):
        lanes = slice(128 * source, 128 * source + 128)
        at = 40 * source
        from_up = source >= gy
        stay = got_ref[source, 0:32, :]
        moved = jnp.where(from_up, up_ref[at : at + 32, :], down_ref[at : at + 32, :])
        high, low = split(jnp.where(low_lane, stay, pltpu.roll(moved, 64, 1)))
        packed[0:32, lanes] = high
        packed[64:96, lanes] = low
        high, low = split(jnp.where(low_lane, pltpu.roll(stay, 64, 1), moved))
        packed[32:64, lanes] = high
        packed[96:128, lanes] = low
        tags = jnp.where(
            tag_low,
            got_ref[source, 64:72, :],
            jnp.where(from_up, up_ref[at + 32 : at + 40, :], down_ref[at + 32 : at + 40, :]),
        )
        labels[:, lanes] = (tags[0:1, :] + 0.5).astype(I32) - jnp.where(tags[0:1, :] < 0, 1, 0)
        row = iota((16, 128), 0)
        packed[128:144, lanes] = jnp.where(row == 0, tags[1:2, :], tags[2:3, :]).astype(BF16)
    for part in range(patches // 128):
        match[128 * part : 128 * part + 128, :] = as_bf16(
            iota((128, slots), 0) + 128 * part == labels[...]
        )
    placed = lax.dot_general(
        packed[...], match[...], (((1,), (1,)), ((), ())), preferred_element_type=F32
    )
    classes = (placed[128:129] + 0.5).astype(I32)
    levels = (placed[129:130] + 0.5).astype(I32)
    soil = soil_rows(soil_ref, classes)
    half_cell = 0.5 * cell_width(levels)
    head = placed[0:64] + placed[64:128]
    conductivity, _, _ = curve(head, soil)
    row_of = lax.shift_right_logical(iota((128, patches), 0), 3)
    own_row = row_of == lax.shift_right_logical(iota((128, patches), 1), 5)
    depth_high, depth_low = split(depth_ref[...])
    depth_both = jnp.concatenate([depth_high, depth_low], axis=0)
    cols = depth_ref.shape[1]
    pieces = []
    for i in range(8):
        pick = as_bf16(iota((cols, patches), 0) == 8 * jnp.bitwise_and(iota((cols, patches), 1), 31) + i)
        spread = jnp.dot(depth_both, pick, preferred_element_type=F32)
        spread = jnp.where(own_row, spread[0:128] + spread[128:256], 0.0)
        pieces.append(jnp.sum(spread.reshape(16, 8, patches), axis=0))
    depth = jnp.concatenate(pieces, axis=0)
    infiltration = jnp.minimum(
        conductivity / half_cell * (depth - (head - half_cell)), depth / (3.0 * SURF_STEP)
    )
    high, low = split(infiltration)
    both = jnp.concatenate([high, low], axis=0)
    answer = jnp.dot(both, match[...], preferred_element_type=F32)
    answer = answer[0:64] + answer[64:128]
    for source in range(width):
        lanes = slice(128 * source, 128 * source + 128)
        first, second = answer[0:32, lanes], answer[32:64, lanes]
        stay_ref[source] = jnp.where(low_lane, first, pltpu.roll(second, 64, 1))
        moved = jnp.where(low_lane, pltpu.roll(first, 64, 1), second)
        back_ref[0, 32 * source : 32 * source + 32, :] = moved
        back_ref[1, 32 * source : 32 * source + 32, :] = moved
    total = jnp.zeros(depth_ref.shape, F32)
    for i in range(8):
        pick = as_bf16(iota((patches, cols), 1) == 8 * jnp.bitwise_and(iota((patches, cols), 0), 31) + i)
        rows = jnp.concatenate([infiltration[8 * i : 8 * i + 8]] * 16, axis=0)
        high, low = split(jnp.where(own_row, rows, 0.0))
        spread = jnp.dot(jnp.concatenate([high, low], axis=0), pick, preferred_element_type=F32)
        total = total + (spread[0:128] + spread[128:256])
    tile_ref[...] = total
    base = 32 * width
    for half in range(2):
        lanes = slice(128 * half, 128 * half + 128)
        back_ref[0, base + 2 * half : base + 2 * half + 2, :] = total[0:2, lanes]
        back_ref[1, base + 2 * half : base + 2 * half + 2, :] = total[126:128, lanes]
    cols_ref[0, 0:2, :] = total[:, 0:128].T[0:2, :]
    cols_ref[1, 0:2, :] = total[:, 128:256].T[126:128, :]


def surface(place, soil, got, up, down, water_depth, patches):
    width = got.shape[0]
    return pl.pallas_call(
        surface_kernel,
        in_specs=[SMEM, SMEM, VMEM, VMEM, VMEM, VMEM],
        out_specs=[VMEM, VMEM, VMEM, VMEM],
        out_shape=[
            jax.ShapeDtypeStruct((width, 32, 128), F32),
            jax.ShapeDtypeStruct((2, 32 * width + 8, 128), F32),
            jax.ShapeDtypeStruct(water_depth.shape, F32),
            jax.ShapeDtypeStruct((2, 8, 128), F32),
        ],
        scratch_shapes=[
            pltpu.VMEM((144, width * 128), BF16),
            pltpu.VMEM((1, width * 128), I32),
            pltpu.VMEM((patches, width * 128), BF16),
        ],
        compiler_params=pltpu.CompilerParams(vmem_limit_bytes=40 * MIB),
        name="surface",
    )(place, soil, got, up, down, water_depth)


def sweep_kernel(place_ref, depth_ref, bed_ref, rough_ref, left_ref, right_ref, up_ref, down_ref,
                 source_ref, above_ref, below_ref, west_ref, east_ref,
                 out_ref, depth_ext, bed_ext, rough_ext, source_ext, turn):
    gx, gy = place_ref[1], place_ref[2]
    rows_total, cols_total = place_ref[5], place_ref[6]
    shape = depth_ext.shape
    depth_ext[...] = jnp.zeros(shape, F32)
    bed_ext[...] = jnp.zeros(shape, F32)
    rough_ext[...] = jnp.ones(shape, F32)
    source_ext[...] = jnp.zeros(shape, F32)
    for number, (ext, field) in enumerate(
        ((depth_ext, depth_ref), (bed_ext, bed_ref), (rough_ext, rough_ref))
    ):
        ext[8:136, 128:384] = field[...]
        for half in range(2):
            at = 3 * (2 * number + half)
            lanes = slice(128 + 128 * half, 256 + 128 * half)
            ext[5:8, lanes] = up_ref[at : at + 3, :]
            ext[136:139, lanes] = down_ref[at : at + 3, :]
        col = 3 * number
        fill = 1.0 if number == 2 else 0.0
        for side, lanes in ((0, slice(0, 128)), (1, slice(384, 512))):
            to = slice(125, 128) if side == 0 else slice(0, 3)
            center_ref = left_ref if side == 0 else right_ref
            away = 24 + 16 * side + col
            turn[...] = jnp.full((128, 128), fill, F32)
            turn[to, :] = center_ref[col : col + 3, :]
            ext[8:136, lanes] = turn[...].T
            turn[to, :] = up_ref[away : away + 3, :]
            ext[0:8, lanes] = turn[...].T[120:128, :]
            turn[to, :] = down_ref[away : away + 3, :]
            ext[136:144, lanes] = turn[...].T[0:8, :]
    source_ext[8:136, 128:384] = source_ref[...]
    for half in range(2):
        lanes = slice(128 + 128 * half, 256 + 128 * half)
        source_ext[6:8, lanes] = above_ref[2 * half : 2 * half + 2, :]
        source_ext[136:138, lanes] = below_ref[2 * half : 2 * half + 2, :]
    for side, lanes in ((0, slice(0, 128)), (1, slice(384, 512))):
        to = slice(126, 128) if side == 0 else slice(0, 2)
        ref = west_ref if side == 0 else east_ref
        turn[...] = jnp.zeros((128, 128), F32)
        turn[to, :] = ref[0:2, :]
        source_ext[8:136, lanes] = turn[...].T
        source_ext[6:8, lanes] = ref[2:4, :]
        source_ext[136:138, lanes] = ref[4:6, :]
    row_id = gx * depth_ref.shape[0] - 8 + iota(shape, 0)
    col_id = gy * depth_ref.shape[1] - 128 + iota(shape, 1)
    row_open = (row_id >= 0) & (row_id + 1 < rows_total)
    col_open = (col_id >= 0) & (col_id + 1 < cols_total)
    bed = bed_ext[...]
    rough = rough_ext[...]
    inverse = {
        0: jnp.where(row_open, 2.0 / (rough + pltpu.roll(rough, shape[0] - 1, 0)), 0.0),
        1: jnp.where(col_open, 2.0 / (rough + pltpu.roll(rough, shape[1] - 1, 1)), 0.0),
    }
    head = depth_ext[...]
    source = source_ext[...]
    for _ in range(3):
        wet = jnp.maximum(head, 0.0)
        section = head + bed
        net = jnp.zeros(shape, F32) - source
        for axis in range(2):
            back = shape[axis] - 1
            slope = pltpu.roll(section, back, axis) - section
            mean = 0.5 * (wet + pltpu.roll(wet, back, axis))
            flux = (
                jnp.exp2((5.0 / 3.0) * jnp.log2(mean))
                * inverse[axis]
                * slope
                * lax.rsqrt(jnp.abs(slope) + SLOPE_FLOOR)
            )
            net = net + flux - pltpu.roll(flux, 1, axis)
        head = head + SURF_STEP * net
    out_ref[...] = head[8:136, 128:384]


def sweeps(place, water_depth, bed_height, roughness, left, right, up, down, source, above, below, west, east):
    shape = (144, 512)
    return pl.pallas_call(
        sweep_kernel,
        in_specs=[SMEM] + [VMEM] * 12,
        out_specs=VMEM,
        out_shape=jax.ShapeDtypeStruct(water_depth.shape, F32),
        scratch_shapes=[pltpu.VMEM(shape, F32)] * 4 + [pltpu.VMEM((128, 128), F32)],
        compiler_params=pltpu.CompilerParams(vmem_limit_bytes=40 * MIB),
        name="sweeps",
    )(place, water_depth, bed_height, roughness, left, right, up, down, source, above, below, west, east)


def inside_kernel(soil_ref, meta_ref, head_ref, base_ref, factor_ref, table_ref, turned, cond):
    open_i = iota((8, 8, 128), 1) < 7
    nothing = jnp.zeros((1, 8, 128), F32)
    for half in range(head_ref.shape[0] // 128):
        lanes = slice(128 * half, 128 * half + 128)
        turned[half] = head_ref[lanes, :].T
        soil = soil_rows(soil_ref, meta_ref[0:1, lanes])
        width = cell_width(meta_ref[1:2, lanes])
        half_over = 0.5 / width
        scaled = SUB_STEP / width
        for k in range(8):
            rows = slice(64 * k, 64 * k + 64)
            conductivity, base, ratio = curve(turned[half, rows, :], soil)
            cond[half, rows, :] = conductivity
            factor_ref[half, rows, :] = scaled / (soil[4] * ratio / base + STORAGE)
        below = None
        for k in range(8):
            rows = slice(64 * k, 64 * k + 64)
            head = turned[half, rows, :].reshape(8, 8, 128)
            cnd = cond[half, rows, :].reshape(8, 8, 128)
            flux = (cnd + pltpu.roll(cnd, 7, 1)) * (pltpu.roll(head, 7, 1) - head) * half_over
            flux = jnp.where(open_i, flux, 0.0)
            inflow = flux - pltpu.roll(flux, 1, 1)
            flux = (cnd[1:] + cnd[:-1]) * (head[1:] - head[:-1]) * half_over
            inflow = inflow + jnp.concatenate([flux, nothing], 0) - jnp.concatenate([nothing, flux], 0)
            if k < 7:
                above = slice(64 * k + 64, 64 * k + 128)
                head_up = turned[half, above, :].reshape(8, 8, 128)
                cnd_up = cond[half, above, :].reshape(8, 8, 128)
                flux = (cnd + cnd_up) * ((head_up - head) * half_over + 0.5)
                inflow = inflow + flux
            if below is not None:
                inflow = inflow - below
            below = flux
            base_ref[half, rows, :] = (
                turned[half, rows, :] + factor_ref[half, rows, :] * inflow.reshape(64, 128)
            )

    def put(row, half, value):
        table_ref[row : row + 64, 128 * half : 128 * half + 128] = value

    for half in range(head_ref.shape[0] // 128):
        write_faces(turned, cond, half, put)


def inside(soil, meta, pressure):
    blocks = pressure.shape[0]
    return pl.pallas_call(
        inside_kernel,
        grid=(blocks // TILE,),
        in_specs=[
            SMEM,
            pl.BlockSpec((16, TILE), lambda t: (0, t)),
            pl.BlockSpec((TILE, 512), lambda t: (t, 0)),
        ],
        out_specs=[
            pl.BlockSpec((TILE // 128, 512, 128), lambda t: (t, 0, 0)),
            pl.BlockSpec((TILE // 128, 512, 128), lambda t: (t, 0, 0)),
            pl.BlockSpec((1536, TILE), lambda t: (0, t)),
        ],
        out_shape=[
            jax.ShapeDtypeStruct((blocks // 128, 512, 128), F32),
            jax.ShapeDtypeStruct((blocks // 128, 512, 128), F32),
            jax.ShapeDtypeStruct((1536, blocks), BF16),
        ],
        scratch_shapes=[pltpu.VMEM((TILE // 128, 512, 128), F32)] * 2,
        compiler_params=pltpu.CompilerParams(vmem_limit_bytes=40 * MIB),
        name="inside",
    )(soil, meta, pressure)


def across_kernel(place_ref, soil_ref, meta_ref, low_ref, high_ref, base_ref, factor_ref, table_ref,
                  out_ref, table, turned, cond, arrived):
    step = pl.program_id(0)
    blocks = table_ref.shape[1]
    own_lanes = pl.ds(HB, blocks)

    @pl.when(step == 0)
    def _():
        copy = pltpu.make_async_copy(table_ref, table.at[:, own_lanes], arrived)
        copy.start()
        for number, ref in enumerate((low_ref, high_ref)):
            start = 0 if number == 0 else HB + blocks

            def put(row, half, value):
                table[row : row + 64, start + 128 * half : start + 128 * half + 128] = value

            for half in range(HB // 128):
                lanes = slice(128 * half, 128 * half + 128)
                turned[half] = ref[lanes, :].T
                classes = ref[HB : HB + 8, lanes][0:1, :].astype(I32)
                soil = soil_rows(soil_ref, classes)
                for k in range(8):
                    rows = slice(64 * k, 64 * k + 64)
                    cond[half, rows, :] = curve(turned[half, rows, :], soil)[0]
                write_faces(turned, cond, half, put)
        copy.wait()

    turned[...] = base_ref[...]
    window = pl.ds(pl.multiple_of(step * TILE, TILE), TILE + 2 * HB)
    own = pl.ds(pl.multiple_of(step * TILE + HB, TILE), TILE)
    width = cell_width(meta_ref[1:2, :])
    first_row = place_ref[0] * blocks - HB + step * TILE
    for face in range(6):
        neighbor = meta_ref[3 + face : 4 + face, :]
        far_width = cell_width(meta_ref[9 + face : 10 + face, :])
        over_gap = 2.0 / (width + far_width)
        half = jnp.where(neighbor >= 0, 0.5, 0.0)
        chosen = as_bf16(iota((TILE + 2 * HB, TILE), 0) == neighbor - first_row)
        there = 256 * OPPOSITE[face]
        far = jnp.dot(table[there : there + 256, window], chosen, preferred_element_type=F32)
        near = table[256 * face : 256 * face + 256, own].astype(F32)
        head_diff = (far[0:64] - near[0:64]) + (far[64:128] - near[64:128])
        conds = (far[128:192] + near[128:192]) + (far[192:256] + near[192:256])
        flux = conds * half * (head_diff * over_gap + GRAVITY[face])
        for part in range(TILE // 128):
            added = flux[:, 128 * part : 128 * part + 128]
            if face < 2:
                rows = pl.ds(7 * face, 64, stride=8)
                turned[part, rows, :] += factor_ref[part, rows, :] * added
            elif face < 4:
                for k in range(8):
                    at = slice(64 * k + 56 * (face - 2), 64 * k + 56 * (face - 2) + 8)
                    turned[part, at, :] += factor_ref[part, at, :] * added[8 * k : 8 * k + 8]
            else:
                at = slice(448 * (face - 4), 448 * (face - 4) + 64)
                turned[part, at, :] += factor_ref[part, at, :] * added
    for part in range(TILE // 128):
        out_ref[128 * part : 128 * part + 128, :] = turned[part].T


def across(place, soil, meta, low, high, base, factor, table):
    blocks = table.shape[1]
    return pl.pallas_call(
        across_kernel,
        grid=(blocks // TILE,),
        in_specs=[
            SMEM,
            SMEM,
            pl.BlockSpec((16, TILE), lambda t: (0, t)),
            pl.BlockSpec(low.shape, lambda t: (0, 0)),
            pl.BlockSpec(high.shape, lambda t: (0, 0)),
            pl.BlockSpec((TILE // 128, 512, 128), lambda t: (t, 0, 0)),
            pl.BlockSpec((TILE // 128, 512, 128), lambda t: (t, 0, 0)),
            pl.BlockSpec(memory_space=pl.ANY),
        ],
        out_specs=pl.BlockSpec((TILE, 512), lambda t: (t, 0)),
        out_shape=jax.ShapeDtypeStruct((blocks, 512), F32),
        scratch_shapes=[
            pltpu.VMEM((1536, blocks + 2 * HB), BF16),
            pltpu.VMEM((TILE // 128, 512, 128), F32),
            pltpu.VMEM((TILE // 128, 512, 128), F32),
            pltpu.SemaphoreType.DMA,
        ],
        compiler_params=pltpu.CompilerParams(vmem_limit_bytes=48 * MIB),
        name="across",
    )(place, soil, meta, low, high, base, factor, table)


def top_kernel(got_ref, slot_ref, factor_ref, head_ref, out_ref, packed, turned):
    low_lane = iota((32, 128), 1) < 64
    width = got_ref.shape[0]
    slots = width * 128

    @pl.when(pl.program_id(0) == 0)
    def _():
        for number in range(width):
            lanes = slice(128 * number, 128 * number + 128)
            stay, moved = got_ref[number, 0:32, :], got_ref[number, 32:64, :]
            high, low = split(jnp.where(low_lane, stay, pltpu.roll(moved, 64, 1)))
            packed[0:32, lanes] = high
            packed[64:96, lanes] = low
            high, low = split(jnp.where(low_lane, pltpu.roll(stay, 64, 1), moved))
            packed[32:64, lanes] = high
            packed[96:128, lanes] = low

    blocks = slot_ref.shape[1]
    wanted = as_bf16(iota((slots, blocks), 0) == slot_ref[...])
    flux = jnp.dot(packed[...], wanted, preferred_element_type=F32)
    flux = flux[0:64] + flux[64:128]
    for part in range(blocks // 128):
        lanes = slice(128 * part, 128 * part + 128)
        turned[part, 0:64, :] = jnp.zeros((64, 128), F32)
        for i in range(8):
            turned[part, pl.ds(64 + i, 8, stride=8), :] = flux[8 * i : 8 * i + 8, lanes]
        turned[part, 64:128, :] = turned[part, 64:128, :] * factor_ref[part]
        out_ref[lanes, :] = head_ref[lanes, :] + turned[part].T


def top(got, slot, factor, head):
    blocks = head.shape[0]
    part = 2 * TILE
    return pl.pallas_call(
        top_kernel,
        grid=(blocks // part,),
        in_specs=[
            pl.BlockSpec(got.shape, lambda t: (0, 0, 0)),
            pl.BlockSpec((1, part), lambda t: (0, t)),
            pl.BlockSpec((part // 128, 64, 128), lambda t: (t, 7, 0)),
            pl.BlockSpec((part, 128), lambda t: (t, 3)),
        ],
        out_specs=pl.BlockSpec((part, 128), lambda t: (t, 3)),
        out_shape=jax.ShapeDtypeStruct(head.shape, F32),
        input_output_aliases={3: 0},
        scratch_shapes=[
            pltpu.VMEM((128, got.shape[0] * 128), BF16),
            pltpu.VMEM((part // 128, 128, 128), F32),
        ],
        compiler_params=pltpu.CompilerParams(vmem_limit_bytes=40 * MIB),
        name="top",
    )(got, slot, factor, head)


def shifted(value, axis, steps, wrap=True):
    count = lax.axis_size(axis)
    pairs = [(i, (i + steps) % count) for i in range(count) if wrap or 0 <= i + steps < count]
    return lax.ppermute(value, axis, pairs)


def per_device(pressure, soil_class, levels, neighbors, neighbor_levels, patch_of_block, soil_params,
               water_depth, bed_height, roughness):
    blocks = pressure.shape[0]
    rows, cols = water_depth.shape
    patches = rows // 8 * (cols // 8)
    along, width = lax.axis_size("gx"), lax.axis_size("gy")
    gx, gy = lax.axis_index("gx"), lax.axis_index("gy")
    place = jnp.stack(
        [gx * width + gy, gx, gy]
        + [jnp.int32(v) for v in (along * width, width, rows * along, cols * width, 0)]
    ).astype(I32)
    meta = jnp.concatenate(
        [
            soil_class[None],
            levels[None],
            patch_of_block[None],
            neighbors.T,
            neighbor_levels.T,
            jnp.zeros((1, blocks), I32),
        ],
        axis=0,
    )

    def edge(part):
        classes = jnp.pad(soil_class[part].astype(F32)[None], ((0, 7), (0, 512 - HB)))
        return jnp.concatenate([pressure[part], classes], axis=0)

    low_edge = shifted(edge(slice(blocks - HB, blocks)), ("gx", "gy"), 1, wrap=False)
    high_edge = shifted(edge(slice(0, HB)), ("gx", "gy"), -1, wrap=False)

    send, slot, edge_rows = route(place, meta, pressure, water_depth, bed_height, roughness, width)
    got = lax.all_to_all(send, "gy", 0, 0)
    halos = got[:, 72:88]
    left = lax.dynamic_index_in_dim(halos, jnp.maximum(gy - 1, 0), 0, keepdims=False)
    right = lax.dynamic_index_in_dim(halos, jnp.minimum(gy + 1, width - 1), 0, keepdims=False)
    moving = got[:, 32:72].reshape(40 * width, 128)
    from_low = shifted(jnp.concatenate([moving, edge_rows[1], left, right], axis=0), "gx", 1)
    from_high = shifted(jnp.concatenate([moving, edge_rows[0], left, right], axis=0), "gx", -1)

    base, factor, table = inside(soil_params, meta, pressure)

    stay, back, tile, edge_cols = surface(
        place, soil_params, got, from_low, from_high, water_depth, patches
    )
    back_high = shifted(back[0], "gx", -1)
    back_low = shifted(back[1], "gx", 1)

    head = across(place, soil_params, meta, low_edge, high_edge, base, factor, table)

    number = jnp.arange(width, dtype=I32)[:, None, None]
    moved = jnp.where(
        number >= gy,
        back_high[: 32 * width].reshape(width, 32, 128),
        back_low[: 32 * width].reshape(width, 32, 128),
    )
    above, below = back_low[32 * width :], back_high[32 * width :]

    def side(kind):
        lines = slice(2 * kind, 2 * kind + 2)
        return jnp.concatenate(
            [edge_cols[kind, 0:2], above[lines], below[lines], jnp.zeros((2, 128), F32)], axis=0
        )

    sides = jnp.where(number == gy + 1, side(1)[None], side(0)[None])
    returned = lax.all_to_all(jnp.concatenate([stay, moved, sides], axis=1), "gy", 0, 0)
    ends = returned[:, 64:72]
    west = lax.dynamic_index_in_dim(ends, jnp.maximum(gy - 1, 0), 0, keepdims=False)
    east = lax.dynamic_index_in_dim(ends, jnp.minimum(gy + 1, width - 1), 0, keepdims=False)
    new_depth = sweeps(
        place, water_depth, bed_height, roughness, left, right,
        from_low[40 * width :], from_high[40 * width :], tile, above, below, west, east,
    )
    new_pressure = top(returned, slot, factor, head)
    return new_pressure, new_depth


def solution(mesh):
    blocks = P(("gx", "gy"))
    wide = P(("gx", "gy"), None)
    tile = P("gx", "gy")
    return jax.shard_map(
        per_device,
        mesh=mesh,
        in_specs=(wide, blocks, blocks, wide, wide, blocks, P(), tile, tile, tile),
        out_specs=(wide, tile),
        check_vma=False,
    )
```

```python
import functools

import jax
import jax.numpy as jnp
from jax import lax
from jax.experimental import pallas as pl
from jax.experimental.pallas import tpu as pltpu
from jax.sharding import PartitionSpec as P

F32 = jnp.float32
BF16 = jnp.bfloat16
I32 = jnp.int32

HB = 256
TILE = 256
SLOTS = 64
GROUPS = 16
STORAGE = 0.05
SUB_STEP = 0.02
SURF_STEP = 0.003
SLOPE_FLOOR = 0.01
OPPOSITE = (1, 0, 3, 2, 5, 4)
GRAVITY = (0.0, 0.0, 0.0, 0.0, -1.0, 1.0)
VMEM_LIMIT = 60 * 1024 * 1024

VMEM = pl.BlockSpec(memory_space=pltpu.VMEM)
SMEM = pl.BlockSpec(memory_space=pltpu.SMEM)
ANY = pl.BlockSpec(memory_space=pl.ANY)


def split(value):
    high = value.astype(BF16)
    low = (value - high.astype(F32)).astype(BF16)
    return high, low


def iota(shape, dim):
    return lax.broadcasted_iota(I32, shape, dim)


def as_bf16(mask):
    return jnp.where(mask, 1.0, 0.0).astype(BF16)


def cell_width(levels):
    return jnp.where(levels == 0, 0.25, jnp.where(levels == 1, 0.5, 1.0)).astype(F32)


def soil_rows(soil_ref, classes):
    rows = []
    for row in range(5):
        value = jnp.full(classes.shape, soil_ref[row, 0], F32)
        for cls in range(1, soil_ref.shape[1]):
            value = jnp.where(classes == cls, soil_ref[row, cls], value)
        rows.append(value)
    residual, saturated, alpha, power, cond = rows
    exponent = 1.0 - 1.0 / power
    return alpha, power - 1.0, -0.5 * exponent, cond, (saturated - residual) * alpha * (exponent * power)


def curve(pressure, soil):
    alpha, lesser, half, _, _ = soil
    suction = alpha * jnp.maximum(-pressure, 0.0)
    powered = jnp.exp2(lesser * jnp.log2(suction))
    base = 1.0 + powered * suction
    root = jnp.exp2(half * jnp.log2(base))
    ratio = powered * (root * root)
    rest = 1.0 - ratio
    conductivity = soil[3] * root * (rest * rest)
    return conductivity, base, ratio


def face_rows(ref, half, face):
    if face < 2:
        return ref[half, pl.ds(7 * face, 64, stride=8), :]
    if face < 4:
        start = 56 * (face - 2)
        return jnp.concatenate([ref[half, 64 * k + start : 64 * k + start + 8, :] for k in range(8)], axis=0)
    start = 448 * (face - 4)
    return ref[half, start : start + 64, :]


def write_faces(head_ref, cond_ref, half, put):
    for face in range(6):
        head_high, head_low = split(face_rows(head_ref, half, face))
        cond_high, cond_low = split(face_rows(cond_ref, half, face))
        for part, value in enumerate((head_high, head_low, cond_high, cond_low)):
            put(256 * face + 64 * part, half, value)


def route_kernel(place_ref, meta_ref, top_ref, depth_ref, bed_ref, rough_ref,
                 send_ref, slot_ref, rows_ref, match_ref, turned, packed, edges):
    number = pl.program_id(0)
    gy = place_ref[2]

    @pl.when(number == 0)
    def _():
        route_once(place_ref, meta_ref, top_ref, depth_ref, bed_ref, rough_ref,
                   slot_ref, rows_ref, turned, packed, edges)

    blocks = meta_ref.shape[1]
    low_lane = iota((32, 128), 1) < 64
    wanted = as_bf16(iota((128, blocks), 0) + 128 * number == slot_ref[...])
    match_ref[...] = wanted
    out = lax.dot_general(packed[...], wanted, (((1,), (1,)), ((), ())), preferred_element_type=F32)
    first = out[0:32] + out[64:96]
    second = out[32:64] + out[96:128]
    send_ref[0, 0:32, :] = jnp.where(low_lane, first, pltpu.roll(second, 64, 1))
    send_ref[0, 32:64, :] = jnp.where(low_lane, pltpu.roll(first, 64, 1), second)
    label = out[130:131] * (out[128:129] + 256.0 * out[129:130] + 1.0) - 1.0
    row = iota((8, 128), 0)
    send_ref[0, 64:72, :] = jnp.where(row == 0, label, jnp.where(row == 1, out[131:132], out[132:133]))
    send_ref[0, 72:88, :] = jnp.where(number == gy + 1, edges[1], edges[0])


def route_once(place_ref, meta_ref, top_ref, depth_ref, bed_ref, rough_ref,
               slot_ref, rows_ref, turned, packed, edges):
    own, gy = place_ref[0], place_ref[2]
    devices, width = place_ref[3], place_ref[4]
    blocks = meta_ref.shape[1]
    patch = meta_ref[2:3, :]
    is_top = patch >= 0
    safe = jnp.where(is_top, patch, 0)
    offset = lax.rem(lax.shift_right_logical(safe, 9) - own + (GROUPS // 2 - 1) + devices, devices) - (GROUPS // 2 - 1)
    column = gy + offset
    moved = (column < 0) | (column >= width)
    group = 2 * lax.rem(column + width, width) + moved.astype(I32)
    upper = as_bf16(iota((TILE, TILE), 0) < iota((TILE, TILE), 1))
    carry = jnp.zeros((GROUPS, 1), F32)
    for part in range(blocks // TILE):
        lanes = slice(part * TILE, (part + 1) * TILE)
        member = jnp.where(
            (iota((GROUPS, TILE), 0) == group[:, lanes]) & is_top[:, lanes], 1.0, 0.0
        )
        before = jnp.dot(member.astype(BF16), upper, preferred_element_type=F32) + carry
        rank = jnp.sum(member * before, axis=0, keepdims=True)
        carry = carry + jnp.sum(member, axis=1, keepdims=True)
        slot_ref[:, lanes] = jnp.where(
            is_top[:, lanes], group[:, lanes] * SLOTS + rank.astype(I32), -1
        )
        for half in (2 * part, 2 * part + 1):
            turned[half] = top_ref[128 * half : 128 * half + 128, :].T
    for half in range(blocks // 128):
        lanes = slice(128 * half, 128 * half + 128)
        heads = jnp.concatenate(
            [turned[half, pl.ds(64 + i, 8, stride=8), :] for i in range(8)], axis=0
        )
        high, low = split(heads)
        packed[0:64, lanes] = high
        packed[64:128, lanes] = low
    place = jnp.bitwise_and(safe, 511)
    row = iota((16, blocks), 0)
    tags = jnp.where(row == 0, jnp.bitwise_and(place, 255), 0)
    tags = jnp.where(row == 1, lax.shift_right_logical(place, 8), tags)
    tags = jnp.where(row == 2, 1, tags)
    tags = jnp.where(row == 3, meta_ref[0:1, :], tags)
    tags = jnp.where(row == 4, meta_ref[1:2, :], tags)
    packed[128:144, :] = tags.astype(F32).astype(BF16)
    for number, field in enumerate((depth_ref, bed_ref, rough_ref)):
        edges[0, 3 * number : 3 * number + 3, :] = field[:, 0:128].T[0:3, :]
        edges[1, 3 * number : 3 * number + 3, :] = field[:, 128:256].T[125:128, :]
        for half in range(2):
            at = 3 * (2 * number + half)
            lanes = slice(128 * half, 128 * half + 128)
            rows_ref[0, at : at + 3, :] = field[0:3, lanes]
            rows_ref[1, at : at + 3, :] = field[125:128, lanes]


def route(place, meta, pressure, water_depth, bed_height, roughness, width):
    blocks = meta.shape[1]
    return pl.pallas_call(
        route_kernel,
        grid=(width,),
        in_specs=[
            SMEM,
            pl.BlockSpec(meta.shape, lambda t: (0, 0)),
            pl.BlockSpec((blocks, 128), lambda t: (0, 3)),
            pl.BlockSpec(water_depth.shape, lambda t: (0, 0)),
            pl.BlockSpec(water_depth.shape, lambda t: (0, 0)),
            pl.BlockSpec(water_depth.shape, lambda t: (0, 0)),
        ],
        out_specs=[
            pl.BlockSpec((1, 88, 128), lambda t: (t, 0, 0)),
            pl.BlockSpec((1, blocks), lambda t: (0, 0)),
            pl.BlockSpec((2, 24, 128), lambda t: (0, 0, 0)),
            pl.BlockSpec((128, blocks), lambda t: (t, 0)),
        ],
        out_shape=[
            jax.ShapeDtypeStruct((width, 88, 128), F32),
            jax.ShapeDtypeStruct((1, blocks), I32),
            jax.ShapeDtypeStruct((2, 24, 128), F32),
            jax.ShapeDtypeStruct((128 * width, blocks), BF16),
        ],
        scratch_shapes=[
            pltpu.VMEM((blocks // 128, 128, 128), F32),
            pltpu.VMEM((144, blocks), BF16),
            pltpu.VMEM((2, 16, 128), F32),
        ],
        compiler_params=pltpu.CompilerParams(vmem_limit_bytes=VMEM_LIMIT),
        name="route",
    )(place, meta, pressure, water_depth, bed_height, roughness)


def surface_kernel(place_ref, soil_ref, got_ref, up_ref, down_ref, depth_ref, after_ref,
                   stay_ref, back_ref, tile_ref, cols_ref, packed, labels, match):
    gy = place_ref[2]
    low_lane = iota((32, 128), 1) < 64
    tag_low = iota((8, 128), 1) < 64
    width = got_ref.shape[0]
    slots = width * 128
    patches = match.shape[0]
    for source in range(width):
        lanes = slice(128 * source, 128 * source + 128)
        at = 40 * source
        from_up = source >= gy
        stay = got_ref[source, 0:32, :]
        moved = jnp.where(from_up, up_ref[at : at + 32, :], down_ref[at : at + 32, :])
        high, low = split(jnp.where(low_lane, stay, pltpu.roll(moved, 64, 1)))
        packed[0:32, lanes] = high
        packed[64:96, lanes] = low
        high, low = split(jnp.where(low_lane, pltpu.roll(stay, 64, 1), moved))
        packed[32:64, lanes] = high
        packed[96:128, lanes] = low
        tags = jnp.where(
            tag_low,
            got_ref[source, 64:72, :],
            jnp.where(from_up, up_ref[at + 32 : at + 40, :], down_ref[at + 32 : at + 40, :]),
        )
        labels[:, lanes] = (tags[0:1, :] + 0.5).astype(I32) - jnp.where(tags[0:1, :] < 0, 1, 0)
        row = iota((16, 128), 0)
        packed[128:144, lanes] = jnp.where(row == 0, tags[1:2, :], tags[2:3, :]).astype(BF16)
    for part in range(patches // 128):
        match[128 * part : 128 * part + 128, :] = as_bf16(
            iota((128, slots), 0) + 128 * part == labels[...]
        )
    placed = lax.dot_general(
        packed[...], match[...], (((1,), (1,)), ((), ())), preferred_element_type=F32
    )
    classes = (placed[128:129] + 0.5).astype(I32)
    levels = (placed[129:130] + 0.5).astype(I32)
    soil = soil_rows(soil_ref, classes)
    half_cell = 0.5 * cell_width(levels)
    head = placed[0:64] + placed[64:128]
    conductivity, _, _ = curve(head, soil)
    row_of = lax.shift_right_logical(iota((128, patches), 0), 3)
    own_row = row_of == lax.shift_right_logical(iota((128, patches), 1), 5)
    depth_high, depth_low = split(depth_ref[...])
    depth_both = jnp.concatenate([depth_high, depth_low], axis=0)
    cols = depth_ref.shape[1]
    pieces = []
    for i in range(8):
        pick = as_bf16(iota((cols, patches), 0) == 8 * jnp.bitwise_and(iota((cols, patches), 1), 31) + i)
        spread = jnp.dot(depth_both, pick, preferred_element_type=F32)
        spread = jnp.where(own_row, spread[0:128] + spread[128:256], 0.0)
        pieces.append(jnp.sum(spread.reshape(16, 8, patches), axis=0))
    depth = jnp.concatenate(pieces, axis=0)
    infiltration = jnp.minimum(
        conductivity / half_cell * (depth - (head - half_cell)), depth / (3.0 * SURF_STEP)
    )
    high, low = split(infiltration)
    both = jnp.concatenate([high, low], axis=0)
    answer = jnp.dot(both, match[...], preferred_element_type=F32)
    answer = answer[0:64] + answer[64:128]
    for source in range(width):
        lanes = slice(128 * source, 128 * source + 128)
        first, second = answer[0:32, lanes], answer[32:64, lanes]
        stay_ref[source] = jnp.where(low_lane, first, pltpu.roll(second, 64, 1))
        moved = jnp.where(low_lane, pltpu.roll(first, 64, 1), second)
        back_ref[0, 32 * source : 32 * source + 32, :] = moved
        back_ref[1, 32 * source : 32 * source + 32, :] = moved
    total = jnp.zeros(depth_ref.shape, F32)
    for i in range(8):
        pick = as_bf16(iota((patches, cols), 1) == 8 * jnp.bitwise_and(iota((patches, cols), 0), 31) + i)
        rows = jnp.concatenate([infiltration[8 * i : 8 * i + 8]] * 16, axis=0)
        high, low = split(jnp.where(own_row, rows, 0.0))
        spread = jnp.dot(jnp.concatenate([high, low], axis=0), pick, preferred_element_type=F32)
        total = total + (spread[0:128] + spread[128:256])
    tile_ref[...] = total
    base = 32 * width
    for half in range(2):
        lanes = slice(128 * half, 128 * half + 128)
        back_ref[0, base + 2 * half : base + 2 * half + 2, :] = total[0:2, lanes]
        back_ref[1, base + 2 * half : base + 2 * half + 2, :] = total[126:128, lanes]
    cols_ref[0, 0:2, :] = total[:, 0:128].T[0:2, :]
    cols_ref[1, 0:2, :] = total[:, 128:256].T[126:128, :]


def surface(place, soil, got, up, down, water_depth, patches, after):
    width = got.shape[0]
    return pl.pallas_call(
        surface_kernel,
        in_specs=[SMEM, SMEM, VMEM, VMEM, VMEM, VMEM, ANY],
        out_specs=[VMEM, VMEM, VMEM, VMEM],
        out_shape=[
            jax.ShapeDtypeStruct((width, 32, 128), F32),
            jax.ShapeDtypeStruct((2, 32 * width + 8, 128), F32),
            jax.ShapeDtypeStruct(water_depth.shape, F32),
            jax.ShapeDtypeStruct((2, 8, 128), F32),
        ],
        scratch_shapes=[
            pltpu.VMEM((144, width * 128), BF16),
            pltpu.VMEM((1, width * 128), I32),
            pltpu.VMEM((patches, width * 128), BF16),
        ],
        compiler_params=pltpu.CompilerParams(vmem_limit_bytes=VMEM_LIMIT),
        name="surface",
    )(place, soil, got, up, down, water_depth, after)


def sweep_kernel(place_ref, depth_ref, bed_ref, rough_ref, got_ref, up_ref, down_ref,
                 source_ref, low_ref, high_ref, back_ref, after_ref,
                 out_ref, depth_ext, bed_ext, rough_ext, source_ext, turn):
    gx, gy = place_ref[1], place_ref[2]
    left_at, right_at = jnp.maximum(gy - 1, 0), jnp.minimum(gy + 1, place_ref[4] - 1)
    rows_total, cols_total = place_ref[5], place_ref[6]
    shape = depth_ext.shape
    halo = 40 * got_ref.shape[0]
    edge = 32 * got_ref.shape[0]
    depth_ext[...] = jnp.zeros(shape, F32)
    bed_ext[...] = jnp.zeros(shape, F32)
    rough_ext[...] = jnp.ones(shape, F32)
    source_ext[...] = jnp.zeros(shape, F32)
    for number, (ext, field) in enumerate(
        ((depth_ext, depth_ref), (bed_ext, bed_ref), (rough_ext, rough_ref))
    ):
        ext[8:136, 128:384] = field[...]
        for half in range(2):
            at = 3 * (2 * number + half)
            lanes = slice(128 + 128 * half, 256 + 128 * half)
            ext[5:8, lanes] = up_ref[halo + at : halo + at + 3, :]
            ext[136:139, lanes] = down_ref[halo + at : halo + at + 3, :]
        col = 3 * number
        fill = 1.0 if number == 2 else 0.0
        for side, lanes in ((0, slice(0, 128)), (1, slice(384, 512))):
            to = slice(125, 128) if side == 0 else slice(0, 3)
            beside = left_at if side == 0 else right_at
            away = halo + 24 + 16 * side + col
            turn[...] = jnp.full((128, 128), fill, F32)
            turn[to, :] = got_ref[beside, 72:88, :][col : col + 3, :]
            ext[8:136, lanes] = turn[...].T
            turn[to, :] = up_ref[away : away + 3, :]
            ext[0:8, lanes] = turn[...].T[120:128, :]
            turn[to, :] = down_ref[away : away + 3, :]
            ext[136:144, lanes] = turn[...].T[0:8, :]
    source_ext[8:136, 128:384] = source_ref[...]
    for half in range(2):
        lanes = slice(128 + 128 * half, 256 + 128 * half)
        source_ext[6:8, lanes] = low_ref[edge + 2 * half : edge + 2 * half + 2, :]
        source_ext[136:138, lanes] = high_ref[edge + 2 * half : edge + 2 * half + 2, :]
    for side, lanes in ((0, slice(0, 128)), (1, slice(384, 512))):
        to = slice(126, 128) if side == 0 else slice(0, 2)
        ends = back_ref[left_at if side == 0 else right_at, 64:72, :]
        turn[...] = jnp.zeros((128, 128), F32)
        turn[to, :] = ends[0:2, :]
        source_ext[8:136, lanes] = turn[...].T
        source_ext[6:8, lanes] = ends[2:4, :]
        source_ext[136:138, lanes] = ends[4:6, :]
    row_id = gx * depth_ref.shape[0] - 8 + iota(shape, 0)
    col_id = gy * depth_ref.shape[1] - 128 + iota(shape, 1)
    row_open = (row_id >= 0) & (row_id + 1 < rows_total)
    col_open = (col_id >= 0) & (col_id + 1 < cols_total)
    bed = bed_ext[...]
    rough = rough_ext[...]
    inverse = {
        0: jnp.where(row_open, 2.0 / (rough + pltpu.roll(rough, shape[0] - 1, 0)), 0.0),
        1: jnp.where(col_open, 2.0 / (rough + pltpu.roll(rough, shape[1] - 1, 1)), 0.0),
    }
    head = depth_ext[...]
    source = source_ext[...]
    for _ in range(3):
        wet = jnp.maximum(head, 0.0)
        section = head + bed
        net = jnp.zeros(shape, F32) - source
        for axis in range(2):
            back = shape[axis] - 1
            slope = pltpu.roll(section, back, axis) - section
            mean = 0.5 * (wet + pltpu.roll(wet, back, axis))
            flux = (
                jnp.exp2((5.0 / 3.0) * jnp.log2(mean))
                * inverse[axis]
                * slope
                * lax.rsqrt(jnp.abs(slope) + SLOPE_FLOOR)
            )
            net = net + flux - pltpu.roll(flux, 1, axis)
        head = head + SURF_STEP * net
    out_ref[...] = head[8:136, 128:384]


def sweeps(place, water_depth, *rest):
    shape = (144, 512)
    return pl.pallas_call(
        sweep_kernel,
        in_specs=[SMEM] + [VMEM] * 10 + [ANY],
        out_specs=VMEM,
        out_shape=jax.ShapeDtypeStruct(water_depth.shape, F32),
        scratch_shapes=[pltpu.VMEM(shape, F32)] * 4 + [pltpu.VMEM((128, 128), F32)],
        compiler_params=pltpu.CompilerParams(vmem_limit_bytes=VMEM_LIMIT),
        name="sweeps",
    )(place, water_depth, *rest)


def inside_kernel(soil_ref, meta_ref, head_ref, after_ref, base_ref, factor_ref, table_ref, turned, cond):
    open_i = iota((8, 8, 128), 1) < 7
    nothing = jnp.zeros((1, 8, 128), F32)
    for half in range(head_ref.shape[0] // 128):
        lanes = slice(128 * half, 128 * half + 128)
        turned[half] = head_ref[lanes, :].T
        soil = soil_rows(soil_ref, meta_ref[0:1, lanes])
        width = cell_width(meta_ref[1:2, lanes])
        half_over = 0.5 / width
        scaled = SUB_STEP / width
        for k in range(8):
            rows = slice(64 * k, 64 * k + 64)
            conductivity, base, ratio = curve(turned[half, rows, :], soil)
            cond[half, rows, :] = conductivity
            factor_ref[half, rows, :] = scaled * base / (soil[4] * ratio + STORAGE * base)
        below = None
        for k in range(8):
            rows = slice(64 * k, 64 * k + 64)
            head = turned[half, rows, :].reshape(8, 8, 128)
            cnd = cond[half, rows, :].reshape(8, 8, 128)
            flux = (cnd + pltpu.roll(cnd, 7, 1)) * (pltpu.roll(head, 7, 1) - head) * half_over
            flux = jnp.where(open_i, flux, 0.0)
            inflow = flux - pltpu.roll(flux, 1, 1)
            flux = (cnd[1:] + cnd[:-1]) * (head[1:] - head[:-1]) * half_over
            inflow = inflow + jnp.concatenate([flux, nothing], 0) - jnp.concatenate([nothing, flux], 0)
            if k < 7:
                above = slice(64 * k + 64, 64 * k + 128)
                head_up = turned[half, above, :].reshape(8, 8, 128)
                cnd_up = cond[half, above, :].reshape(8, 8, 128)
                flux = (cnd + cnd_up) * ((head_up - head) * half_over + 0.5)
                inflow = inflow + flux
            if below is not None:
                inflow = inflow - below
            below = flux
            base_ref[half, rows, :] = (
                turned[half, rows, :] + factor_ref[half, rows, :] * inflow.reshape(64, 128)
            )

    def put(row, half, value):
        table_ref[row : row + 64, 128 * half : 128 * half + 128] = value

    for half in range(head_ref.shape[0] // 128):
        write_faces(turned, cond, half, put)


def inside(soil, meta, pressure, after, part):
    blocks = pressure.shape[0] // 2
    steps = blocks // TILE
    return pl.pallas_call(
        inside_kernel,
        grid=(steps,),
        in_specs=[
            SMEM,
            pl.BlockSpec((meta.shape[0], TILE), lambda t: (0, t + part * steps)),
            pl.BlockSpec((TILE, 512), lambda t: (t + part * steps, 0)),
            ANY,
        ],
        out_specs=[
            pl.BlockSpec((TILE // 128, 512, 128), lambda t: (t, 0, 0)),
            pl.BlockSpec((TILE // 128, 512, 128), lambda t: (t, 0, 0)),
            pl.BlockSpec((1536, TILE), lambda t: (0, t)),
        ],
        out_shape=[
            jax.ShapeDtypeStruct((blocks // 128, 512, 128), F32),
            jax.ShapeDtypeStruct((blocks // 128, 512, 128), F32),
            jax.ShapeDtypeStruct((1536, blocks), BF16),
        ],
        scratch_shapes=[pltpu.VMEM((TILE // 128, 512, 128), F32)] * 2,
        compiler_params=pltpu.CompilerParams(vmem_limit_bytes=VMEM_LIMIT),
        cost_estimate=pl.CostEstimate(flops=blocks * 512 * 60, bytes_accessed=blocks * 512 * 18, transcendentals=blocks * 512 * 5),
        name="inside",
    )(soil, meta, pressure, after)


def across_kernel(part, place_ref, soil_ref, meta_ref, near_ref, edge_ref, base_ref, factor_ref, table_ref,
                  other_ref, after_ref, out_ref, table, turned, cond, arrived):
    step = pl.program_id(0)
    blocks = table_ref.shape[1]
    start = (0, HB + blocks)[part]

    @pl.when(step == 0)
    def _():
        own_copy = pltpu.make_async_copy(table_ref, table.at[:, pl.ds(HB, blocks)], arrived.at[0])
        own_copy.start()
        next_copy = pltpu.make_async_copy(
            other_ref.at[:, pl.ds((0, blocks - HB)[part], HB)],
            table.at[:, pl.ds((HB + blocks, 0)[part], HB)],
            arrived.at[1],
        )
        next_copy.start()

        def put(row, half, value):
            table[row : row + 64, start + 128 * half : start + 128 * half + 128] = value

        for half in range(HB // 128):
            lanes = slice(128 * half, 128 * half + 128)
            turned[half] = edge_ref[lanes, :].T
            classes = edge_ref[HB : HB + 8, lanes][0:1, :].astype(I32)
            soil = soil_rows(soil_ref, classes)
            for k in range(8):
                rows = slice(64 * k, 64 * k + 64)
                cond[half, rows, :] = curve(turned[half, rows, :], soil)[0]
            write_faces(turned, cond, half, put)
        own_copy.wait()
        next_copy.wait()

    turned[...] = base_ref[...]
    window = pl.ds(pl.multiple_of(step * TILE, TILE), TILE + 2 * HB)
    own = pl.ds(pl.multiple_of(step * TILE + HB, TILE), TILE)
    width = cell_width(meta_ref[1:2, :])
    first_row = (2 * place_ref[0] + part) * blocks - HB + step * TILE
    for face in range(6):
        neighbor = near_ref[face : face + 1, :]
        far_width = cell_width(near_ref[6 + face : 7 + face, :])
        over_gap = 2.0 / (width + far_width)
        half = jnp.where(neighbor >= 0, 0.5, 0.0)
        chosen = as_bf16(iota((TILE + 2 * HB, TILE), 0) == neighbor - first_row)
        there = 256 * OPPOSITE[face]
        far = jnp.dot(table[there : there + 256, window], chosen, preferred_element_type=F32)
        near = table[256 * face : 256 * face + 256, own].astype(F32)
        head_diff = (far[0:64] - near[0:64]) + (far[64:128] - near[64:128])
        conds = (far[128:192] + near[128:192]) + (far[192:256] + near[192:256])
        flux = conds * half * (head_diff * over_gap + GRAVITY[face])
        for part in range(TILE // 128):
            added = flux[:, 128 * part : 128 * part + 128]
            if face < 2:
                rows = pl.ds(7 * face, 64, stride=8)
                turned[part, rows, :] += factor_ref[part, rows, :] * added
            elif face < 4:
                for k in range(8):
                    at = slice(64 * k + 56 * (face - 2), 64 * k + 56 * (face - 2) + 8)
                    turned[part, at, :] += factor_ref[part, at, :] * added[8 * k : 8 * k + 8]
            else:
                at = slice(448 * (face - 4), 448 * (face - 4) + 64)
                turned[part, at, :] += factor_ref[part, at, :] * added
    for part in range(TILE // 128):
        out_ref[128 * part : 128 * part + 128, :] = turned[part].T


def across(place, soil, meta, near, edge, inner, other, after, part, head):
    base, factor, table = inner
    blocks = table.shape[1]
    steps = blocks // TILE
    kernel = functools.partial(across_kernel, part)
    kernel_in = kernel
    aliases = {}
    extra, extra_specs = [], []
    if head is not None:
        def kernel_in(*refs):
            kernel(*refs[:10], *refs[11:])

        aliases = {10: 0}
        extra, extra_specs = [head], [ANY]
    return pl.pallas_call(
        kernel_in,
        grid=(steps,),
        in_specs=[
            SMEM,
            SMEM,
            pl.BlockSpec((meta.shape[0], TILE), lambda t: (0, t + part * steps)),
            pl.BlockSpec((near.shape[0], TILE), lambda t: (0, t + part * steps)),
            pl.BlockSpec(edge.shape, lambda t: (0, 0)),
            pl.BlockSpec((TILE // 128, 512, 128), lambda t: (t, 0, 0)),
            pl.BlockSpec((TILE // 128, 512, 128), lambda t: (t, 0, 0)),
            ANY,
            ANY,
            ANY,
        ]
        + extra_specs,
        out_specs=pl.BlockSpec((TILE, 512), lambda t: (t + part * steps, 0)),
        out_shape=jax.ShapeDtypeStruct((2 * blocks, 512), F32),
        input_output_aliases=aliases,
        scratch_shapes=[
            pltpu.VMEM((1536, blocks + 2 * HB), BF16),
            pltpu.VMEM((TILE // 128, 512, 128), F32),
            pltpu.VMEM((TILE // 128, 512, 128), F32),
            pltpu.SemaphoreType.DMA((2,)),
        ],
        compiler_params=pltpu.CompilerParams(vmem_limit_bytes=VMEM_LIMIT),
        cost_estimate=pl.CostEstimate(flops=steps * 6 * 2 * 256 * 256 * 768, bytes_accessed=blocks * 512 * 18, transcendentals=0),
        name="across",
    )(place, soil, meta, near, edge, base, factor, table, other, after, *extra)


def top_kernel(got_ref, match_ref, factor_ref, head_ref, out_ref, packed, turned):
    low_lane = iota((32, 128), 1) < 64
    width = got_ref.shape[0]

    @pl.when(pl.program_id(0) == 0)
    def _():
        for number in range(width):
            lanes = slice(128 * number, 128 * number + 128)
            stay, moved = got_ref[number, 0:32, :], got_ref[number, 32:64, :]
            high, low = split(jnp.where(low_lane, stay, pltpu.roll(moved, 64, 1)))
            packed[0:32, lanes] = high
            packed[64:96, lanes] = low
            high, low = split(jnp.where(low_lane, pltpu.roll(stay, 64, 1), moved))
            packed[32:64, lanes] = high
            packed[96:128, lanes] = low

    blocks = match_ref.shape[1]
    flux = jnp.dot(packed[...], match_ref[...], preferred_element_type=F32)
    flux = flux[0:64] + flux[64:128]
    for part in range(blocks // 128):
        lanes = slice(128 * part, 128 * part + 128)
        turned[part, 0:64, :] = jnp.zeros((64, 128), F32)
        for i in range(8):
            turned[part, pl.ds(64 + i, 8, stride=8), :] = flux[8 * i : 8 * i + 8, lanes]
        turned[part, 64:128, :] = turned[part, 64:128, :] * factor_ref[part]
        out_ref[lanes, :] = head_ref[lanes, :] + turned[part].T


def top(got, match, factors, head):
    blocks = head.shape[0]
    part = 2 * TILE
    steps = blocks // part
    half = steps // 2

    def kernel(got_ref, match_ref, first_ref, second_ref, head_ref, out_ref, packed, turned):
        step = pl.program_id(0)

        @pl.when(step < half)
        def _():
            top_kernel(got_ref, match_ref, first_ref, head_ref, out_ref, packed, turned)

        @pl.when(step >= half)
        def _():
            top_kernel(got_ref, match_ref, second_ref, head_ref, out_ref, packed, turned)

    return pl.pallas_call(
        kernel,
        grid=(steps,),
        in_specs=[
            pl.BlockSpec(got.shape, lambda t: (0, 0, 0)),
            pl.BlockSpec((match.shape[0], part), lambda t: (0, t)),
            pl.BlockSpec((part // 128, 64, 128), lambda t: (jnp.minimum(t, half - 1), 7, 0)),
            pl.BlockSpec((part // 128, 64, 128), lambda t: (jnp.maximum(t - half, 0), 7, 0)),
            pl.BlockSpec((part, 128), lambda t: (t, 3)),
        ],
        out_specs=pl.BlockSpec((part, 128), lambda t: (t, 3)),
        out_shape=jax.ShapeDtypeStruct(head.shape, F32),
        input_output_aliases={4: 0},
        scratch_shapes=[
            pltpu.VMEM((128, got.shape[0] * 128), BF16),
            pltpu.VMEM((part // 128, 128, 128), F32),
        ],
        compiler_params=pltpu.CompilerParams(vmem_limit_bytes=VMEM_LIMIT),
        name="top",
    )(got, match, *factors, head)


def forward_kernel(place_ref, got_ref, rows_ref, after_ref, up_ref, down_ref):
    gy, width = place_ref[2], got_ref.shape[0]
    west = jnp.maximum(gy - 1, 0)
    east = jnp.minimum(gy + 1, width - 1)
    base = 40 * width
    for number, ref in ((1, up_ref), (0, down_ref)):
        for source in range(width):
            ref[40 * source : 40 * source + 40, :] = got_ref[source, 32:72, :]
        ref[base : base + 24, :] = rows_ref[number]
        ref[base + 24 : base + 40, :] = got_ref[west, 72:88, :]
        ref[base + 40 : base + 56, :] = got_ref[east, 72:88, :]


def forward(place, got, rows, after):
    width = got.shape[0]
    shape = jax.ShapeDtypeStruct((40 * width + 56, 128), F32)
    return pl.pallas_call(
        forward_kernel,
        in_specs=[SMEM, VMEM, VMEM, ANY],
        out_specs=[VMEM, VMEM],
        out_shape=[shape, shape],
        compiler_params=pltpu.CompilerParams(vmem_limit_bytes=VMEM_LIMIT),
        name="forward",
    )(place, got, rows, after)


def backward_kernel(place_ref, stay_ref, low_ref, high_ref, cols_ref, after_ref, send_ref):
    gy, width = place_ref[2], stay_ref.shape[0]
    base = 32 * width
    sides = []
    for kind in range(2):
        lines = slice(base + 2 * kind, base + 2 * kind + 2)
        sides.append(
            jnp.concatenate(
                [cols_ref[kind, 0:2, :], low_ref[lines, :], high_ref[lines, :], jnp.zeros((2, 128), F32)],
                axis=0,
            )
        )
    for number in range(width):
        rows = slice(32 * number, 32 * number + 32)
        send_ref[number, 0:32, :] = stay_ref[number]
        send_ref[number, 32:64, :] = jnp.where(number >= gy, high_ref[rows, :], low_ref[rows, :])
        send_ref[number, 64:72, :] = jnp.where(number == gy + 1, sides[1], sides[0])


def backward(place, stay, low, high, cols, after):
    width = stay.shape[0]
    return pl.pallas_call(
        backward_kernel,
        in_specs=[SMEM, VMEM, VMEM, VMEM, VMEM, ANY],
        out_specs=VMEM,
        out_shape=jax.ShapeDtypeStruct((width, 72, 128), F32),
        compiler_params=pltpu.CompilerParams(vmem_limit_bytes=VMEM_LIMIT),
        name="backward",
    )(place, stay, low, high, cols, after)


def shifted(value, axis, steps, wrap=True):
    count = lax.axis_size(axis)
    pairs = [(i, (i + steps) % count) for i in range(count) if wrap or 0 <= i + steps < count]
    return lax.ppermute(value, axis, pairs)


def per_device(pressure, soil_class, levels, neighbors, neighbor_levels, patch_of_block, soil_params,
               water_depth, bed_height, roughness):
    blocks = pressure.shape[0]
    rows, cols = water_depth.shape
    patches = rows // 8 * (cols // 8)
    along, width = lax.axis_size("gx"), lax.axis_size("gy")
    gx, gy = lax.axis_index("gx"), lax.axis_index("gy")
    place = jnp.stack(
        [gx * width + gy, gx, gy]
        + [jnp.int32(v) for v in (along * width, width, rows * along, cols * width, 0)]
    ).astype(I32)
    meta = jnp.stack([soil_class, levels, patch_of_block])
    near = jnp.concatenate([neighbors.T, neighbor_levels.T], axis=0)

    def edge(part):
        classes = jnp.pad(soil_class[part].astype(F32)[None], ((0, 7), (0, 512 - HB)))
        return jnp.concatenate([pressure[part], classes], axis=0)

    low_edge = shifted(edge(slice(blocks - HB, blocks)), ("gx", "gy"), 1, wrap=False)
    high_edge = shifted(edge(slice(0, HB)), ("gx", "gy"), -1, wrap=False)

    send, slot, edge_rows, match = route(
        place, meta, pressure, water_depth, bed_height, roughness, width
    )
    got = lax.all_to_all(send, "gy", 0, 0)
    first = inside(soil_params, meta, pressure, slot, 0)
    up, down = forward(place, got, edge_rows, first[0])
    from_low = shifted(up, "gx", 1)
    from_high = shifted(down, "gx", -1)
    second = inside(soil_params, meta, pressure, up, 1)
    stay, back, tile, edge_cols = surface(
        place, soil_params, got, from_low, from_high, water_depth, patches, second[0]
    )
    back_high = shifted(back[0], "gx", -1)
    back_low = shifted(back[1], "gx", 1)
    head = across(place, soil_params, meta, near, low_edge, first, second[2], stay, 0, None)
    reply = backward(place, stay, back_low, back_high, edge_cols, head)
    returned = lax.all_to_all(reply, "gy", 0, 0)
    head = across(place, soil_params, meta, near, high_edge, second, first[2], reply, 1, head)
    new_depth = sweeps(
        place, water_depth, bed_height, roughness, got, from_low, from_high, tile,
        back_low, back_high, returned, head,
    )
    new_pressure = top(returned, match, (first[1], second[1]), head)
    return new_pressure, new_depth


def solution(mesh):
    blocks = P(("gx", "gy"))
    wide = P(("gx", "gy"), None)
    tile = P("gx", "gy")
    return jax.shard_map(
        per_device,
        mesh=mesh,
        in_specs=(wide, blocks, blocks, wide, wide, blocks, P(), tile, tile, tile),
        out_specs=(wide, tile),
        check_vma=False,
    )
```

```python
import functools

import jax
import jax.numpy as jnp
from jax import lax
from jax.experimental import pallas as pl
from jax.experimental.pallas import tpu as pltpu
from jax.sharding import PartitionSpec as P

F32 = jnp.float32
BF16 = jnp.bfloat16
I32 = jnp.int32

HB = 256
TILE = 256
SLOTS = 64
GROUPS = 16
STORAGE = 0.05
SUB_STEP = 0.02
SURF_STEP = 0.003
SLOPE_FLOOR = 0.01
OPPOSITE = (1, 0, 3, 2, 5, 4)
GRAVITY = (0.0, 0.0, 0.0, 0.0, -1.0, 1.0)
VMEM_LIMIT = 60 * 1024 * 1024

VMEM = pl.BlockSpec(memory_space=pltpu.VMEM)
SMEM = pl.BlockSpec(memory_space=pltpu.SMEM)
ANY = pl.BlockSpec(memory_space=pl.ANY)


def split(value):
    high = value.astype(BF16)
    low = (value - high.astype(F32)).astype(BF16)
    return high, low


def iota(shape, dim):
    return lax.broadcasted_iota(I32, shape, dim)


def as_bf16(mask):
    return jnp.where(mask, 1.0, 0.0).astype(BF16)


def cell_width(levels):
    return jnp.where(levels == 0, 0.25, jnp.where(levels == 1, 0.5, 1.0)).astype(F32)


def soil_rows(soil_ref, classes):
    rows = []
    for row in range(5):
        value = jnp.full(classes.shape, soil_ref[row, 0], F32)
        for cls in range(1, soil_ref.shape[1]):
            value = jnp.where(classes == cls, soil_ref[row, cls], value)
        rows.append(value)
    residual, saturated, alpha, power, cond = rows
    exponent = 1.0 - 1.0 / power
    return alpha, power - 1.0, -0.5 * exponent, cond, (saturated - residual) * alpha * (exponent * power)


def curve(pressure, soil):
    alpha, lesser, half, _, _ = soil
    suction = alpha * jnp.maximum(-pressure, 0.0)
    powered = jnp.exp2(lesser * jnp.log2(suction))
    base = 1.0 + powered * suction
    root = jnp.exp2(half * jnp.log2(base))
    ratio = powered * (root * root)
    rest = 1.0 - ratio
    conductivity = soil[3] * root * (rest * rest)
    return conductivity, base, ratio


def face_rows(ref, half, face):
    if face < 2:
        return ref[half, pl.ds(7 * face, 64, stride=8), :]
    if face < 4:
        start = 56 * (face - 2)
        return jnp.concatenate([ref[half, 64 * k + start : 64 * k + start + 8, :] for k in range(8)], axis=0)
    start = 448 * (face - 4)
    return ref[half, start : start + 64, :]


def write_faces(head_ref, cond_ref, half, slot, table):
    lanes = pl.ds(pl.multiple_of(slot * TILE, TILE) + 128 * half, 128)
    for face in range(6):
        head_high, head_low = split(face_rows(head_ref, half, face))
        cond_high, cond_low = split(face_rows(cond_ref, half, face))
        for part, value in enumerate((head_high, head_low, cond_high, cond_low)):
            row = 256 * face + 64 * part
            table[row : row + 64, lanes] = value


def route_kernel(place_ref, meta_ref, top_ref, depth_ref, bed_ref, rough_ref,
                 send_ref, slot_ref, rows_ref, match_ref, turned, packed, edges):
    number = pl.program_id(0)
    gy = place_ref[2]

    @pl.when(number == 0)
    def _():
        route_once(place_ref, meta_ref, top_ref, depth_ref, bed_ref, rough_ref,
                   slot_ref, rows_ref, turned, packed, edges)

    blocks = meta_ref.shape[1]
    low_lane = iota((32, 128), 1) < 64
    wanted = as_bf16(iota((128, blocks), 0) + 128 * number == slot_ref[...])
    match_ref[...] = wanted
    out = lax.dot_general(packed[...], wanted, (((1,), (1,)), ((), ())), preferred_element_type=F32)
    first = out[0:32] + out[64:96]
    second = out[32:64] + out[96:128]
    send_ref[0, 0:32, :] = jnp.where(low_lane, first, pltpu.roll(second, 64, 1))
    send_ref[0, 32:64, :] = jnp.where(low_lane, pltpu.roll(first, 64, 1), second)
    label = out[130:131] * (out[128:129] + 256.0 * out[129:130] + 1.0) - 1.0
    row = iota((8, 128), 0)
    send_ref[0, 64:72, :] = jnp.where(row == 0, label, jnp.where(row == 1, out[131:132], out[132:133]))
    send_ref[0, 72:88, :] = jnp.where(number == gy + 1, edges[1], edges[0])


def route_once(place_ref, meta_ref, top_ref, depth_ref, bed_ref, rough_ref,
               slot_ref, rows_ref, turned, packed, edges):
    own, gy = place_ref[0], place_ref[2]
    devices, width = place_ref[3], place_ref[4]
    blocks = meta_ref.shape[1]
    patch = meta_ref[2:3, :]
    is_top = patch >= 0
    safe = jnp.where(is_top, patch, 0)
    offset = lax.rem(lax.shift_right_logical(safe, 9) - own + (GROUPS // 2 - 1) + devices, devices) - (GROUPS // 2 - 1)
    column = gy + offset
    moved = (column < 0) | (column >= width)
    group = 2 * lax.rem(column + width, width) + moved.astype(I32)
    upper = as_bf16(iota((TILE, TILE), 0) < iota((TILE, TILE), 1))
    carry = jnp.zeros((GROUPS, 1), F32)
    for part in range(blocks // TILE):
        lanes = slice(part * TILE, (part + 1) * TILE)
        member = jnp.where(
            (iota((GROUPS, TILE), 0) == group[:, lanes]) & is_top[:, lanes], 1.0, 0.0
        )
        before = jnp.dot(member.astype(BF16), upper, preferred_element_type=F32) + carry
        rank = jnp.sum(member * before, axis=0, keepdims=True)
        carry = carry + jnp.sum(member, axis=1, keepdims=True)
        slot_ref[:, lanes] = jnp.where(
            is_top[:, lanes], group[:, lanes] * SLOTS + rank.astype(I32), -1
        )
        for half in (2 * part, 2 * part + 1):
            turned[half] = top_ref[128 * half : 128 * half + 128, :].T
    for half in range(blocks // 128):
        lanes = slice(128 * half, 128 * half + 128)
        heads = jnp.concatenate(
            [turned[half, pl.ds(64 + i, 8, stride=8), :] for i in range(8)], axis=0
        )
        high, low = split(heads)
        packed[0:64, lanes] = high
        packed[64:128, lanes] = low
    place = jnp.bitwise_and(safe, 511)
    row = iota((16, blocks), 0)
    tags = jnp.where(row == 0, jnp.bitwise_and(place, 255), 0)
    tags = jnp.where(row == 1, lax.shift_right_logical(place, 8), tags)
    tags = jnp.where(row == 2, 1, tags)
    tags = jnp.where(row == 3, meta_ref[0:1, :], tags)
    tags = jnp.where(row == 4, meta_ref[1:2, :], tags)
    packed[128:144, :] = tags.astype(F32).astype(BF16)
    for number, field in enumerate((depth_ref, bed_ref, rough_ref)):
        edges[0, 3 * number : 3 * number + 3, :] = field[:, 0:128].T[0:3, :]
        edges[1, 3 * number : 3 * number + 3, :] = field[:, 128:256].T[125:128, :]
        for half in range(2):
            at = 3 * (2 * number + half)
            lanes = slice(128 * half, 128 * half + 128)
            rows_ref[0, at : at + 3, :] = field[0:3, lanes]
            rows_ref[1, at : at + 3, :] = field[125:128, lanes]


def route(place, meta, pressure, water_depth, bed_height, roughness, width):
    blocks = meta.shape[1]
    return pl.pallas_call(
        route_kernel,
        grid=(width,),
        in_specs=[
            SMEM,
            pl.BlockSpec(meta.shape, lambda t: (0, 0)),
            pl.BlockSpec((blocks, 128), lambda t: (0, 3)),
            pl.BlockSpec(water_depth.shape, lambda t: (0, 0)),
            pl.BlockSpec(water_depth.shape, lambda t: (0, 0)),
            pl.BlockSpec(water_depth.shape, lambda t: (0, 0)),
        ],
        out_specs=[
            pl.BlockSpec((1, 88, 128), lambda t: (t, 0, 0)),
            pl.BlockSpec((1, blocks), lambda t: (0, 0)),
            pl.BlockSpec((2, 24, 128), lambda t: (0, 0, 0)),
            pl.BlockSpec((128, blocks), lambda t: (t, 0)),
        ],
        out_shape=[
            jax.ShapeDtypeStruct((width, 88, 128), F32),
            jax.ShapeDtypeStruct((1, blocks), I32),
            jax.ShapeDtypeStruct((2, 24, 128), F32),
            jax.ShapeDtypeStruct((128 * width, blocks), BF16),
        ],
        scratch_shapes=[
            pltpu.VMEM((blocks // 128, 128, 128), F32),
            pltpu.VMEM((144, blocks), BF16),
            pltpu.VMEM((2, 16, 128), F32),
        ],
        compiler_params=pltpu.CompilerParams(vmem_limit_bytes=VMEM_LIMIT),
        name="route",
    )(place, meta, pressure, water_depth, bed_height, roughness)


def surface_kernel(place_ref, soil_ref, got_ref, up_ref, down_ref, depth_ref, after_ref,
                   stay_ref, back_ref, tile_ref, cols_ref, packed, labels, match):
    gy = place_ref[2]
    low_lane = iota((32, 128), 1) < 64
    tag_low = iota((8, 128), 1) < 64
    width = got_ref.shape[0]
    slots = width * 128
    patches = match.shape[0]
    for source in range(width):
        lanes = slice(128 * source, 128 * source + 128)
        at = 40 * source
        from_up = source >= gy
        stay = got_ref[source, 0:32, :]
        moved = jnp.where(from_up, up_ref[at : at + 32, :], down_ref[at : at + 32, :])
        high, low = split(jnp.where(low_lane, stay, pltpu.roll(moved, 64, 1)))
        packed[0:32, lanes] = high
        packed[64:96, lanes] = low
        high, low = split(jnp.where(low_lane, pltpu.roll(stay, 64, 1), moved))
        packed[32:64, lanes] = high
        packed[96:128, lanes] = low
        tags = jnp.where(
            tag_low,
            got_ref[source, 64:72, :],
            jnp.where(from_up, up_ref[at + 32 : at + 40, :], down_ref[at + 32 : at + 40, :]),
        )
        labels[:, lanes] = (tags[0:1, :] + 0.5).astype(I32) - jnp.where(tags[0:1, :] < 0, 1, 0)
        row = iota((16, 128), 0)
        packed[128:144, lanes] = jnp.where(row == 0, tags[1:2, :], tags[2:3, :]).astype(BF16)
    for part in range(patches // 128):
        match[128 * part : 128 * part + 128, :] = as_bf16(
            iota((128, slots), 0) + 128 * part == labels[...]
        )
    placed = lax.dot_general(
        packed[...], match[...], (((1,), (1,)), ((), ())), preferred_element_type=F32
    )
    classes = (placed[128:129] + 0.5).astype(I32)
    levels = (placed[129:130] + 0.5).astype(I32)
    soil = soil_rows(soil_ref, classes)
    half_cell = 0.5 * cell_width(levels)
    head = placed[0:64] + placed[64:128]
    conductivity, _, _ = curve(head, soil)
    row_of = lax.shift_right_logical(iota((128, patches), 0), 3)
    own_row = row_of == lax.shift_right_logical(iota((128, patches), 1), 5)
    depth_high, depth_low = split(depth_ref[...])
    depth_both = jnp.concatenate([depth_high, depth_low], axis=0)
    cols = depth_ref.shape[1]
    pieces = []
    for i in range(8):
        pick = as_bf16(iota((cols, patches), 0) == 8 * jnp.bitwise_and(iota((cols, patches), 1), 31) + i)
        spread = jnp.dot(depth_both, pick, preferred_element_type=F32)
        spread = jnp.where(own_row, spread[0:128] + spread[128:256], 0.0)
        pieces.append(jnp.sum(spread.reshape(16, 8, patches), axis=0))
    depth = jnp.concatenate(pieces, axis=0)
    infiltration = jnp.minimum(
        conductivity / half_cell * (depth - (head - half_cell)), depth / (3.0 * SURF_STEP)
    )
    high, low = split(infiltration)
    both = jnp.concatenate([high, low], axis=0)
    answer = jnp.dot(both, match[...], preferred_element_type=F32)
    answer = answer[0:64] + answer[64:128]
    for source in range(width):
        lanes = slice(128 * source, 128 * source + 128)
        first, second = answer[0:32, lanes], answer[32:64, lanes]
        stay_ref[source] = jnp.where(low_lane, first, pltpu.roll(second, 64, 1))
        moved = jnp.where(low_lane, pltpu.roll(first, 64, 1), second)
        back_ref[0, 32 * source : 32 * source + 32, :] = moved
        back_ref[1, 32 * source : 32 * source + 32, :] = moved
    total = jnp.zeros(depth_ref.shape, F32)
    for i in range(8):
        pick = as_bf16(iota((patches, cols), 1) == 8 * jnp.bitwise_and(iota((patches, cols), 0), 31) + i)
        rows = jnp.concatenate([infiltration[8 * i : 8 * i + 8]] * 16, axis=0)
        high, low = split(jnp.where(own_row, rows, 0.0))
        spread = jnp.dot(jnp.concatenate([high, low], axis=0), pick, preferred_element_type=F32)
        total = total + (spread[0:128] + spread[128:256])
    tile_ref[...] = total
    base = 32 * width
    for half in range(2):
        lanes = slice(128 * half, 128 * half + 128)
        back_ref[0, base + 2 * half : base + 2 * half + 2, :] = total[0:2, lanes]
        back_ref[1, base + 2 * half : base + 2 * half + 2, :] = total[126:128, lanes]
    cols_ref[0, 0:2, :] = total[:, 0:128].T[0:2, :]
    cols_ref[1, 0:2, :] = total[:, 128:256].T[126:128, :]


def surface(place, soil, got, up, down, water_depth, patches, after):
    width = got.shape[0]
    return pl.pallas_call(
        surface_kernel,
        in_specs=[SMEM, SMEM, VMEM, VMEM, VMEM, VMEM, ANY],
        out_specs=[VMEM, VMEM, VMEM, VMEM],
        out_shape=[
            jax.ShapeDtypeStruct((width, 32, 128), F32),
            jax.ShapeDtypeStruct((2, 32 * width + 8, 128), F32),
            jax.ShapeDtypeStruct(water_depth.shape, F32),
            jax.ShapeDtypeStruct((2, 8, 128), F32),
        ],
        scratch_shapes=[
            pltpu.VMEM((144, width * 128), BF16),
            pltpu.VMEM((1, width * 128), I32),
            pltpu.VMEM((patches, width * 128), BF16),
        ],
        compiler_params=pltpu.CompilerParams(vmem_limit_bytes=VMEM_LIMIT),
        name="surface",
    )(place, soil, got, up, down, water_depth, after)


def sweep_kernel(place_ref, depth_ref, bed_ref, rough_ref, got_ref, up_ref, down_ref,
                 source_ref, low_ref, high_ref, back_ref, after_ref,
                 out_ref, depth_ext, bed_ext, rough_ext, source_ext, turn):
    gx, gy = place_ref[1], place_ref[2]
    left_at, right_at = jnp.maximum(gy - 1, 0), jnp.minimum(gy + 1, place_ref[4] - 1)
    rows_total, cols_total = place_ref[5], place_ref[6]
    shape = depth_ext.shape
    halo = 40 * got_ref.shape[0]
    edge = 32 * got_ref.shape[0]
    depth_ext[...] = jnp.zeros(shape, F32)
    bed_ext[...] = jnp.zeros(shape, F32)
    rough_ext[...] = jnp.ones(shape, F32)
    source_ext[...] = jnp.zeros(shape, F32)
    for number, (ext, field) in enumerate(
        ((depth_ext, depth_ref), (bed_ext, bed_ref), (rough_ext, rough_ref))
    ):
        ext[8:136, 128:384] = field[...]
        for half in range(2):
            at = 3 * (2 * number + half)
            lanes = slice(128 + 128 * half, 256 + 128 * half)
            ext[5:8, lanes] = up_ref[halo + at : halo + at + 3, :]
            ext[136:139, lanes] = down_ref[halo + at : halo + at + 3, :]
        col = 3 * number
        fill = 1.0 if number == 2 else 0.0
        for side, lanes in ((0, slice(0, 128)), (1, slice(384, 512))):
            to = slice(125, 128) if side == 0 else slice(0, 3)
            beside = left_at if side == 0 else right_at
            away = halo + 24 + 16 * side + col
            turn[...] = jnp.full((128, 128), fill, F32)
            turn[to, :] = got_ref[beside, 72:88, :][col : col + 3, :]
            ext[8:136, lanes] = turn[...].T
            turn[to, :] = up_ref[away : away + 3, :]
            ext[0:8, lanes] = turn[...].T[120:128, :]
            turn[to, :] = down_ref[away : away + 3, :]
            ext[136:144, lanes] = turn[...].T[0:8, :]
    source_ext[8:136, 128:384] = source_ref[...]
    for half in range(2):
        lanes = slice(128 + 128 * half, 256 + 128 * half)
        source_ext[6:8, lanes] = low_ref[edge + 2 * half : edge + 2 * half + 2, :]
        source_ext[136:138, lanes] = high_ref[edge + 2 * half : edge + 2 * half + 2, :]
    for side, lanes in ((0, slice(0, 128)), (1, slice(384, 512))):
        to = slice(126, 128) if side == 0 else slice(0, 2)
        ends = back_ref[left_at if side == 0 else right_at, 64:72, :]
        turn[...] = jnp.zeros((128, 128), F32)
        turn[to, :] = ends[0:2, :]
        source_ext[8:136, lanes] = turn[...].T
        source_ext[6:8, lanes] = ends[2:4, :]
        source_ext[136:138, lanes] = ends[4:6, :]
    row_id = gx * depth_ref.shape[0] - 8 + iota(shape, 0)
    col_id = gy * depth_ref.shape[1] - 128 + iota(shape, 1)
    row_open = (row_id >= 0) & (row_id + 1 < rows_total)
    col_open = (col_id >= 0) & (col_id + 1 < cols_total)
    bed = bed_ext[...]
    rough = rough_ext[...]
    inverse = {
        0: jnp.where(row_open, 2.0 / (rough + pltpu.roll(rough, shape[0] - 1, 0)), 0.0),
        1: jnp.where(col_open, 2.0 / (rough + pltpu.roll(rough, shape[1] - 1, 1)), 0.0),
    }
    head = depth_ext[...]
    source = source_ext[...]
    for _ in range(3):
        wet = jnp.maximum(head, 0.0)
        section = head + bed
        net = jnp.zeros(shape, F32) - source
        for axis in range(2):
            back = shape[axis] - 1
            slope = pltpu.roll(section, back, axis) - section
            mean = 0.5 * (wet + pltpu.roll(wet, back, axis))
            flux = (
                jnp.exp2((5.0 / 3.0) * jnp.log2(mean))
                * inverse[axis]
                * slope
                * lax.rsqrt(jnp.abs(slope) + SLOPE_FLOOR)
            )
            net = net + flux - pltpu.roll(flux, 1, axis)
        head = head + SURF_STEP * net
    out_ref[...] = head[8:136, 128:384]


def sweeps(place, water_depth, *rest):
    shape = (144, 512)
    return pl.pallas_call(
        sweep_kernel,
        in_specs=[SMEM] + [VMEM] * 10 + [ANY],
        out_specs=VMEM,
        out_shape=jax.ShapeDtypeStruct(water_depth.shape, F32),
        scratch_shapes=[pltpu.VMEM(shape, F32)] * 4 + [pltpu.VMEM((128, 128), F32)],
        compiler_params=pltpu.CompilerParams(vmem_limit_bytes=VMEM_LIMIT),
        name="sweeps",
    )(place, water_depth, *rest)


def halo_tile(soil_ref, classes, source, slot, table, turned, cond):
    for half in range(TILE // 128):
        lanes = slice(128 * half, 128 * half + 128)
        turned[half] = source(lanes).T
        soil = soil_rows(soil_ref, classes(lanes))
        for k in range(8):
            rows = slice(64 * k, 64 * k + 64)
            cond[half, rows, :] = curve(turned[half, rows, :], soil)[0]
        write_faces(turned, cond, half, slot, table)


def inner_tile(soil_ref, meta_ref, head_ref, slot, table, turned, cond, base_sc, factor_sc, top_ref):
    open_i = iota((8, 8, 128), 1) < 7
    nothing = jnp.zeros((1, 8, 128), F32)
    for half in range(TILE // 128):
        lanes = slice(128 * half, 128 * half + 128)
        at = 2 * (slot - 1) + half
        turned[half] = head_ref[lanes, :].T
        soil = soil_rows(soil_ref, meta_ref[0:1, lanes])
        width = cell_width(meta_ref[1:2, lanes])
        half_over = 0.5 / width
        scaled = SUB_STEP / width

        def conduct(k):
            rows = slice(64 * k, 64 * k + 64)
            conductivity, base, ratio = curve(turned[half, rows, :], soil)
            cond[half, rows, :] = conductivity
            factor = scaled * base / (soil[4] * ratio + STORAGE * base)
            factor_sc[at, rows, :] = factor
            if k == 7:
                top_ref[half] = factor

        conduct(0)
        below = None
        for k in range(8):
            if k < 7:
                conduct(k + 1)
            rows = slice(64 * k, 64 * k + 64)
            head = turned[half, rows, :].reshape(8, 8, 128)
            cnd = cond[half, rows, :].reshape(8, 8, 128)
            flux = (cnd + pltpu.roll(cnd, 7, 1)) * (pltpu.roll(head, 7, 1) - head) * half_over
            flux = jnp.where(open_i, flux, 0.0)
            inflow = flux - pltpu.roll(flux, 1, 1)
            flux = (cnd[1:] + cnd[:-1]) * (head[1:] - head[:-1]) * half_over
            inflow = inflow + jnp.concatenate([flux, nothing], 0) - jnp.concatenate([nothing, flux], 0)
            if k < 7:
                above = slice(64 * k + 64, 64 * k + 128)
                head_up = turned[half, above, :].reshape(8, 8, 128)
                cnd_up = cond[half, above, :].reshape(8, 8, 128)
                flux = (cnd + cnd_up) * ((head_up - head) * half_over + 0.5)
                inflow = inflow + flux
            if below is not None:
                inflow = inflow - below
            below = flux
            base_sc[at, rows, :] = (
                turned[half, rows, :] + factor_sc[at, rows, :] * inflow.reshape(64, 128)
            )
        write_faces(turned, cond, half, slot, table)


def face_tile(first_row, levels, near_ref, slot, table, base_sc, factor_sc, out_ref):
    width = cell_width(levels)
    window = pl.ds(pl.multiple_of((slot - 1) * TILE, TILE), 3 * TILE)
    own = pl.ds(pl.multiple_of(slot * TILE, TILE), TILE)
    for face in range(6):
        neighbor = near_ref[face : face + 1, :]
        far_width = cell_width(near_ref[6 + face : 7 + face, :])
        over_gap = 2.0 / (width + far_width)
        half = jnp.where(neighbor >= 0, 0.5, 0.0)
        chosen = as_bf16(iota((3 * TILE, TILE), 0) == neighbor - first_row)
        there = 256 * OPPOSITE[face]
        far = jnp.dot(table[there : there + 256, window], chosen, preferred_element_type=F32)
        near = table[256 * face : 256 * face + 256, own].astype(F32)
        head_diff = (far[0:64] - near[0:64]) + (far[64:128] - near[64:128])
        conds = (far[128:192] + near[128:192]) + (far[192:256] + near[192:256])
        flux = conds * half * (head_diff * over_gap + GRAVITY[face])
        for part in range(TILE // 128):
            at = 2 * (slot - 1) + part
            added = flux[:, 128 * part : 128 * part + 128]
            if face < 2:
                rows = pl.ds(7 * face, 64, stride=8)
                base_sc[at, rows, :] += factor_sc[at, rows, :] * added
            elif face < 4:
                for k in range(8):
                    rows = slice(64 * k + 56 * (face - 2), 64 * k + 56 * (face - 2) + 8)
                    base_sc[at, rows, :] += factor_sc[at, rows, :] * added[8 * k : 8 * k + 8]
            else:
                rows = slice(448 * (face - 4), 448 * (face - 4) + 64)
                base_sc[at, rows, :] += factor_sc[at, rows, :] * added
    for part in range(TILE // 128):
        out_ref[128 * part : 128 * part + 128, :] = base_sc[2 * (slot - 1) + part].T


def cells_kernel(part, inner, place_ref, soil_ref, meta_ref, head_ref, edge_ref, own_ref, near_ref, after_ref,
                 out_ref, top_ref, table, turned, cond, base_sc, factor_sc):
    step = pl.program_id(0)
    last = inner + 1
    blocks = inner * TILE

    def at_edge():
        halo_tile(
            soil_ref,
            lambda lanes: edge_ref[HB : HB + 8, lanes][0:1, :].astype(I32),
            lambda lanes: edge_ref[lanes, :],
            step, table, turned, cond,
        )

    def beside():
        halo_tile(
            soil_ref,
            lambda lanes: meta_ref[0:1, lanes],
            lambda lanes: head_ref[lanes, :],
            step, table, turned, cond,
        )

    def within():
        inner_tile(
            soil_ref, meta_ref, head_ref, step, table, turned, cond, base_sc, factor_sc, top_ref
        )

    def faces():
        slot = step - 2
        first_row = (2 * place_ref[0] + part) * blocks + (slot - 2) * TILE
        face_tile(
            first_row, own_ref[1:2, :], near_ref, slot, table, base_sc, factor_sc, out_ref
        )

    first, final = (at_edge, beside) if part == 0 else (beside, at_edge)

    @pl.when(step == 0)
    def _():
        first()

    @pl.when((step > 0) & (step < 3))
    def _():
        within()

    @pl.when((step >= 3) & (step < last))
    def _():
        faces()
        within()

    @pl.when(step == last)
    def _():
        faces()
        final()

    @pl.when(step == last + 1)
    def _():
        faces()


def cells(place, soil, meta, near, pressure, edge, after, part, head):
    inner = pressure.shape[0] // TILE // 2
    tiles = 2 * inner
    kernel = functools.partial(cells_kernel, part, inner)
    kernel_in = kernel
    aliases = {}
    extra, extra_specs = [], []
    if head is not None:
        def kernel_in(*refs):
            kernel(*refs[:8], *refs[9:])

        aliases = {8: 0}
        extra, extra_specs = [head], [ANY]
    low = part * inner
    seen = lambda t: jnp.clip(t + low - 1, max(low - 1, 0), min(low + inner, tiles - 1))
    done = lambda t: jnp.clip(t + low - 3, low, low + inner - 1)
    return pl.pallas_call(
        kernel_in,
        grid=(inner + 3,),
        in_specs=[
            SMEM,
            SMEM,
            pl.BlockSpec((meta.shape[0], TILE), lambda t: (0, seen(t))),
            pl.BlockSpec((TILE, 512), lambda t: (seen(t), 0)),
            pl.BlockSpec(edge.shape, lambda t: (0, 0)),
            pl.BlockSpec((meta.shape[0], TILE), lambda t: (0, done(t))),
            pl.BlockSpec((near.shape[0], TILE), lambda t: (0, done(t))),
            ANY,
        ]
        + extra_specs,
        out_specs=[
            pl.BlockSpec((TILE, 512), lambda t: (done(t), 0)),
            pl.BlockSpec((TILE // 128, 64, 128), lambda t: (jnp.clip(t - 1, 0, inner - 1), 0, 0)),
        ],
        out_shape=[
            jax.ShapeDtypeStruct(pressure.shape, F32),
            jax.ShapeDtypeStruct((2 * inner, 64, 128), F32),
        ],
        input_output_aliases=aliases,
        scratch_shapes=[
            pltpu.VMEM((1536, (inner + 2) * TILE), BF16),
            pltpu.VMEM((TILE // 128, 512, 128), F32),
            pltpu.VMEM((TILE // 128, 512, 128), F32),
            pltpu.VMEM((2 * inner, 512, 128), F32),
            pltpu.VMEM((2 * inner, 512, 128), F32),
        ],
        compiler_params=pltpu.CompilerParams(vmem_limit_bytes=VMEM_LIMIT),
        cost_estimate=pl.CostEstimate(
            flops=inner * 6 * 2 * 256 * 256 * 768,
            bytes_accessed=inner * TILE * 512 * 16,
            transcendentals=inner * TILE * 512 * 8,
        ),
        name="cells",
    )(place, soil, meta, pressure, edge, meta, near, after, *extra)


def top_kernel(got_ref, match_ref, factor_ref, head_ref, out_ref, packed, turned):
    low_lane = iota((32, 128), 1) < 64
    width = got_ref.shape[0]

    @pl.when(pl.program_id(0) == 0)
    def _():
        for number in range(width):
            lanes = slice(128 * number, 128 * number + 128)
            stay, moved = got_ref[number, 0:32, :], got_ref[number, 32:64, :]
            high, low = split(jnp.where(low_lane, stay, pltpu.roll(moved, 64, 1)))
            packed[0:32, lanes] = high
            packed[64:96, lanes] = low
            high, low = split(jnp.where(low_lane, pltpu.roll(stay, 64, 1), moved))
            packed[32:64, lanes] = high
            packed[96:128, lanes] = low

    blocks = match_ref.shape[1]
    flux = jnp.dot(packed[...], match_ref[...], preferred_element_type=F32)
    flux = flux[0:64] + flux[64:128]
    for part in range(blocks // 128):
        lanes = slice(128 * part, 128 * part + 128)
        turned[part, 0:64, :] = jnp.zeros((64, 128), F32)
        for i in range(8):
            turned[part, pl.ds(64 + i, 8, stride=8), :] = flux[8 * i : 8 * i + 8, lanes]
        turned[part, 64:128, :] = turned[part, 64:128, :] * factor_ref[part]
        out_ref[lanes, :] = head_ref[lanes, :] + turned[part].T


def top(got, match, factors, head):
    blocks = head.shape[0]
    part = 2 * TILE
    steps = blocks // part
    half = steps // 2

    def kernel(got_ref, match_ref, first_ref, second_ref, head_ref, out_ref, packed, turned):
        step = pl.program_id(0)

        @pl.when(step < half)
        def _():
            top_kernel(got_ref, match_ref, first_ref, head_ref, out_ref, packed, turned)

        @pl.when(step >= half)
        def _():
            top_kernel(got_ref, match_ref, second_ref, head_ref, out_ref, packed, turned)

    return pl.pallas_call(
        kernel,
        grid=(steps,),
        in_specs=[
            pl.BlockSpec(got.shape, lambda t: (0, 0, 0)),
            pl.BlockSpec((match.shape[0], part), lambda t: (0, t)),
            pl.BlockSpec((part // 128, 64, 128), lambda t: (jnp.minimum(t, half - 1), 0, 0)),
            pl.BlockSpec((part // 128, 64, 128), lambda t: (jnp.maximum(t - half, 0), 0, 0)),
            pl.BlockSpec((part, 128), lambda t: (t, 3)),
        ],
        out_specs=pl.BlockSpec((part, 128), lambda t: (t, 3)),
        out_shape=jax.ShapeDtypeStruct(head.shape, F32),
        input_output_aliases={4: 0},
        scratch_shapes=[
            pltpu.VMEM((128, got.shape[0] * 128), BF16),
            pltpu.VMEM((part // 128, 128, 128), F32),
        ],
        compiler_params=pltpu.CompilerParams(vmem_limit_bytes=VMEM_LIMIT),
        name="top",
    )(got, match, *factors, head)


def forward_kernel(place_ref, got_ref, rows_ref, after_ref, up_ref, down_ref):
    gy, width = place_ref[2], got_ref.shape[0]
    west = jnp.maximum(gy - 1, 0)
    east = jnp.minimum(gy + 1, width - 1)
    base = 40 * width
    for number, ref in ((1, up_ref), (0, down_ref)):
        for source in range(width):
            ref[40 * source : 40 * source + 40, :] = got_ref[source, 32:72, :]
        ref[base : base + 24, :] = rows_ref[number]
        ref[base + 24 : base + 40, :] = got_ref[west, 72:88, :]
        ref[base + 40 : base + 56, :] = got_ref[east, 72:88, :]


def forward(place, got, rows, after):
    width = got.shape[0]
    shape = jax.ShapeDtypeStruct((40 * width + 56, 128), F32)
    return pl.pallas_call(
        forward_kernel,
        in_specs=[SMEM, VMEM, VMEM, ANY],
        out_specs=[VMEM, VMEM],
        out_shape=[shape, shape],
        compiler_params=pltpu.CompilerParams(vmem_limit_bytes=VMEM_LIMIT),
        name="forward",
    )(place, got, rows, after)


def backward_kernel(place_ref, stay_ref, low_ref, high_ref, cols_ref, after_ref, send_ref):
    gy, width = place_ref[2], stay_ref.shape[0]
    base = 32 * width
    sides = []
    for kind in range(2):
        lines = slice(base + 2 * kind, base + 2 * kind + 2)
        sides.append(
            jnp.concatenate(
                [cols_ref[kind, 0:2, :], low_ref[lines, :], high_ref[lines, :], jnp.zeros((2, 128), F32)],
                axis=0,
            )
        )
    for number in range(width):
        rows = slice(32 * number, 32 * number + 32)
        send_ref[number, 0:32, :] = stay_ref[number]
        send_ref[number, 32:64, :] = jnp.where(number >= gy, high_ref[rows, :], low_ref[rows, :])
        send_ref[number, 64:72, :] = jnp.where(number == gy + 1, sides[1], sides[0])


def backward(place, stay, low, high, cols, after):
    width = stay.shape[0]
    return pl.pallas_call(
        backward_kernel,
        in_specs=[SMEM, VMEM, VMEM, VMEM, VMEM, ANY],
        out_specs=VMEM,
        out_shape=jax.ShapeDtypeStruct((width, 72, 128), F32),
        compiler_params=pltpu.CompilerParams(vmem_limit_bytes=VMEM_LIMIT),
        name="backward",
    )(place, stay, low, high, cols, after)


def shifted(value, axis, steps, wrap=True):
    count = lax.axis_size(axis)
    pairs = [(i, (i + steps) % count) for i in range(count) if wrap or 0 <= i + steps < count]
    return lax.ppermute(value, axis, pairs)


def per_device(pressure, soil_class, levels, neighbors, neighbor_levels, patch_of_block, soil_params,
               water_depth, bed_height, roughness):
    blocks = pressure.shape[0]
    rows, cols = water_depth.shape
    patches = rows // 8 * (cols // 8)
    along, width = lax.axis_size("gx"), lax.axis_size("gy")
    gx, gy = lax.axis_index("gx"), lax.axis_index("gy")
    place = jnp.stack(
        [gx * width + gy, gx, gy]
        + [jnp.int32(v) for v in (along * width, width, rows * along, cols * width, 0)]
    ).astype(I32)
    meta = jnp.stack([soil_class, levels, patch_of_block])
    near = jnp.concatenate([neighbors.T, neighbor_levels.T], axis=0)

    def edge(part):
        classes = jnp.pad(soil_class[part].astype(F32)[None], ((0, 7), (0, 512 - HB)))
        return jnp.concatenate([pressure[part], classes], axis=0)

    low_edge = shifted(edge(slice(blocks - HB, blocks)), ("gx", "gy"), 1, wrap=False)
    high_edge = shifted(edge(slice(0, HB)), ("gx", "gy"), -1, wrap=False)

    send, slot, edge_rows, match = route(
        place, meta, pressure, water_depth, bed_height, roughness, width
    )
    got = lax.all_to_all(send, "gy", 0, 0)
    up, down = forward(place, got, edge_rows, slot)
    from_low = shifted(up, "gx", 1)
    from_high = shifted(down, "gx", -1)
    head, first = cells(place, soil_params, meta, near, pressure, low_edge, up, 0, None)
    stay, back, tile, edge_cols = surface(
        place, soil_params, got, from_low, from_high, water_depth, patches, first
    )
    back_high = shifted(back[0], "gx", -1)
    back_low = shifted(back[1], "gx", 1)
    head, second = cells(place, soil_params, meta, near, pressure, high_edge, stay, 1, head)
    reply = backward(place, stay, back_low, back_high, edge_cols, second)
    returned = lax.all_to_all(reply, "gy", 0, 0)
    new_depth = sweeps(
        place, water_depth, bed_height, roughness, got, from_low, from_high, tile,
        back_low, back_high, returned, head,
    )
    new_pressure = top(returned, match, (first, second), head)
    return new_pressure, new_depth


def solution(mesh):
    blocks = P(("gx", "gy"))
    wide = P(("gx", "gy"), None)
    tile = P("gx", "gy")
    return jax.shard_map(
        per_device,
        mesh=mesh,
        in_specs=(wide, blocks, blocks, wide, wide, blocks, P(), tile, tile, tile),
        out_specs=(wide, tile),
        check_vma=False,
    )
```

```python
import functools

import jax
import jax.numpy as jnp
from jax import lax
from jax.experimental import pallas as pl
from jax.experimental.pallas import tpu as pltpu
from jax.sharding import PartitionSpec as P

F32 = jnp.float32
BF16 = jnp.bfloat16
I32 = jnp.int32

HB = 256
TILE = 256
PARTS = 4
SLOTS = 64
GROUPS = 16
STORAGE = 0.05
SUB_STEP = 0.02
SURF_STEP = 0.003
SLOPE_FLOOR = 0.01
OPPOSITE = (1, 0, 3, 2, 5, 4)
GRAVITY = (0.0, 0.0, 0.0, 0.0, -1.0, 1.0)
VMEM_LIMIT = 60 * 1024 * 1024

VMEM = pl.BlockSpec(memory_space=pltpu.VMEM)
SMEM = pl.BlockSpec(memory_space=pltpu.SMEM)
ANY = pl.BlockSpec(memory_space=pl.ANY)


def position(width):
    gx, gy = lax.axis_index("gx"), lax.axis_index("gy")
    return gx * width + gy, gx, gy


def split(value):
    high = value.astype(BF16)
    low = (value - high.astype(F32)).astype(BF16)
    return high, low


def iota(shape, dim):
    return lax.broadcasted_iota(I32, shape, dim)


def as_bf16(mask):
    return jnp.where(mask, 1.0, 0.0).astype(BF16)


def cell_width(levels):
    return jnp.where(levels == 0, 0.25, jnp.where(levels == 1, 0.5, 1.0)).astype(F32)


def soil_rows(soil_ref, classes):
    rows = []
    for row in range(5):
        value = jnp.full(classes.shape, soil_ref[row, 0], F32)
        for cls in range(1, soil_ref.shape[1]):
            value = jnp.where(classes == cls, soil_ref[row, cls], value)
        rows.append(value)
    residual, saturated, alpha, power, cond = rows
    exponent = 1.0 - 1.0 / power
    return alpha, power - 1.0, -0.5 * exponent, cond, (saturated - residual) * alpha * (exponent * power)


def curve(pressure, soil):
    alpha, lesser, half, _, _ = soil
    suction = alpha * jnp.maximum(-pressure, 0.0)
    powered = jnp.exp2(lesser * jnp.log2(suction))
    base = 1.0 + powered * suction
    root = jnp.exp2(half * jnp.log2(base))
    ratio = powered * (root * root)
    rest = 1.0 - ratio
    conductivity = soil[3] * root * (rest * rest)
    return conductivity, base, ratio


def face_rows(ref, half, face):
    if face < 2:
        return ref[half, pl.ds(7 * face, 64, stride=8), :]
    if face < 4:
        start = 56 * (face - 2)
        return jnp.concatenate([ref[half, 64 * k + start : 64 * k + start + 8, :] for k in range(8)], axis=0)
    start = 448 * (face - 4)
    return ref[half, start : start + 64, :]


def write_faces(head_ref, cond_ref, half, slot, table):
    lanes = pl.ds(pl.multiple_of(slot * TILE, TILE) + 128 * half, 128)
    for face in range(6):
        head_high, head_low = split(face_rows(head_ref, half, face))
        cond_high, cond_low = split(face_rows(cond_ref, half, face))
        for part, value in enumerate((head_high, head_low, cond_high, cond_low)):
            row = 256 * face + 64 * part
            table[row : row + 64, lanes] = value


def route_kernel(shape, class_ref, level_ref, patch_ref, top_ref, depth_ref, bed_ref, rough_ref,
                 send_ref, slot_ref, rows_ref, match_ref, turned, packed, edges):
    number = pl.program_id(0)
    own, _, gy = position(shape[1])

    @pl.when(number == 0)
    def _():
        route_once(own, gy, shape, class_ref, level_ref, patch_ref, top_ref, depth_ref, bed_ref, rough_ref,
                   slot_ref, rows_ref, turned, packed, edges)

    blocks = patch_ref.shape[1]
    low_lane = iota((32, 128), 1) < 64
    wanted = as_bf16(iota((128, blocks), 0) + 128 * number == slot_ref[...])
    match_ref[...] = wanted
    out = lax.dot_general(packed[...], wanted, (((1,), (1,)), ((), ())), preferred_element_type=F32)
    first = out[0:32] + out[64:96]
    second = out[32:64] + out[96:128]
    send_ref[0, 0:32, :] = jnp.where(low_lane, first, pltpu.roll(second, 64, 1))
    send_ref[0, 32:64, :] = jnp.where(low_lane, pltpu.roll(first, 64, 1), second)
    label = out[130:131] * (out[128:129] + 256.0 * out[129:130] + 1.0) - 1.0
    row = iota((8, 128), 0)
    send_ref[0, 64:72, :] = jnp.where(row == 0, label, jnp.where(row == 1, out[131:132], out[132:133]))
    send_ref[0, 72:88, :] = jnp.where(number == gy + 1, edges[1], edges[0])


def route_once(own, gy, shape, class_ref, level_ref, patch_ref, top_ref, depth_ref, bed_ref, rough_ref,
               slot_ref, rows_ref, turned, packed, edges):
    devices, width = shape[0] * shape[1], shape[1]
    blocks = patch_ref.shape[1]
    patch = patch_ref[...]
    is_top = patch >= 0
    safe = jnp.where(is_top, patch, 0)
    offset = lax.rem(lax.shift_right_logical(safe, 9) - own + (GROUPS // 2 - 1) + devices, devices) - (GROUPS // 2 - 1)
    column = gy + offset
    moved = (column < 0) | (column >= width)
    group = 2 * lax.rem(column + width, width) + moved.astype(I32)
    upper = as_bf16(iota((TILE, TILE), 0) < iota((TILE, TILE), 1))
    carry = jnp.zeros((GROUPS, 1), F32)
    for part in range(blocks // TILE):
        lanes = slice(part * TILE, (part + 1) * TILE)
        member = jnp.where(
            (iota((GROUPS, TILE), 0) == group[:, lanes]) & is_top[:, lanes], 1.0, 0.0
        )
        before = jnp.dot(member.astype(BF16), upper, preferred_element_type=F32) + carry
        rank = jnp.sum(member * before, axis=0, keepdims=True)
        carry = carry + jnp.sum(member, axis=1, keepdims=True)
        slot_ref[:, lanes] = jnp.where(
            is_top[:, lanes], group[:, lanes] * SLOTS + rank.astype(I32), -1
        )
        for half in (2 * part, 2 * part + 1):
            turned[half] = top_ref[128 * half : 128 * half + 128, :].T
    for half in range(blocks // 128):
        lanes = slice(128 * half, 128 * half + 128)
        heads = jnp.concatenate(
            [turned[half, pl.ds(64 + i, 8, stride=8), :] for i in range(8)], axis=0
        )
        high, low = split(heads)
        packed[0:64, lanes] = high
        packed[64:128, lanes] = low
    place = jnp.bitwise_and(safe, 511)
    row = iota((16, blocks), 0)
    tags = jnp.where(row == 0, jnp.bitwise_and(place, 255), 0)
    tags = jnp.where(row == 1, lax.shift_right_logical(place, 8), tags)
    tags = jnp.where(row == 2, 1, tags)
    tags = jnp.where(row == 3, class_ref[...], tags)
    tags = jnp.where(row == 4, level_ref[...], tags)
    packed[128:144, :] = tags.astype(F32).astype(BF16)
    for number, field in enumerate((depth_ref, bed_ref, rough_ref)):
        edges[0, 3 * number : 3 * number + 3, :] = field[:, 0:128].T[0:3, :]
        edges[1, 3 * number : 3 * number + 3, :] = field[:, 128:256].T[125:128, :]
        for half in range(2):
            at = 3 * (2 * number + half)
            lanes = slice(128 * half, 128 * half + 128)
            rows_ref[0, at : at + 3, :] = field[0:3, lanes]
            rows_ref[1, at : at + 3, :] = field[125:128, lanes]


def route(shape, kinds, pressure, water_depth, bed_height, roughness):
    blocks = pressure.shape[0]
    width = shape[1]
    row = pl.BlockSpec((1, blocks), lambda t: (0, 0))
    return pl.pallas_call(
        functools.partial(route_kernel, shape),
        grid=(width,),
        in_specs=[
            row,
            row,
            row,
            pl.BlockSpec((blocks, 128), lambda t: (0, 3)),
            pl.BlockSpec(water_depth.shape, lambda t: (0, 0)),
            pl.BlockSpec(water_depth.shape, lambda t: (0, 0)),
            pl.BlockSpec(water_depth.shape, lambda t: (0, 0)),
        ],
        out_specs=[
            pl.BlockSpec((1, 88, 128), lambda t: (t, 0, 0)),
            pl.BlockSpec((1, blocks), lambda t: (0, 0)),
            pl.BlockSpec((2, 24, 128), lambda t: (0, 0, 0)),
            pl.BlockSpec((128, blocks), lambda t: (t, 0)),
        ],
        out_shape=[
            jax.ShapeDtypeStruct((width, 88, 128), F32),
            jax.ShapeDtypeStruct((1, blocks), I32),
            jax.ShapeDtypeStruct((2, 24, 128), F32),
            jax.ShapeDtypeStruct((128 * width, blocks), BF16),
        ],
        scratch_shapes=[
            pltpu.VMEM((blocks // 128, 128, 128), F32),
            pltpu.VMEM((144, blocks), BF16),
            pltpu.VMEM((2, 16, 128), F32),
        ],
        compiler_params=pltpu.CompilerParams(vmem_limit_bytes=VMEM_LIMIT),
        name="route",
    )(*kinds, pressure, water_depth, bed_height, roughness)


def surface_kernel(shape, soil_ref, got_ref, up_ref, down_ref, depth_ref, after_ref,
                   stay_ref, back_high_ref, back_low_ref, tile_ref, cols_ref, packed, labels, match):
    _, _, gy = position(shape[1])
    low_lane = iota((32, 128), 1) < 64
    tag_low = iota((8, 128), 1) < 64
    width = got_ref.shape[0]
    slots = width * 128
    patches = match.shape[0]
    for source in range(width):
        lanes = slice(128 * source, 128 * source + 128)
        at = 40 * source
        from_up = source >= gy
        stay = got_ref[source, 0:32, :]
        moved = jnp.where(from_up, up_ref[at : at + 32, :], down_ref[at : at + 32, :])
        high, low = split(jnp.where(low_lane, stay, pltpu.roll(moved, 64, 1)))
        packed[0:32, lanes] = high
        packed[64:96, lanes] = low
        high, low = split(jnp.where(low_lane, pltpu.roll(stay, 64, 1), moved))
        packed[32:64, lanes] = high
        packed[96:128, lanes] = low
        tags = jnp.where(
            tag_low,
            got_ref[source, 64:72, :],
            jnp.where(from_up, up_ref[at + 32 : at + 40, :], down_ref[at + 32 : at + 40, :]),
        )
        labels[:, lanes] = (tags[0:1, :] + 0.5).astype(I32) - jnp.where(tags[0:1, :] < 0, 1, 0)
        row = iota((16, 128), 0)
        packed[128:144, lanes] = jnp.where(row == 0, tags[1:2, :], tags[2:3, :]).astype(BF16)
    for part in range(patches // 128):
        match[128 * part : 128 * part + 128, :] = as_bf16(
            iota((128, slots), 0) + 128 * part == labels[...]
        )
    placed = lax.dot_general(
        packed[...], match[...], (((1,), (1,)), ((), ())), preferred_element_type=F32
    )
    classes = (placed[128:129] + 0.5).astype(I32)
    levels = (placed[129:130] + 0.5).astype(I32)
    soil = soil_rows(soil_ref, classes)
    half_cell = 0.5 * cell_width(levels)
    head = placed[0:64] + placed[64:128]
    conductivity, _, _ = curve(head, soil)
    row_of = lax.shift_right_logical(iota((128, patches), 0), 3)
    own_row = row_of == lax.shift_right_logical(iota((128, patches), 1), 5)
    depth_high, depth_low = split(depth_ref[...])
    depth_both = jnp.concatenate([depth_high, depth_low], axis=0)
    cols = depth_ref.shape[1]
    pieces = []
    for i in range(8):
        pick = as_bf16(iota((cols, patches), 0) == 8 * jnp.bitwise_and(iota((cols, patches), 1), 31) + i)
        spread = jnp.dot(depth_both, pick, preferred_element_type=F32)
        spread = jnp.where(own_row, spread[0:128] + spread[128:256], 0.0)
        pieces.append(jnp.sum(spread.reshape(16, 8, patches), axis=0))
    depth = jnp.concatenate(pieces, axis=0)
    infiltration = jnp.minimum(
        conductivity / half_cell * (depth - (head - half_cell)), depth / (3.0 * SURF_STEP)
    )
    high, low = split(infiltration)
    both = jnp.concatenate([high, low], axis=0)
    answer = jnp.dot(both, match[...], preferred_element_type=F32)
    answer = answer[0:64] + answer[64:128]
    for source in range(width):
        lanes = slice(128 * source, 128 * source + 128)
        first, second = answer[0:32, lanes], answer[32:64, lanes]
        stay_ref[source] = jnp.where(low_lane, first, pltpu.roll(second, 64, 1))
        moved = jnp.where(low_lane, pltpu.roll(first, 64, 1), second)
        back_high_ref[32 * source : 32 * source + 32, :] = moved
        back_low_ref[32 * source : 32 * source + 32, :] = moved
    total = jnp.zeros(depth_ref.shape, F32)
    for i in range(8):
        pick = as_bf16(iota((patches, cols), 1) == 8 * jnp.bitwise_and(iota((patches, cols), 0), 31) + i)
        rows = jnp.concatenate([infiltration[8 * i : 8 * i + 8]] * 16, axis=0)
        high, low = split(jnp.where(own_row, rows, 0.0))
        spread = jnp.dot(jnp.concatenate([high, low], axis=0), pick, preferred_element_type=F32)
        total = total + (spread[0:128] + spread[128:256])
    tile_ref[...] = total
    base = 32 * width
    for half in range(2):
        lanes = slice(128 * half, 128 * half + 128)
        back_high_ref[base + 2 * half : base + 2 * half + 2, :] = total[0:2, lanes]
        back_low_ref[base + 2 * half : base + 2 * half + 2, :] = total[126:128, lanes]
    cols_ref[0, 0:2, :] = total[:, 0:128].T[0:2, :]
    cols_ref[1, 0:2, :] = total[:, 128:256].T[126:128, :]


def surface(shape, soil, got, up, down, water_depth, patches, after):
    width = got.shape[0]
    return pl.pallas_call(
        functools.partial(surface_kernel, shape),
        in_specs=[SMEM, VMEM, VMEM, VMEM, VMEM, ANY],
        out_specs=[VMEM] * 5,
        out_shape=[
            jax.ShapeDtypeStruct((width, 32, 128), F32),
            jax.ShapeDtypeStruct((32 * width + 8, 128), F32),
            jax.ShapeDtypeStruct((32 * width + 8, 128), F32),
            jax.ShapeDtypeStruct(water_depth.shape, F32),
            jax.ShapeDtypeStruct((2, 8, 128), F32),
        ],
        scratch_shapes=[
            pltpu.VMEM((144, width * 128), BF16),
            pltpu.VMEM((1, width * 128), I32),
            pltpu.VMEM((patches, width * 128), BF16),
        ],
        compiler_params=pltpu.CompilerParams(vmem_limit_bytes=VMEM_LIMIT),
        name="surface",
    )(soil, got, up, down, water_depth, after)


def sweep_kernel(place, depth_ref, bed_ref, rough_ref, got_ref, up_ref, down_ref,
                 source_ref, low_ref, high_ref, back_ref, after_ref,
                 out_ref, depth_ext, bed_ext, rough_ext, source_ext, turn):
    _, gx, gy = position(place[1])
    left_at, right_at = jnp.maximum(gy - 1, 0), jnp.minimum(gy + 1, place[1] - 1)
    rows_total, cols_total = depth_ref.shape[0] * place[0], depth_ref.shape[1] * place[1]
    shape = depth_ext.shape
    halo = 40 * got_ref.shape[0]
    edge = 32 * got_ref.shape[0]
    depth_ext[...] = jnp.zeros(shape, F32)
    bed_ext[...] = jnp.zeros(shape, F32)
    rough_ext[...] = jnp.ones(shape, F32)
    source_ext[...] = jnp.zeros(shape, F32)
    for number, (ext, field) in enumerate(
        ((depth_ext, depth_ref), (bed_ext, bed_ref), (rough_ext, rough_ref))
    ):
        ext[8:136, 128:384] = field[...]
        for half in range(2):
            at = 3 * (2 * number + half)
            lanes = slice(128 + 128 * half, 256 + 128 * half)
            ext[5:8, lanes] = up_ref[halo + at : halo + at + 3, :]
            ext[136:139, lanes] = down_ref[halo + at : halo + at + 3, :]
        col = 3 * number
        fill = 1.0 if number == 2 else 0.0
        for side, lanes in ((0, slice(0, 128)), (1, slice(384, 512))):
            to = slice(125, 128) if side == 0 else slice(0, 3)
            beside = left_at if side == 0 else right_at
            away = halo + 24 + 16 * side + col
            turn[...] = jnp.full((128, 128), fill, F32)
            turn[to, :] = got_ref[beside, 72:88, :][col : col + 3, :]
            ext[8:136, lanes] = turn[...].T
            turn[to, :] = up_ref[away : away + 3, :]
            ext[0:8, lanes] = turn[...].T[120:128, :]
            turn[to, :] = down_ref[away : away + 3, :]
            ext[136:144, lanes] = turn[...].T[0:8, :]
    source_ext[8:136, 128:384] = source_ref[...]
    for half in range(2):
        lanes = slice(128 + 128 * half, 256 + 128 * half)
        source_ext[6:8, lanes] = low_ref[edge + 2 * half : edge + 2 * half + 2, :]
        source_ext[136:138, lanes] = high_ref[edge + 2 * half : edge + 2 * half + 2, :]
    for side, lanes in ((0, slice(0, 128)), (1, slice(384, 512))):
        to = slice(126, 128) if side == 0 else slice(0, 2)
        ends = back_ref[left_at if side == 0 else right_at, 64:72, :]
        turn[...] = jnp.zeros((128, 128), F32)
        turn[to, :] = ends[0:2, :]
        source_ext[8:136, lanes] = turn[...].T
        source_ext[6:8, lanes] = ends[2:4, :]
        source_ext[136:138, lanes] = ends[4:6, :]
    row_id = gx * depth_ref.shape[0] - 8 + iota(shape, 0)
    col_id = gy * depth_ref.shape[1] - 128 + iota(shape, 1)
    row_open = (row_id >= 0) & (row_id + 1 < rows_total)
    col_open = (col_id >= 0) & (col_id + 1 < cols_total)
    bed = bed_ext[...]
    rough = rough_ext[...]
    inverse = {
        0: jnp.where(row_open, 2.0 / (rough + pltpu.roll(rough, shape[0] - 1, 0)), 0.0),
        1: jnp.where(col_open, 2.0 / (rough + pltpu.roll(rough, shape[1] - 1, 1)), 0.0),
    }
    head = depth_ext[...]
    source = source_ext[...]
    for _ in range(3):
        wet = jnp.maximum(head, 0.0)
        section = head + bed
        net = jnp.zeros(shape, F32) - source
        for axis in range(2):
            back = shape[axis] - 1
            slope = pltpu.roll(section, back, axis) - section
            mean = 0.5 * (wet + pltpu.roll(wet, back, axis))
            flux = (
                jnp.exp2((5.0 / 3.0) * jnp.log2(mean))
                * inverse[axis]
                * slope
                * lax.rsqrt(jnp.abs(slope) + SLOPE_FLOOR)
            )
            net = net + flux - pltpu.roll(flux, 1, axis)
        head = head + SURF_STEP * net
    out_ref[...] = head[8:136, 128:384]


def sweeps(place, water_depth, *rest):
    shape = (144, 512)
    return pl.pallas_call(
        functools.partial(sweep_kernel, place),
        in_specs=[VMEM] * 10 + [ANY],
        out_specs=VMEM,
        out_shape=jax.ShapeDtypeStruct(water_depth.shape, F32),
        scratch_shapes=[pltpu.VMEM(shape, F32)] * 4 + [pltpu.VMEM((128, 128), F32)],
        compiler_params=pltpu.CompilerParams(vmem_limit_bytes=VMEM_LIMIT),
        name="sweeps",
    )(water_depth, *rest)


def halo_tile(soil_ref, classes, source, slot, table, turned, cond):
    for half in range(TILE // 128):
        lanes = slice(128 * half, 128 * half + 128)
        turned[half] = source(lanes).T
        soil = soil_rows(soil_ref, classes(lanes))
        for k in range(8):
            rows = slice(64 * k, 64 * k + 64)
            cond[half, rows, :] = curve(turned[half, rows, :], soil)[0]
        write_faces(turned, cond, half, slot, table)


def inner_tile(soil_ref, class_ref, level_ref, head_ref, slot, table, turned, cond, base_sc, factor_sc, top_ref):
    open_i = iota((8, 8, 128), 1) < 7
    nothing = jnp.zeros((1, 8, 128), F32)
    for half in range(TILE // 128):
        lanes = slice(128 * half, 128 * half + 128)
        at = 2 * (slot - 1) + half
        turned[half] = head_ref[lanes, :].T
        soil = soil_rows(soil_ref, class_ref[:, lanes])
        width = cell_width(level_ref[:, lanes])
        half_over = 0.5 / width
        scaled = SUB_STEP / width

        def conduct(k):
            rows = slice(64 * k, 64 * k + 64)
            conductivity, base, ratio = curve(turned[half, rows, :], soil)
            cond[half, rows, :] = conductivity
            factor = scaled * base / (soil[4] * ratio + STORAGE * base)
            factor_sc[at, rows, :] = factor
            if k == 7:
                top_ref[half] = factor

        conduct(0)
        below = None
        for k in range(8):
            if k < 7:
                conduct(k + 1)
            rows = slice(64 * k, 64 * k + 64)
            head = turned[half, rows, :].reshape(8, 8, 128)
            cnd = cond[half, rows, :].reshape(8, 8, 128)
            flux = (cnd + pltpu.roll(cnd, 7, 1)) * (pltpu.roll(head, 7, 1) - head) * half_over
            flux = jnp.where(open_i, flux, 0.0)
            inflow = flux - pltpu.roll(flux, 1, 1)
            flux = (cnd[1:] + cnd[:-1]) * (head[1:] - head[:-1]) * half_over
            inflow = inflow + jnp.concatenate([flux, nothing], 0) - jnp.concatenate([nothing, flux], 0)
            if k < 7:
                above = slice(64 * k + 64, 64 * k + 128)
                head_up = turned[half, above, :].reshape(8, 8, 128)
                cnd_up = cond[half, above, :].reshape(8, 8, 128)
                flux = (cnd + cnd_up) * ((head_up - head) * half_over + 0.5)
                inflow = inflow + flux
            if below is not None:
                inflow = inflow - below
            below = flux
            base_sc[at, rows, :] = (
                turned[half, rows, :] + factor_sc[at, rows, :] * inflow.reshape(64, 128)
            )
        write_faces(turned, cond, half, slot, table)


def face_tile(first_row, levels, near_ref, slot, table, base_sc, factor_sc, out_ref):
    width = cell_width(levels)
    window = pl.ds(pl.multiple_of((slot - 1) * TILE, TILE), 3 * TILE)
    own = pl.ds(pl.multiple_of(slot * TILE, TILE), TILE)
    for face in range(6):
        neighbor = near_ref[face : face + 1, :]
        far_width = cell_width(near_ref[6 + face : 7 + face, :])
        over_gap = 2.0 / (width + far_width)
        half = jnp.where(neighbor >= 0, 0.5, 0.0)
        chosen = as_bf16(iota((3 * TILE, TILE), 0) == neighbor - first_row)
        there = 256 * OPPOSITE[face]
        far = jnp.dot(table[there : there + 256, window], chosen, preferred_element_type=F32)
        near = table[256 * face : 256 * face + 256, own].astype(F32)
        head_diff = (far[0:64] - near[0:64]) + (far[64:128] - near[64:128])
        conds = (far[128:192] + near[128:192]) + (far[192:256] + near[192:256])
        flux = conds * half * (head_diff * over_gap + GRAVITY[face])
        for part in range(TILE // 128):
            at = 2 * (slot - 1) + part
            added = flux[:, 128 * part : 128 * part + 128]
            if face < 2:
                rows = pl.ds(7 * face, 64, stride=8)
                base_sc[at, rows, :] += factor_sc[at, rows, :] * added
            elif face < 4:
                for k in range(8):
                    rows = slice(64 * k + 56 * (face - 2), 64 * k + 56 * (face - 2) + 8)
                    base_sc[at, rows, :] += factor_sc[at, rows, :] * added[8 * k : 8 * k + 8]
            else:
                rows = slice(448 * (face - 4), 448 * (face - 4) + 64)
                base_sc[at, rows, :] += factor_sc[at, rows, :] * added
    for part in range(TILE // 128):
        out_ref[128 * part : 128 * part + 128, :] = base_sc[2 * (slot - 1) + part].T


def cells_kernel(part, inner, width, has_edge, chained, *refs):
    soil_ref, class_ref, level_ref, head_ref, own_ref, near_ref, after_ref = refs[:7]
    edge_ref = refs[7] if has_edge else None
    out_ref, top_ref, table, turned, cond, base_sc, factor_sc = refs[7 + has_edge + chained :]
    step = pl.program_id(0)
    last = inner + 1
    own, _, _ = position(width)
    blocks = inner * TILE

    def at_edge():
        halo_tile(
            soil_ref,
            lambda lanes: edge_ref[HB : HB + 8, lanes][0:1, :].astype(I32),
            lambda lanes: edge_ref[lanes, :],
            step, table, turned, cond,
        )

    def beside():
        halo_tile(
            soil_ref,
            lambda lanes: class_ref[:, lanes],
            lambda lanes: head_ref[lanes, :],
            step, table, turned, cond,
        )

    def within():
        inner_tile(
            soil_ref, class_ref, level_ref, head_ref, step, table, turned, cond, base_sc, factor_sc, top_ref
        )

    def faces():
        slot = step - 2
        first_row = (PARTS * own + part) * blocks + (slot - 2) * TILE
        face_tile(first_row, own_ref[...], near_ref, slot, table, base_sc, factor_sc, out_ref)

    first = at_edge if part == 0 else beside
    final = at_edge if part == PARTS - 1 else beside

    @pl.when(step == 0)
    def _():
        first()

    @pl.when((step > 0) & (step < 3))
    def _():
        within()

    if last > 3:
        @pl.when((step >= 3) & (step < last))
        def _():
            faces()
            within()

    @pl.when(step == last)
    def _():
        faces()
        final()

    @pl.when(step == last + 1)
    def _():
        faces()


def cells(shape, soil, kinds, near, pressure, edge, after, part, head):
    inner = pressure.shape[0] // TILE // PARTS
    tiles = PARTS * inner
    low = part * inner
    extra = [value for value in (edge, head) if value is not None]
    extra_specs = [] if edge is None else [pl.BlockSpec(edge.shape, lambda t: (0, 0))]
    aliases = {}
    if head is not None:
        aliases = {7 + len(extra_specs): 0}
        extra_specs = extra_specs + [ANY]
    seen = lambda t: jnp.clip(t + low - 1, max(low - 1, 0), min(low + inner, tiles - 1))
    done = lambda t: jnp.clip(t + low - 3, low, low + inner - 1)
    return pl.pallas_call(
        functools.partial(
            cells_kernel, part, inner, shape[1], int(edge is not None), int(head is not None)
        ),
        grid=(inner + 3,),
        in_specs=[
            SMEM,
            pl.BlockSpec((1, TILE), lambda t: (0, seen(t))),
            pl.BlockSpec((1, TILE), lambda t: (0, seen(t))),
            pl.BlockSpec((TILE, 512), lambda t: (seen(t), 0)),
            pl.BlockSpec((1, TILE), lambda t: (0, done(t))),
            pl.BlockSpec((near.shape[0], TILE), lambda t: (0, done(t))),
            ANY,
        ]
        + extra_specs,
        out_specs=[
            pl.BlockSpec((TILE, 512), lambda t: (done(t), 0)),
            pl.BlockSpec((TILE // 128, 64, 128), lambda t: (jnp.clip(t - 1, 0, inner - 1), 0, 0)),
        ],
        out_shape=[
            jax.ShapeDtypeStruct(pressure.shape, F32),
            jax.ShapeDtypeStruct((2 * inner, 64, 128), F32),
        ],
        input_output_aliases=aliases,
        scratch_shapes=[
            pltpu.VMEM((1536, (inner + 2) * TILE), BF16),
            pltpu.VMEM((TILE // 128, 512, 128), F32),
            pltpu.VMEM((TILE // 128, 512, 128), F32),
            pltpu.VMEM((2 * inner, 512, 128), F32),
            pltpu.VMEM((2 * inner, 512, 128), F32),
        ],
        compiler_params=pltpu.CompilerParams(vmem_limit_bytes=VMEM_LIMIT),
        cost_estimate=pl.CostEstimate(
            flops=inner * 6 * 2 * 256 * 256 * 768,
            bytes_accessed=inner * TILE * 512 * 16,
            transcendentals=inner * TILE * 512 * 8,
        ),
        name="cells",
    )(soil, *kinds, pressure, kinds[1], near, after, *extra)


def top_kernel(got_ref, match_ref, factor_ref, head_ref, out_ref, packed, turned):
    low_lane = iota((32, 128), 1) < 64
    width = got_ref.shape[0]

    @pl.when(pl.program_id(0) == 0)
    def _():
        for number in range(width):
            lanes = slice(128 * number, 128 * number + 128)
            stay, moved = got_ref[number, 0:32, :], got_ref[number, 32:64, :]
            high, low = split(jnp.where(low_lane, stay, pltpu.roll(moved, 64, 1)))
            packed[0:32, lanes] = high
            packed[64:96, lanes] = low
            high, low = split(jnp.where(low_lane, pltpu.roll(stay, 64, 1), moved))
            packed[32:64, lanes] = high
            packed[96:128, lanes] = low

    blocks = match_ref.shape[1]
    flux = jnp.dot(packed[...], match_ref[...], preferred_element_type=F32)
    flux = flux[0:64] + flux[64:128]
    for part in range(blocks // 128):
        lanes = slice(128 * part, 128 * part + 128)
        turned[part, 0:64, :] = jnp.zeros((64, 128), F32)
        for i in range(8):
            turned[part, pl.ds(64 + i, 8, stride=8), :] = flux[8 * i : 8 * i + 8, lanes]
        turned[part, 64:128, :] = turned[part, 64:128, :] * factor_ref[part]
        out_ref[lanes, :] = head_ref[lanes, :] + turned[part].T


def top(got, match, factors, head):
    blocks = head.shape[0]
    part = 2 * TILE
    steps = blocks // part

    def kernel(got_ref, match_ref, *refs):
        head_ref, out_ref, packed, turned = refs[steps:]
        for number in range(steps):
            @pl.when(pl.program_id(0) == number)
            def _():
                top_kernel(got_ref, match_ref, refs[number], head_ref, out_ref, packed, turned)

    return pl.pallas_call(
        kernel,
        grid=(steps,),
        in_specs=[
            pl.BlockSpec(got.shape, lambda t: (0, 0, 0)),
            pl.BlockSpec((match.shape[0], part), lambda t: (0, t)),
        ]
        + [pl.BlockSpec(factors[0].shape, lambda t: (0, 0, 0))] * steps
        + [pl.BlockSpec((part, 128), lambda t: (t, 3))],
        out_specs=pl.BlockSpec((part, 128), lambda t: (t, 3)),
        out_shape=jax.ShapeDtypeStruct(head.shape, F32),
        input_output_aliases={2 + steps: 0},
        scratch_shapes=[
            pltpu.VMEM((128, got.shape[0] * 128), BF16),
            pltpu.VMEM((part // 128, 128, 128), F32),
        ],
        compiler_params=pltpu.CompilerParams(vmem_limit_bytes=VMEM_LIMIT),
        name="top",
    )(got, match, *factors, head)


def shifted(value, axis, steps, wrap=True):
    count = lax.axis_size(axis)
    pairs = [(i, (i + steps) % count) for i in range(count) if wrap or 0 <= i + steps < count]
    return lax.ppermute(value, axis, pairs)


def per_device(pressure, soil_class, levels, neighbors, neighbor_levels, patch_of_block, soil_params,
               water_depth, bed_height, roughness):
    blocks = pressure.shape[0]
    rows, cols = water_depth.shape
    patches = rows // 8 * (cols // 8)
    shape = (lax.axis_size("gx"), lax.axis_size("gy"))
    width = shape[1]
    gy = lax.axis_index("gy")
    kinds = [value.reshape(1, blocks) for value in (soil_class, levels)]
    patch = patch_of_block.reshape(1, blocks)
    near = jnp.concatenate([neighbors.T, neighbor_levels.T], axis=0)

    def edge(part):
        classes = jnp.pad(soil_class[part].astype(F32)[None], ((0, 7), (0, 512 - HB)))
        return jnp.concatenate([pressure[part], classes], axis=0)

    low_edge = shifted(edge(slice(blocks - HB, blocks)), ("gx", "gy"), 1, wrap=False)
    high_edge = shifted(edge(slice(0, HB)), ("gx", "gy"), -1, wrap=False)

    send, slot, edge_rows, match = route(
        shape, kinds + [patch], pressure, water_depth, bed_height, roughness
    )
    got = lax.all_to_all(send, "gy", 0, 0)
    head, top_1 = cells(shape, soil_params, kinds, near, pressure, None, slot, 1, None)
    got, top_1 = lax.optimization_barrier((got, top_1))
    halos = got[:, 72:88]
    west = lax.dynamic_index_in_dim(halos, jnp.maximum(gy - 1, 0), 0, keepdims=False)
    east = lax.dynamic_index_in_dim(halos, jnp.minimum(gy + 1, width - 1), 0, keepdims=False)
    moving = got[:, 32:72].reshape(40 * width, 128)
    up = jnp.concatenate([moving, edge_rows[1], west, east], axis=0)
    down = jnp.concatenate([moving, edge_rows[0], west, east], axis=0)
    from_low = shifted(up, "gx", 1)
    from_high = shifted(down, "gx", -1)
    head, top_2 = cells(shape, soil_params, kinds, near, pressure, None, up, 2, head)
    stay, back_high, back_low, tile, edge_cols = surface(
        shape, soil_params, got, from_low, from_high, water_depth, patches, top_2
    )
    back_high = shifted(back_high, "gx", -1)
    back_low = shifted(back_low, "gx", 1)
    head, top_0 = cells(shape, soil_params, kinds, near, pressure, low_edge, stay, 0, head)
    back_low, back_high, top_0 = lax.optimization_barrier((back_low, back_high, top_0))
    number = jnp.arange(width, dtype=I32)[:, None, None]
    answers = 32 * width
    moved = jnp.where(
        number >= gy,
        back_high[:answers].reshape(width, 32, 128),
        back_low[:answers].reshape(width, 32, 128),
    )

    def side(kind):
        lines = slice(answers + 2 * kind, answers + 2 * kind + 2)
        return jnp.concatenate(
            [edge_cols[kind, 0:2], back_low[lines], back_high[lines], jnp.zeros((2, 128), F32)], axis=0
        )

    sides = jnp.where(number == gy + 1, side(1)[None], side(0)[None])
    reply = jnp.concatenate([stay, moved, sides], axis=1)
    returned = lax.all_to_all(reply, "gy", 0, 0)
    head, top_3 = cells(shape, soil_params, kinds, near, pressure, high_edge, reply, 3, head)
    new_depth = sweeps(
        shape, water_depth, bed_height, roughness, got, from_low, from_high, tile,
        back_low, back_high, returned, head,
    )
    new_pressure = top(returned, match, (top_0, top_1, top_2, top_3), head)
    return new_pressure, new_depth


def solution(mesh):
    blocks = P(("gx", "gy"))
    wide = P(("gx", "gy"), None)
    tile = P("gx", "gy")
    return jax.shard_map(
        per_device,
        mesh=mesh,
        in_specs=(wide, blocks, blocks, wide, wide, blocks, P(), tile, tile, tile),
        out_specs=(wide, tile),
        check_vma=False,
    )
```

```python
import functools

import jax
import jax.numpy as jnp
from jax import lax
from jax.experimental import pallas as pl
from jax.experimental.pallas import tpu as pltpu
from jax.sharding import PartitionSpec as P

F32 = jnp.float32
BF16 = jnp.bfloat16
I32 = jnp.int32

HB = 256
TILE = 256
PARTS = ((0, 3), (3, 2), (5, 3))
SLOTS = 64
GROUPS = 16
STORAGE = 0.05
SUB_STEP = 0.02
SURF_STEP = 0.003
SLOPE_FLOOR = 0.01
OPPOSITE = (1, 0, 3, 2, 5, 4)
GRAVITY = (0.0, 0.0, 0.0, 0.0, -1.0, 1.0)
VMEM_LIMIT = 60 * 1024 * 1024

VMEM = pl.BlockSpec(memory_space=pltpu.VMEM)
SMEM = pl.BlockSpec(memory_space=pltpu.SMEM)
ANY = pl.BlockSpec(memory_space=pl.ANY)


def position(width):
    gx, gy = lax.axis_index("gx"), lax.axis_index("gy")
    return gx * width + gy, gx, gy


def split(value):
    high = value.astype(BF16)
    low = (value - high.astype(F32)).astype(BF16)
    return high, low


def iota(shape, dim):
    return lax.broadcasted_iota(I32, shape, dim)


def as_bf16(mask):
    return jnp.where(mask, 1.0, 0.0).astype(BF16)


def cell_width(levels):
    return jnp.where(levels == 0, 0.25, jnp.where(levels == 1, 0.5, 1.0)).astype(F32)


def soil_rows(soil_ref, classes):
    rows = []
    for row in range(5):
        value = jnp.full(classes.shape, soil_ref[row, 0], F32)
        for cls in range(1, soil_ref.shape[1]):
            value = jnp.where(classes == cls, soil_ref[row, cls], value)
        rows.append(value)
    residual, saturated, alpha, power, cond = rows
    exponent = 1.0 - 1.0 / power
    return alpha, power - 1.0, -0.5 * exponent, cond, (saturated - residual) * alpha * (exponent * power)


def curve(pressure, soil):
    alpha, lesser, half, _, _ = soil
    suction = alpha * jnp.maximum(-pressure, 0.0)
    powered = jnp.exp2(lesser * jnp.log2(suction))
    base = 1.0 + powered * suction
    root = jnp.exp2(half * jnp.log2(base))
    ratio = powered * (root * root)
    rest = 1.0 - ratio
    conductivity = soil[3] * root * (rest * rest)
    return conductivity, base, ratio


def face_rows(ref, half, face):
    if face < 2:
        return ref[half, pl.ds(7 * face, 64, stride=8), :]
    if face < 4:
        start = 56 * (face - 2)
        return jnp.concatenate([ref[half, 64 * k + start : 64 * k + start + 8, :] for k in range(8)], axis=0)
    start = 448 * (face - 4)
    return ref[half, start : start + 64, :]


def write_faces(head_ref, cond_ref, half, slot, table):
    lanes = pl.ds(pl.multiple_of(slot * TILE, TILE) + 128 * half, 128)
    for face in range(6):
        head_high, head_low = split(face_rows(head_ref, half, face))
        cond_high, cond_low = split(face_rows(cond_ref, half, face))
        for part, value in enumerate((head_high, head_low, cond_high, cond_low)):
            row = 256 * face + 64 * part
            table[row : row + 64, lanes] = value


def route_kernel(shape, class_ref, level_ref, patch_ref, top_ref, depth_ref, bed_ref, rough_ref,
                 send_ref, slot_ref, rows_ref, turned, packed, edges):
    own, _, gy = position(shape[1])
    route_once(own, gy, shape, class_ref, level_ref, patch_ref, top_ref, depth_ref, bed_ref, rough_ref,
               slot_ref, rows_ref, turned, packed, edges)
    blocks = patch_ref.shape[1]
    low_lane = iota((32, 128), 1) < 64
    for number in range(send_ref.shape[0]):
        wanted = as_bf16(iota((128, blocks), 0) == slot_ref[...] - 128 * number)
        out = lax.dot_general(packed[...], wanted, (((1,), (1,)), ((), ())), preferred_element_type=F32)
        first = out[0:32] + out[64:96]
        second = out[32:64] + out[96:128]
        send_ref[number, 0:32, :] = jnp.where(low_lane, first, pltpu.roll(second, 64, 1))
        send_ref[number, 32:64, :] = jnp.where(low_lane, pltpu.roll(first, 64, 1), second)
        label = out[130:131] * (out[128:129] + 256.0 * out[129:130] + 1.0) - 1.0
        row = iota((8, 128), 0)
        send_ref[number, 64:72, :] = jnp.where(row == 0, label, jnp.where(row == 1, out[131:132], out[132:133]))
        send_ref[number, 72:88, :] = jnp.where(number == gy + 1, edges[1], edges[0])


def route_once(own, gy, shape, class_ref, level_ref, patch_ref, top_ref, depth_ref, bed_ref, rough_ref,
               slot_ref, rows_ref, turned, packed, edges):
    devices, width = shape[0] * shape[1], shape[1]
    blocks = patch_ref.shape[1]
    patch = patch_ref[...]
    is_top = patch >= 0
    safe = jnp.where(is_top, patch, 0)
    offset = lax.rem(lax.shift_right_logical(safe, 9) - own + (GROUPS // 2 - 1) + devices, devices) - (GROUPS // 2 - 1)
    column = gy + offset
    moved = (column < 0) | (column >= width)
    group = 2 * lax.rem(column + width, width) + moved.astype(I32)
    upper = as_bf16(iota((TILE, TILE), 0) < iota((TILE, TILE), 1))
    carry = jnp.zeros((GROUPS, 1), F32)
    for part in range(blocks // TILE):
        lanes = slice(part * TILE, (part + 1) * TILE)
        member = jnp.where(
            (iota((GROUPS, TILE), 0) == group[:, lanes]) & is_top[:, lanes], 1.0, 0.0
        )
        before = jnp.dot(member.astype(BF16), upper, preferred_element_type=F32) + carry
        rank = jnp.sum(member * before, axis=0, keepdims=True)
        carry = carry + jnp.sum(member, axis=1, keepdims=True)
        slot_ref[:, lanes] = jnp.where(
            is_top[:, lanes], group[:, lanes] * SLOTS + rank.astype(I32), -1
        )
        for half in (2 * part, 2 * part + 1):
            turned[half] = top_ref[128 * half : 128 * half + 128, :].T
    for half in range(blocks // 128):
        lanes = slice(128 * half, 128 * half + 128)
        heads = jnp.concatenate(
            [turned[half, pl.ds(64 + i, 8, stride=8), :] for i in range(8)], axis=0
        )
        high, low = split(heads)
        packed[0:64, lanes] = high
        packed[64:128, lanes] = low
    place = jnp.bitwise_and(safe, 511)
    row = iota((16, blocks), 0)
    tags = jnp.where(row == 0, jnp.bitwise_and(place, 255), 0)
    tags = jnp.where(row == 1, lax.shift_right_logical(place, 8), tags)
    tags = jnp.where(row == 2, 1, tags)
    tags = jnp.where(row == 3, class_ref[...], tags)
    tags = jnp.where(row == 4, level_ref[...], tags)
    packed[128:144, :] = tags.astype(F32).astype(BF16)
    for number, field in enumerate((depth_ref, bed_ref, rough_ref)):
        edges[0, 3 * number : 3 * number + 3, :] = field[:, 0:128].T[0:3, :]
        edges[1, 3 * number : 3 * number + 3, :] = field[:, 128:256].T[125:128, :]
        for half in range(2):
            at = 3 * (2 * number + half)
            lanes = slice(128 * half, 128 * half + 128)
            rows_ref[0, at : at + 3, :] = field[0:3, lanes]
            rows_ref[1, at : at + 3, :] = field[125:128, lanes]


def route(shape, kinds, pressure, water_depth, bed_height, roughness):
    blocks = pressure.shape[0]
    width = shape[1]
    row = pl.BlockSpec((1, blocks), lambda t: (0, 0))
    return pl.pallas_call(
        functools.partial(route_kernel, shape),
        grid=(1,),
        in_specs=[
            row,
            row,
            row,
            pl.BlockSpec((blocks, 128), lambda t: (0, 3)),
            pl.BlockSpec(water_depth.shape, lambda t: (0, 0)),
            pl.BlockSpec(water_depth.shape, lambda t: (0, 0)),
            pl.BlockSpec(water_depth.shape, lambda t: (0, 0)),
        ],
        out_specs=[
            pl.BlockSpec((width, 88, 128), lambda t: (0, 0, 0)),
            pl.BlockSpec((1, blocks), lambda t: (0, 0)),
            pl.BlockSpec((2, 24, 128), lambda t: (0, 0, 0)),
        ],
        out_shape=[
            jax.ShapeDtypeStruct((width, 88, 128), F32),
            jax.ShapeDtypeStruct((1, blocks), I32),
            jax.ShapeDtypeStruct((2, 24, 128), F32),
        ],
        scratch_shapes=[
            pltpu.VMEM((blocks // 128, 128, 128), F32),
            pltpu.VMEM((144, blocks), BF16),
            pltpu.VMEM((2, 16, 128), F32),
        ],
        compiler_params=pltpu.CompilerParams(vmem_limit_bytes=VMEM_LIMIT),
        name="route",
    )(*kinds, pressure, water_depth, bed_height, roughness)


def surface_kernel(shape, soil_ref, got_ref, up_ref, down_ref, depth_ref, after_ref,
                   stay_ref, back_high_ref, back_low_ref, tile_ref, cols_ref, packed, labels, match):
    _, _, gy = position(shape[1])
    low_lane = iota((32, 128), 1) < 64
    tag_low = iota((8, 128), 1) < 64
    width = got_ref.shape[0]
    slots = width * 128
    patches = match.shape[0]
    for source in range(width):
        lanes = slice(128 * source, 128 * source + 128)
        at = 40 * source
        from_up = source >= gy
        stay = got_ref[source, 0:32, :]
        moved = jnp.where(from_up, up_ref[at : at + 32, :], down_ref[at : at + 32, :])
        high, low = split(jnp.where(low_lane, stay, pltpu.roll(moved, 64, 1)))
        packed[0:32, lanes] = high
        packed[64:96, lanes] = low
        high, low = split(jnp.where(low_lane, pltpu.roll(stay, 64, 1), moved))
        packed[32:64, lanes] = high
        packed[96:128, lanes] = low
        tags = jnp.where(
            tag_low,
            got_ref[source, 64:72, :],
            jnp.where(from_up, up_ref[at + 32 : at + 40, :], down_ref[at + 32 : at + 40, :]),
        )
        labels[:, lanes] = (tags[0:1, :] + 0.5).astype(I32) - jnp.where(tags[0:1, :] < 0, 1, 0)
        row = iota((16, 128), 0)
        packed[128:144, lanes] = jnp.where(row == 0, tags[1:2, :], tags[2:3, :]).astype(BF16)
    for part in range(patches // 128):
        match[128 * part : 128 * part + 128, :] = as_bf16(
            iota((128, slots), 0) + 128 * part == labels[...]
        )
    placed = lax.dot_general(
        packed[...], match[...], (((1,), (1,)), ((), ())), preferred_element_type=F32
    )
    classes = (placed[128:129] + 0.5).astype(I32)
    levels = (placed[129:130] + 0.5).astype(I32)
    soil = soil_rows(soil_ref, classes)
    half_cell = 0.5 * cell_width(levels)
    head = placed[0:64] + placed[64:128]
    conductivity, _, _ = curve(head, soil)
    row_of = lax.shift_right_logical(iota((128, patches), 0), 3)
    own_row = row_of == lax.shift_right_logical(iota((128, patches), 1), 5)
    depth_high, depth_low = split(depth_ref[...])
    depth_both = jnp.concatenate([depth_high, depth_low], axis=0)
    cols = depth_ref.shape[1]
    pieces = []
    for i in range(8):
        pick = as_bf16(iota((cols, patches), 0) == 8 * jnp.bitwise_and(iota((cols, patches), 1), 31) + i)
        spread = jnp.dot(depth_both, pick, preferred_element_type=F32)
        spread = jnp.where(own_row, spread[0:128] + spread[128:256], 0.0)
        pieces.append(jnp.sum(spread.reshape(16, 8, patches), axis=0))
    depth = jnp.concatenate(pieces, axis=0)
    infiltration = jnp.minimum(
        conductivity / half_cell * (depth - (head - half_cell)), depth / (3.0 * SURF_STEP)
    )
    high, low = split(infiltration)
    both = jnp.concatenate([high, low], axis=0)
    answer = jnp.dot(both, match[...], preferred_element_type=F32)
    answer = answer[0:64] + answer[64:128]
    for source in range(width):
        lanes = slice(128 * source, 128 * source + 128)
        first, second = answer[0:32, lanes], answer[32:64, lanes]
        stay_ref[source] = jnp.where(low_lane, first, pltpu.roll(second, 64, 1))
        moved = jnp.where(low_lane, pltpu.roll(first, 64, 1), second)
        back_high_ref[32 * source : 32 * source + 32, :] = moved
        back_low_ref[32 * source : 32 * source + 32, :] = moved
    total = jnp.zeros(depth_ref.shape, F32)
    for i in range(8):
        pick = as_bf16(iota((patches, cols), 1) == 8 * jnp.bitwise_and(iota((patches, cols), 0), 31) + i)
        rows = jnp.concatenate([infiltration[8 * i : 8 * i + 8]] * 16, axis=0)
        high, low = split(jnp.where(own_row, rows, 0.0))
        spread = jnp.dot(jnp.concatenate([high, low], axis=0), pick, preferred_element_type=F32)
        total = total + (spread[0:128] + spread[128:256])
    tile_ref[...] = total
    base = 32 * width
    for half in range(2):
        lanes = slice(128 * half, 128 * half + 128)
        back_high_ref[base + 2 * half : base + 2 * half + 2, :] = total[0:2, lanes]
        back_low_ref[base + 2 * half : base + 2 * half + 2, :] = total[126:128, lanes]
    cols_ref[0, 0:2, :] = total[:, 0:128].T[0:2, :]
    cols_ref[1, 0:2, :] = total[:, 128:256].T[126:128, :]


def surface(shape, soil, got, up, down, water_depth, patches, after):
    width = got.shape[0]
    return pl.pallas_call(
        functools.partial(surface_kernel, shape),
        in_specs=[SMEM, VMEM, VMEM, VMEM, VMEM, ANY],
        out_specs=[VMEM] * 5,
        out_shape=[
            jax.ShapeDtypeStruct((width, 32, 128), F32),
            jax.ShapeDtypeStruct((32 * width + 8, 128), F32),
            jax.ShapeDtypeStruct((32 * width + 8, 128), F32),
            jax.ShapeDtypeStruct(water_depth.shape, F32),
            jax.ShapeDtypeStruct((2, 8, 128), F32),
        ],
        scratch_shapes=[
            pltpu.VMEM((144, width * 128), BF16),
            pltpu.VMEM((1, width * 128), I32),
            pltpu.VMEM((patches, width * 128), BF16),
        ],
        compiler_params=pltpu.CompilerParams(vmem_limit_bytes=VMEM_LIMIT),
        name="surface",
    )(soil, got, up, down, water_depth, after)


def sweep_kernel(place, depth_ref, bed_ref, rough_ref, got_ref, up_ref, down_ref,
                 source_ref, low_ref, high_ref, back_ref, slot_ref, factor_0, factor_1, factor_2, head_ref,
                 out_ref, new_ref, depth_ext, bed_ext, rough_ext, source_ext, turn, slab, packed, turned, loaded, stored):
    blocks = slab.shape[0]
    top_lanes = pl.ds(384, 128)
    load = pltpu.make_async_copy(head_ref.at[:, top_lanes], slab, loaded)
    load.start()
    _, gx, gy = position(place[1])
    left_at, right_at = jnp.maximum(gy - 1, 0), jnp.minimum(gy + 1, place[1] - 1)
    rows_total, cols_total = depth_ref.shape[0] * place[0], depth_ref.shape[1] * place[1]
    shape = depth_ext.shape
    halo = 40 * got_ref.shape[0]
    edge = 32 * got_ref.shape[0]
    depth_ext[...] = jnp.zeros(shape, F32)
    bed_ext[...] = jnp.zeros(shape, F32)
    rough_ext[...] = jnp.ones(shape, F32)
    source_ext[...] = jnp.zeros(shape, F32)
    for number, (ext, field) in enumerate(
        ((depth_ext, depth_ref), (bed_ext, bed_ref), (rough_ext, rough_ref))
    ):
        ext[8:136, 128:384] = field[...]
        for half in range(2):
            at = 3 * (2 * number + half)
            lanes = slice(128 + 128 * half, 256 + 128 * half)
            ext[5:8, lanes] = up_ref[halo + at : halo + at + 3, :]
            ext[136:139, lanes] = down_ref[halo + at : halo + at + 3, :]
        col = 3 * number
        fill = 1.0 if number == 2 else 0.0
        for side, lanes in ((0, slice(0, 128)), (1, slice(384, 512))):
            to = slice(125, 128) if side == 0 else slice(0, 3)
            beside = left_at if side == 0 else right_at
            away = halo + 24 + 16 * side + col
            turn[...] = jnp.full((128, 128), fill, F32)
            turn[to, :] = got_ref[beside, 72:88, :][col : col + 3, :]
            ext[8:136, lanes] = turn[...].T
            turn[to, :] = up_ref[away : away + 3, :]
            ext[0:8, lanes] = turn[...].T[120:128, :]
            turn[to, :] = down_ref[away : away + 3, :]
            ext[136:144, lanes] = turn[...].T[0:8, :]
    source_ext[8:136, 128:384] = source_ref[...]
    for half in range(2):
        lanes = slice(128 + 128 * half, 256 + 128 * half)
        source_ext[6:8, lanes] = low_ref[edge + 2 * half : edge + 2 * half + 2, :]
        source_ext[136:138, lanes] = high_ref[edge + 2 * half : edge + 2 * half + 2, :]
    for side, lanes in ((0, slice(0, 128)), (1, slice(384, 512))):
        to = slice(126, 128) if side == 0 else slice(0, 2)
        ends = back_ref[left_at if side == 0 else right_at, 64:72, :]
        turn[...] = jnp.zeros((128, 128), F32)
        turn[to, :] = ends[0:2, :]
        source_ext[8:136, lanes] = turn[...].T
        source_ext[6:8, lanes] = ends[2:4, :]
        source_ext[136:138, lanes] = ends[4:6, :]
    row_id = gx * depth_ref.shape[0] - 8 + iota(shape, 0)
    col_id = gy * depth_ref.shape[1] - 128 + iota(shape, 1)
    row_open = (row_id >= 0) & (row_id + 1 < rows_total)
    col_open = (col_id >= 0) & (col_id + 1 < cols_total)
    bed = bed_ext[...]
    rough = rough_ext[...]
    inverse = {
        0: jnp.where(row_open, 2.0 / (rough + pltpu.roll(rough, shape[0] - 1, 0)), 0.0),
        1: jnp.where(col_open, 2.0 / (rough + pltpu.roll(rough, shape[1] - 1, 1)), 0.0),
    }
    head = depth_ext[...]
    source = source_ext[...]
    for _ in range(3):
        wet = jnp.maximum(head, 0.0)
        section = head + bed
        net = jnp.zeros(shape, F32) - source
        for axis in range(2):
            back = shape[axis] - 1
            slope = pltpu.roll(section, back, axis) - section
            mean = 0.5 * (wet + pltpu.roll(wet, back, axis))
            flux = (
                jnp.exp2((5.0 / 3.0) * jnp.log2(mean))
                * inverse[axis]
                * slope
                * lax.rsqrt(jnp.abs(slope) + SLOPE_FLOOR)
            )
            net = net + flux - pltpu.roll(flux, 1, axis)
        head = head + SURF_STEP * net
    out_ref[...] = head[8:136, 128:384]
    low_lane = iota((32, 128), 1) < 64
    slots = packed.shape[1]
    for number in range(slots // 128):
        lanes = slice(128 * number, 128 * number + 128)
        stay, moved = back_ref[number, 0:32, :], back_ref[number, 32:64, :]
        high, low = split(jnp.where(low_lane, stay, pltpu.roll(moved, 64, 1)))
        packed[0:32, lanes] = high
        packed[64:96, lanes] = low
        high, low = split(jnp.where(low_lane, pltpu.roll(stay, 64, 1), moved))
        packed[32:64, lanes] = high
        packed[96:128, lanes] = low
    load.wait()
    factors = [(ref, at) for ref in (factor_0, factor_1, factor_2) for at in range(ref.shape[0])]
    turned[:, 0:64, :] = jnp.zeros((TILE // 128, 64, 128), F32)
    stores = []
    for tile in range(blocks // TILE):
        wanted = as_bf16(iota((slots, TILE), 0) == slot_ref[:, TILE * tile : TILE * tile + TILE])
        flux = jnp.dot(packed[...], wanted, preferred_element_type=F32)
        flux = flux[0:64] + flux[64:128]
        for half in range(TILE // 128):
            for i in range(8):
                turned[half, pl.ds(64 + i, 8, stride=8), :] = flux[8 * i : 8 * i + 8, 128 * half : 128 * half + 128]
            ref, at = factors[tile * (TILE // 128) + half]
            turned[half, 64:128, :] = turned[half, 64:128, :] * ref[at]
            rows = slice(TILE * tile + 128 * half, TILE * tile + 128 * half + 128)
            slab[rows, :] = slab[rows, :] + turned[half].T
        rows = pl.ds(TILE * tile, TILE)
        store = pltpu.make_async_copy(slab.at[rows, :], new_ref.at[rows, top_lanes], stored.at[tile])
        store.start()
        stores.append(store)
    for store in stores:
        store.wait()


def finish(place, water_depth, *rest):
    shape = (144, 512)
    head = rest[-1]
    blocks = head.shape[0]
    return pl.pallas_call(
        functools.partial(sweep_kernel, place),
        in_specs=[VMEM] * 14 + [ANY],
        out_specs=[VMEM, ANY],
        out_shape=[
            jax.ShapeDtypeStruct(water_depth.shape, F32),
            jax.ShapeDtypeStruct(head.shape, F32),
        ],
        input_output_aliases={14: 1},
        scratch_shapes=[pltpu.VMEM(shape, F32)] * 4
        + [
            pltpu.VMEM((128, 128), F32),
            pltpu.VMEM((blocks, 128), F32),
            pltpu.VMEM((128, place[1] * 128), BF16),
            pltpu.VMEM((TILE // 128, 128, 128), F32),
            pltpu.SemaphoreType.DMA,
            pltpu.SemaphoreType.DMA((blocks // TILE,)),
        ],
        compiler_params=pltpu.CompilerParams(vmem_limit_bytes=VMEM_LIMIT),
        name="finish",
    )(water_depth, *rest)


def halo_tile(soil_ref, classes, source, slot, table, turned, cond):
    for half in range(TILE // 128):
        lanes = slice(128 * half, 128 * half + 128)
        turned[half] = source(lanes).T
        soil = soil_rows(soil_ref, classes(lanes))
        for k in range(8):
            rows = slice(64 * k, 64 * k + 64)
            cond[half, rows, :] = curve(turned[half, rows, :], soil)[0]
        write_faces(turned, cond, half, slot, table)


def inner_tile(soil_ref, class_ref, level_ref, head_ref, slot, table, turned, cond, base_sc, factor_sc, top_ref):
    open_i = iota((8, 8, 128), 1) < 7
    nothing = jnp.zeros((1, 8, 128), F32)
    for half in range(TILE // 128):
        lanes = slice(128 * half, 128 * half + 128)
        at = 2 * (slot - 1) + half
        turned[half] = head_ref[lanes, :].T
        soil = soil_rows(soil_ref, class_ref[:, lanes])
        width = cell_width(level_ref[:, lanes])
        half_over = 0.5 / width
        scaled = SUB_STEP / width

        def conduct(k):
            rows = slice(64 * k, 64 * k + 64)
            conductivity, base, ratio = curve(turned[half, rows, :], soil)
            cond[half, rows, :] = conductivity
            factor = scaled * base / (soil[4] * ratio + STORAGE * base)
            factor_sc[at, rows, :] = factor
            if k == 7:
                top_ref[half] = factor

        conduct(0)
        below = None
        for k in range(8):
            if k < 7:
                conduct(k + 1)
            rows = slice(64 * k, 64 * k + 64)
            head = turned[half, rows, :].reshape(8, 8, 128)
            cnd = cond[half, rows, :].reshape(8, 8, 128)
            flux = (cnd + pltpu.roll(cnd, 7, 1)) * (pltpu.roll(head, 7, 1) - head) * half_over
            flux = jnp.where(open_i, flux, 0.0)
            inflow = flux - pltpu.roll(flux, 1, 1)
            flux = (cnd[1:] + cnd[:-1]) * (head[1:] - head[:-1]) * half_over
            inflow = inflow + jnp.concatenate([flux, nothing], 0) - jnp.concatenate([nothing, flux], 0)
            if k < 7:
                above = slice(64 * k + 64, 64 * k + 128)
                head_up = turned[half, above, :].reshape(8, 8, 128)
                cnd_up = cond[half, above, :].reshape(8, 8, 128)
                flux = (cnd + cnd_up) * ((head_up - head) * half_over + 0.5)
                inflow = inflow + flux
            if below is not None:
                inflow = inflow - below
            below = flux
            base_sc[at, rows, :] = (
                turned[half, rows, :] + factor_sc[at, rows, :] * inflow.reshape(64, 128)
            )
        write_faces(turned, cond, half, slot, table)


def face_tile(first_row, levels, near_ref, slot, table, base_sc, factor_sc, out_ref):
    width = cell_width(levels)
    window = pl.ds(pl.multiple_of((slot - 1) * TILE, TILE), 3 * TILE)
    own = pl.ds(pl.multiple_of(slot * TILE, TILE), TILE)
    for face in range(6):
        neighbor = near_ref[face : face + 1, :]
        far_width = cell_width(near_ref[6 + face : 7 + face, :])
        over_gap = 2.0 / (width + far_width)
        half = jnp.where(neighbor >= 0, 0.5, 0.0)
        chosen = as_bf16(iota((3 * TILE, TILE), 0) == neighbor - first_row)
        there = 256 * OPPOSITE[face]
        far = jnp.dot(table[there : there + 256, window], chosen, preferred_element_type=F32)
        near = table[256 * face : 256 * face + 256, own].astype(F32)
        head_diff = (far[0:64] - near[0:64]) + (far[64:128] - near[64:128])
        conds = (far[128:192] + near[128:192]) + (far[192:256] + near[192:256])
        flux = conds * half * (head_diff * over_gap + GRAVITY[face])
        for part in range(TILE // 128):
            at = 2 * (slot - 1) + part
            added = flux[:, 128 * part : 128 * part + 128]
            if face < 2:
                rows = pl.ds(7 * face, 64, stride=8)
                base_sc[at, rows, :] += factor_sc[at, rows, :] * added
            elif face < 4:
                for k in range(8):
                    rows = slice(64 * k + 56 * (face - 2), 64 * k + 56 * (face - 2) + 8)
                    base_sc[at, rows, :] += factor_sc[at, rows, :] * added[8 * k : 8 * k + 8]
            else:
                rows = slice(448 * (face - 4), 448 * (face - 4) + 64)
                base_sc[at, rows, :] += factor_sc[at, rows, :] * added
    for part in range(TILE // 128):
        out_ref[128 * part : 128 * part + 128, :] = base_sc[2 * (slot - 1) + part].T


def cells_kernel(low, inner, tiles, width, has_edge, chained, *refs):
    soil_ref, class_ref, level_ref, head_ref, own_ref, near_ref, after_ref = refs[:7]
    edge_ref = refs[7] if has_edge else None
    out_ref, top_ref, table, turned, cond, base_sc, factor_sc = refs[7 + has_edge + chained :]
    step = pl.program_id(0)
    last = inner + 1
    own, _, _ = position(width)

    def at_edge():
        halo_tile(
            soil_ref,
            lambda lanes: edge_ref[HB : HB + 8, lanes][0:1, :].astype(I32),
            lambda lanes: edge_ref[lanes, :],
            step, table, turned, cond,
        )

    def beside():
        halo_tile(
            soil_ref,
            lambda lanes: class_ref[:, lanes],
            lambda lanes: head_ref[lanes, :],
            step, table, turned, cond,
        )

    def within():
        inner_tile(
            soil_ref, class_ref, level_ref, head_ref, step, table, turned, cond, base_sc, factor_sc, top_ref
        )

    def faces():
        slot = step - 2
        first_row = own * tiles * TILE + (low + slot - 2) * TILE
        face_tile(first_row, own_ref[...], near_ref, slot, table, base_sc, factor_sc, out_ref)

    first = at_edge if low == 0 else beside
    final = at_edge if low + inner == tiles else beside

    @pl.when(step == 0)
    def _():
        first()

    @pl.when((step > 0) & (step < 3))
    def _():
        within()

    if last > 3:
        @pl.when((step >= 3) & (step < last))
        def _():
            faces()
            within()

    @pl.when(step == last)
    def _():
        faces()
        final()

    @pl.when(step == last + 1)
    def _():
        faces()


def cells(shape, soil, kinds, near, pressure, edge, after, part, head):
    tiles = pressure.shape[0] // TILE
    low, inner = PARTS[part]
    extra = [value for value in (edge, head) if value is not None]
    extra_specs = [] if edge is None else [pl.BlockSpec(edge.shape, lambda t: (0, 0))]
    aliases = {}
    if head is not None:
        aliases = {7 + len(extra_specs): 0}
        extra_specs = extra_specs + [ANY]
    seen = lambda t: jnp.clip(t + low - 1, max(low - 1, 0), min(low + inner, tiles - 1))
    done = lambda t: jnp.clip(t + low - 3, low, low + inner - 1)
    return pl.pallas_call(
        functools.partial(
            cells_kernel, low, inner, tiles, shape[1], int(edge is not None), int(head is not None)
        ),
        grid=(inner + 3,),
        in_specs=[
            SMEM,
            pl.BlockSpec((1, TILE), lambda t: (0, seen(t))),
            pl.BlockSpec((1, TILE), lambda t: (0, seen(t))),
            pl.BlockSpec((TILE, 512), lambda t: (seen(t), 0)),
            pl.BlockSpec((1, TILE), lambda t: (0, done(t))),
            pl.BlockSpec((near.shape[0], TILE), lambda t: (0, done(t))),
            ANY,
        ]
        + extra_specs,
        out_specs=[
            pl.BlockSpec((TILE, 512), lambda t: (done(t), 0)),
            pl.BlockSpec((TILE // 128, 64, 128), lambda t: (jnp.clip(t - 1, 0, inner - 1), 0, 0)),
        ],
        out_shape=[
            jax.ShapeDtypeStruct(pressure.shape, F32),
            jax.ShapeDtypeStruct((2 * inner, 64, 128), F32),
        ],
        input_output_aliases=aliases,
        scratch_shapes=[
            pltpu.VMEM((1536, (inner + 2) * TILE), BF16),
            pltpu.VMEM((TILE // 128, 512, 128), F32),
            pltpu.VMEM((TILE // 128, 512, 128), F32),
            pltpu.VMEM((2 * inner, 512, 128), F32),
            pltpu.VMEM((2 * inner, 512, 128), F32),
        ],
        compiler_params=pltpu.CompilerParams(vmem_limit_bytes=VMEM_LIMIT),
        cost_estimate=pl.CostEstimate(
            flops=inner * 6 * 2 * 256 * 256 * 768,
            bytes_accessed=inner * TILE * 512 * 16,
            transcendentals=inner * TILE * 512 * 8,
        ),
        name="cells",
    )(soil, *kinds, pressure, kinds[1], near, after, *extra)


def shifted(value, axis, steps, wrap=True):
    count = lax.axis_size(axis)
    pairs = [(i, (i + steps) % count) for i in range(count) if wrap or 0 <= i + steps < count]
    return lax.ppermute(value, axis, pairs)


def per_device(pressure, soil_class, levels, neighbors, neighbor_levels, patch_of_block, soil_params,
               water_depth, bed_height, roughness):
    blocks = pressure.shape[0]
    rows, cols = water_depth.shape
    patches = rows // 8 * (cols // 8)
    shape = (lax.axis_size("gx"), lax.axis_size("gy"))
    width = shape[1]
    gy = lax.axis_index("gy")
    kinds = [value.reshape(1, blocks) for value in (soil_class, levels)]
    patch = patch_of_block.reshape(1, blocks)
    near = jnp.concatenate([neighbors.T, neighbor_levels.T], axis=0)

    send, slot, edge_rows = route(
        shape, kinds + [patch], pressure, water_depth, bed_height, roughness
    )
    later, class_later, send = lax.optimization_barrier((pressure, soil_class, send))

    def edge(part):
        classes = jnp.pad(class_later[part].astype(F32)[None], ((0, 7), (0, 512 - HB)))
        return jnp.concatenate([later[part], classes], axis=0)

    low_edge = shifted(edge(slice(blocks - HB, blocks)), ("gx", "gy"), 1, wrap=False)
    high_edge = shifted(edge(slice(0, HB)), ("gx", "gy"), -1, wrap=False)
    got = lax.all_to_all(send, "gy", 0, 0)
    halos = got[:, 72:88]
    west = lax.dynamic_index_in_dim(halos, jnp.maximum(gy - 1, 0), 0, keepdims=False)
    east = lax.dynamic_index_in_dim(halos, jnp.minimum(gy + 1, width - 1), 0, keepdims=False)
    moving = got[:, 32:72].reshape(40 * width, 128)
    up = jnp.concatenate([moving, edge_rows[1], west, east], axis=0)
    down = jnp.concatenate([moving, edge_rows[0], west, east], axis=0)
    from_low = shifted(up, "gx", 1)
    from_high = shifted(down, "gx", -1)
    head, top_1 = cells(shape, soil_params, kinds, near, pressure, None, up, 1, None)
    stay, back_high, back_low, tile, edge_cols = surface(
        shape, soil_params, got, from_low, from_high, water_depth, patches, top_1
    )
    back_high = shifted(back_high, "gx", -1)
    back_low = shifted(back_low, "gx", 1)
    head, top_0 = cells(shape, soil_params, kinds, near, pressure, low_edge, stay, 0, head)
    back_low, back_high, top_0 = lax.optimization_barrier((back_low, back_high, top_0))
    number = jnp.arange(width, dtype=I32)[:, None, None]
    answers = 32 * width
    moved = jnp.where(
        number >= gy,
        back_high[:answers].reshape(width, 32, 128),
        back_low[:answers].reshape(width, 32, 128),
    )

    def side(kind):
        lines = slice(answers + 2 * kind, answers + 2 * kind + 2)
        return jnp.concatenate(
            [edge_cols[kind, 0:2], back_low[lines], back_high[lines], jnp.zeros((2, 128), F32)], axis=0
        )

    sides = jnp.where(number == gy + 1, side(1)[None], side(0)[None])
    reply = jnp.concatenate([stay, moved, sides], axis=1)
    returned = lax.all_to_all(reply, "gy", 0, 0)
    head, top_2 = cells(shape, soil_params, kinds, near, pressure, high_edge, reply, 2, head)
    new_depth, new_pressure = finish(
        shape, water_depth, bed_height, roughness, got, from_low, from_high, tile,
        back_low, back_high, returned, slot, top_0, top_1, top_2, head,
    )
    return new_pressure, new_depth


def solution(mesh):
    blocks = P(("gx", "gy"))
    wide = P(("gx", "gy"), None)
    tile = P("gx", "gy")
    return jax.shard_map(
        per_device,
        mesh=mesh,
        in_specs=(wide, blocks, blocks, wide, wide, blocks, P(), tile, tile, tile),
        out_specs=(wide, tile),
        check_vma=False,
    )
```

```python
import functools

import jax
import jax.numpy as jnp
from jax import lax
from jax.experimental import pallas as pl
from jax.experimental.pallas import tpu as pltpu
from jax.sharding import PartitionSpec as P

F32 = jnp.float32
BF16 = jnp.bfloat16
I32 = jnp.int32
I16 = jnp.int16

HB = 256
TILE = 256
PARTS = ((0, 3), (3, 2), (5, 3))
SLOTS = 64
GROUPS = 16
STORAGE = 0.05
SUB_STEP = 0.02
SURF_STEP = 0.003
SLOPE_FLOOR = 0.01
OPPOSITE = (1, 0, 3, 2, 5, 4)
GRAVITY = (0.0, 0.0, 0.0, 0.0, -1.0, 1.0)
VMEM_LIMIT = 60 * 1024 * 1024

VMEM = pl.BlockSpec(memory_space=pltpu.VMEM)
SMEM = pl.BlockSpec(memory_space=pltpu.SMEM)
ANY = pl.BlockSpec(memory_space=pl.ANY)


def position(width):
    gx, gy = lax.axis_index("gx"), lax.axis_index("gy")
    return gx * width + gy, gx, gy


def split(value):
    high = value.astype(BF16)
    low = (value - high.astype(F32)).astype(BF16)
    return high, low


def iota(shape, dim):
    return lax.broadcasted_iota(I32, shape, dim)


def as_bf16(mask):
    return jnp.where(mask, 1.0, 0.0).astype(BF16)


def cell_width(levels):
    return jnp.where(levels == 0, 0.25, jnp.where(levels == 1, 0.5, 1.0)).astype(F32)


def soil_rows(soil_ref, classes):
    rows = []
    for row in range(5):
        value = jnp.full(classes.shape, soil_ref[row, 0], F32)
        for cls in range(1, soil_ref.shape[1]):
            value = jnp.where(classes == cls, soil_ref[row, cls], value)
        rows.append(value)
    residual, saturated, alpha, power, cond = rows
    exponent = 1.0 - 1.0 / power
    return alpha, power - 1.0, -0.5 * exponent, cond, (saturated - residual) * alpha * (exponent * power)


def curve(pressure, soil):
    alpha, lesser, half, _, _ = soil
    suction = alpha * jnp.maximum(-pressure, 0.0)
    powered = jnp.exp2(lesser * jnp.log2(suction))
    base = 1.0 + powered * suction
    root = jnp.exp2(half * jnp.log2(base))
    ratio = powered * (root * root)
    rest = 1.0 - ratio
    conductivity = soil[3] * root * (rest * rest)
    return conductivity, base, ratio


def face_rows(ref, half, face):
    if face < 2:
        return ref[half, pl.ds(7 * face, 64, stride=8), :]
    if face < 4:
        start = 56 * (face - 2)
        return jnp.concatenate([ref[half, 64 * k + start : 64 * k + start + 8, :] for k in range(8)], axis=0)
    start = 448 * (face - 4)
    return ref[half, start : start + 64, :]


def write_face(head, conductivity, half, face, slot, table):
    lanes = slice(slot * TILE + 128 * half, slot * TILE + 128 * half + 128)
    for part, value in enumerate(split(head) + split(conductivity)):
        row = 256 * face + 64 * part
        table[row : row + 64, lanes] = value


def route_kernel(shape, class_ref, level_ref, patch_ref, top_ref, depth_ref, bed_ref, rough_ref,
                 send_ref, slot_ref, rows_ref, turned, packed, edges):
    own, _, gy = position(shape[1])
    route_once(own, gy, shape, class_ref, level_ref, patch_ref, top_ref, depth_ref, bed_ref, rough_ref,
               slot_ref, rows_ref, turned, packed, edges)
    blocks = patch_ref.shape[1]
    low_lane = iota((32, 128), 1) < 64
    for number in range(send_ref.shape[0]):
        wanted = as_bf16(iota((128, blocks), 0) == slot_ref[...] - 128 * number)
        out = lax.dot_general(packed[...], wanted, (((1,), (1,)), ((), ())), preferred_element_type=F32)
        first = out[0:32] + out[64:96]
        second = out[32:64] + out[96:128]
        send_ref[number, 0:32, :] = jnp.where(low_lane, first, pltpu.roll(second, 64, 1))
        send_ref[number, 32:64, :] = jnp.where(low_lane, pltpu.roll(first, 64, 1), second)
        label = out[130:131] * (out[128:129] + 256.0 * out[129:130] + 1.0) - 1.0
        row = iota((8, 128), 0)
        send_ref[number, 64:72, :] = jnp.where(row == 0, label, jnp.where(row == 1, out[131:132], out[132:133]))
        send_ref[number, 72:88, :] = jnp.where(number == gy + 1, edges[1], edges[0])


def route_once(own, gy, shape, class_ref, level_ref, patch_ref, top_ref, depth_ref, bed_ref, rough_ref,
               slot_ref, rows_ref, turned, packed, edges):
    devices, width = shape[0] * shape[1], shape[1]
    blocks = patch_ref.shape[1]
    patch = patch_ref[...]
    is_top = patch >= 0
    safe = jnp.where(is_top, patch, 0)
    offset = lax.rem(lax.shift_right_logical(safe, 9) - own + (GROUPS // 2 - 1) + devices, devices) - (GROUPS // 2 - 1)
    column = gy + offset
    moved = (column < 0) | (column >= width)
    group = 2 * lax.rem(column + width, width) + moved.astype(I32)
    upper = as_bf16(iota((TILE, TILE), 0) < iota((TILE, TILE), 1))
    carry = jnp.zeros((GROUPS, 1), F32)
    for part in range(blocks // TILE):
        lanes = slice(part * TILE, (part + 1) * TILE)
        member = jnp.where(
            (iota((GROUPS, TILE), 0) == group[:, lanes]) & is_top[:, lanes], 1.0, 0.0
        )
        before = jnp.dot(member.astype(BF16), upper, preferred_element_type=F32) + carry
        rank = jnp.sum(member * before, axis=0, keepdims=True)
        carry = carry + jnp.sum(member, axis=1, keepdims=True)
        slot_ref[:, lanes] = jnp.where(
            is_top[:, lanes], group[:, lanes] * SLOTS + rank.astype(I32), -1
        )
        for half in (2 * part, 2 * part + 1):
            turned[half] = top_ref[128 * half : 128 * half + 128, :].T
    for half in range(blocks // 128):
        lanes = slice(128 * half, 128 * half + 128)
        heads = jnp.concatenate(
            [turned[half, pl.ds(64 + i, 8, stride=8), :] for i in range(8)], axis=0
        )
        high, low = split(heads)
        packed[0:64, lanes] = high
        packed[64:128, lanes] = low
    place = jnp.bitwise_and(safe, 511)
    row = iota((16, blocks), 0)
    tags = jnp.where(row == 0, jnp.bitwise_and(place, 255), 0)
    tags = jnp.where(row == 1, lax.shift_right_logical(place, 8), tags)
    tags = jnp.where(row == 2, 1, tags)
    tags = jnp.where(row == 3, class_ref[...], tags)
    tags = jnp.where(row == 4, level_ref[...], tags)
    packed[128:144, :] = tags.astype(F32).astype(BF16)
    for number, field in enumerate((depth_ref, bed_ref, rough_ref)):
        edges[0, 3 * number : 3 * number + 3, :] = field[:, 0:128].T[0:3, :]
        edges[1, 3 * number : 3 * number + 3, :] = field[:, 128:256].T[125:128, :]
        for half in range(2):
            at = 3 * (2 * number + half)
            lanes = slice(128 * half, 128 * half + 128)
            rows_ref[0, at : at + 3, :] = field[0:3, lanes]
            rows_ref[1, at : at + 3, :] = field[125:128, lanes]


def route(shape, kinds, pressure, water_depth, bed_height, roughness):
    blocks = pressure.shape[0]
    width = shape[1]
    row = pl.BlockSpec((1, blocks), lambda t: (0, 0))
    return pl.pallas_call(
        functools.partial(route_kernel, shape),
        grid=(1,),
        in_specs=[
            row,
            row,
            row,
            pl.BlockSpec((blocks, 128), lambda t: (0, 3)),
            pl.BlockSpec(water_depth.shape, lambda t: (0, 0)),
            pl.BlockSpec(water_depth.shape, lambda t: (0, 0)),
            pl.BlockSpec(water_depth.shape, lambda t: (0, 0)),
        ],
        out_specs=[
            pl.BlockSpec((width, 88, 128), lambda t: (0, 0, 0)),
            pl.BlockSpec((1, blocks), lambda t: (0, 0)),
            pl.BlockSpec((2, 24, 128), lambda t: (0, 0, 0)),
        ],
        out_shape=[
            jax.ShapeDtypeStruct((width, 88, 128), F32),
            jax.ShapeDtypeStruct((1, blocks), I32),
            jax.ShapeDtypeStruct((2, 24, 128), F32),
        ],
        scratch_shapes=[
            pltpu.VMEM((blocks // 128, 128, 128), F32),
            pltpu.VMEM((144, blocks), BF16),
            pltpu.VMEM((2, 16, 128), F32),
        ],
        compiler_params=pltpu.CompilerParams(vmem_limit_bytes=VMEM_LIMIT),
        name="route",
    )(*kinds, pressure, water_depth, bed_height, roughness)


def surface_kernel(shape, soil_ref, got_ref, up_ref, down_ref, depth_ref, after_ref,
                   stay_ref, back_high_ref, back_low_ref, tile_ref, cols_ref, packed, labels, match):
    _, _, gy = position(shape[1])
    low_lane = iota((32, 128), 1) < 64
    tag_low = iota((8, 128), 1) < 64
    width = got_ref.shape[0]
    slots = width * 128
    patches = match.shape[0]
    for source in range(width):
        lanes = slice(128 * source, 128 * source + 128)
        at = 40 * source
        from_up = source >= gy
        stay = got_ref[source, 0:32, :]
        moved = jnp.where(from_up, up_ref[at : at + 32, :], down_ref[at : at + 32, :])
        high, low = split(jnp.where(low_lane, stay, pltpu.roll(moved, 64, 1)))
        packed[0:32, lanes] = high
        packed[64:96, lanes] = low
        high, low = split(jnp.where(low_lane, pltpu.roll(stay, 64, 1), moved))
        packed[32:64, lanes] = high
        packed[96:128, lanes] = low
        tags = jnp.where(
            tag_low,
            got_ref[source, 64:72, :],
            jnp.where(from_up, up_ref[at + 32 : at + 40, :], down_ref[at + 32 : at + 40, :]),
        )
        labels[:, lanes] = (tags[0:1, :] + 0.5).astype(I32) - jnp.where(tags[0:1, :] < 0, 1, 0)
        row = iota((16, 128), 0)
        packed[128:144, lanes] = jnp.where(row == 0, tags[1:2, :], tags[2:3, :]).astype(BF16)
    for part in range(patches // 128):
        match[128 * part : 128 * part + 128, :] = as_bf16(
            iota((128, slots), 0) + 128 * part == labels[...]
        )
    placed = lax.dot_general(
        packed[...], match[...], (((1,), (1,)), ((), ())), preferred_element_type=F32
    )
    classes = (placed[128:129] + 0.5).astype(I32)
    levels = (placed[129:130] + 0.5).astype(I32)
    soil = soil_rows(soil_ref, classes)
    half_cell = 0.5 * cell_width(levels)
    head = placed[0:64] + placed[64:128]
    conductivity, _, _ = curve(head, soil)
    row_of = lax.shift_right_logical(iota((128, patches), 0), 3)
    own_row = row_of == lax.shift_right_logical(iota((128, patches), 1), 5)
    depth_high, depth_low = split(depth_ref[...])
    depth_both = jnp.concatenate([depth_high, depth_low], axis=0)
    cols = depth_ref.shape[1]
    pieces = []
    for i in range(8):
        pick = as_bf16(iota((cols, patches), 0) == 8 * jnp.bitwise_and(iota((cols, patches), 1), 31) + i)
        spread = jnp.dot(depth_both, pick, preferred_element_type=F32)
        spread = jnp.where(own_row, spread[0:128] + spread[128:256], 0.0)
        pieces.append(jnp.sum(spread.reshape(16, 8, patches), axis=0))
    depth = jnp.concatenate(pieces, axis=0)
    infiltration = jnp.minimum(
        conductivity / half_cell * (depth - (head - half_cell)), depth / (3.0 * SURF_STEP)
    )
    high, low = split(infiltration)
    both = jnp.concatenate([high, low], axis=0)
    answer = jnp.dot(both, match[...], preferred_element_type=F32)
    answer = answer[0:64] + answer[64:128]
    for source in range(width):
        lanes = slice(128 * source, 128 * source + 128)
        first, second = answer[0:32, lanes], answer[32:64, lanes]
        stay_ref[source] = jnp.where(low_lane, first, pltpu.roll(second, 64, 1))
        moved = jnp.where(low_lane, pltpu.roll(first, 64, 1), second)
        back_high_ref[32 * source : 32 * source + 32, :] = moved
        back_low_ref[32 * source : 32 * source + 32, :] = moved
    total = jnp.zeros(depth_ref.shape, F32)
    for i in range(8):
        pick = as_bf16(iota((patches, cols), 1) == 8 * jnp.bitwise_and(iota((patches, cols), 0), 31) + i)
        rows = jnp.concatenate([infiltration[8 * i : 8 * i + 8]] * 16, axis=0)
        high, low = split(jnp.where(own_row, rows, 0.0))
        spread = jnp.dot(jnp.concatenate([high, low], axis=0), pick, preferred_element_type=F32)
        total = total + (spread[0:128] + spread[128:256])
    tile_ref[...] = total
    base = 32 * width
    for half in range(2):
        lanes = slice(128 * half, 128 * half + 128)
        back_high_ref[base + 2 * half : base + 2 * half + 2, :] = total[0:2, lanes]
        back_low_ref[base + 2 * half : base + 2 * half + 2, :] = total[126:128, lanes]
    cols_ref[0, 0:2, :] = total[:, 0:128].T[0:2, :]
    cols_ref[1, 0:2, :] = total[:, 128:256].T[126:128, :]


def surface(shape, soil, got, up, down, water_depth, patches, after):
    width = got.shape[0]
    return pl.pallas_call(
        functools.partial(surface_kernel, shape),
        in_specs=[SMEM, VMEM, VMEM, VMEM, VMEM, ANY],
        out_specs=[VMEM] * 5,
        out_shape=[
            jax.ShapeDtypeStruct((width, 32, 128), F32),
            jax.ShapeDtypeStruct((32 * width + 8, 128), F32),
            jax.ShapeDtypeStruct((32 * width + 8, 128), F32),
            jax.ShapeDtypeStruct(water_depth.shape, F32),
            jax.ShapeDtypeStruct((2, 8, 128), F32),
        ],
        scratch_shapes=[
            pltpu.VMEM((144, width * 128), BF16),
            pltpu.VMEM((1, width * 128), I32),
            pltpu.VMEM((patches, width * 128), BF16),
        ],
        compiler_params=pltpu.CompilerParams(vmem_limit_bytes=VMEM_LIMIT),
        name="surface",
    )(soil, got, up, down, water_depth, after)


def sweep_kernel(place, depth_ref, bed_ref, rough_ref, got_ref, up_ref, down_ref,
                 source_ref, low_ref, high_ref, back_ref, slot_ref, factor_0, factor_1, factor_2, head_ref,
                 out_ref, new_ref, depth_ext, bed_ext, rough_ext, source_ext, turn, slab, packed, turned, loaded, stored):
    blocks = slab.shape[0]
    top_lanes = pl.ds(384, 128)
    load = pltpu.make_async_copy(head_ref.at[:, top_lanes], slab, loaded)
    load.start()
    _, gx, gy = position(place[1])
    left_at, right_at = jnp.maximum(gy - 1, 0), jnp.minimum(gy + 1, place[1] - 1)
    rows_total, cols_total = depth_ref.shape[0] * place[0], depth_ref.shape[1] * place[1]
    shape = depth_ext.shape
    halo = 40 * got_ref.shape[0]
    edge = 32 * got_ref.shape[0]
    depth_ext[...] = jnp.zeros(shape, F32)
    bed_ext[...] = jnp.zeros(shape, F32)
    rough_ext[...] = jnp.ones(shape, F32)
    source_ext[...] = jnp.zeros(shape, F32)
    for number, (ext, field) in enumerate(
        ((depth_ext, depth_ref), (bed_ext, bed_ref), (rough_ext, rough_ref))
    ):
        ext[8:136, 128:384] = field[...]
        for half in range(2):
            at = 3 * (2 * number + half)
            lanes = slice(128 + 128 * half, 256 + 128 * half)
            ext[5:8, lanes] = up_ref[halo + at : halo + at + 3, :]
            ext[136:139, lanes] = down_ref[halo + at : halo + at + 3, :]
        col = 3 * number
        fill = 1.0 if number == 2 else 0.0
        for side, lanes in ((0, slice(0, 128)), (1, slice(384, 512))):
            to = slice(125, 128) if side == 0 else slice(0, 3)
            beside = left_at if side == 0 else right_at
            away = halo + 24 + 16 * side + col
            turn[...] = jnp.full((128, 128), fill, F32)
            turn[to, :] = got_ref[beside, 72:88, :][col : col + 3, :]
            ext[8:136, lanes] = turn[...].T
            turn[to, :] = up_ref[away : away + 3, :]
            ext[0:8, lanes] = turn[...].T[120:128, :]
            turn[to, :] = down_ref[away : away + 3, :]
            ext[136:144, lanes] = turn[...].T[0:8, :]
    source_ext[8:136, 128:384] = source_ref[...]
    for half in range(2):
        lanes = slice(128 + 128 * half, 256 + 128 * half)
        source_ext[6:8, lanes] = low_ref[edge + 2 * half : edge + 2 * half + 2, :]
        source_ext[136:138, lanes] = high_ref[edge + 2 * half : edge + 2 * half + 2, :]
    for side, lanes in ((0, slice(0, 128)), (1, slice(384, 512))):
        to = slice(126, 128) if side == 0 else slice(0, 2)
        ends = back_ref[left_at if side == 0 else right_at, 64:72, :]
        turn[...] = jnp.zeros((128, 128), F32)
        turn[to, :] = ends[0:2, :]
        source_ext[8:136, lanes] = turn[...].T
        source_ext[6:8, lanes] = ends[2:4, :]
        source_ext[136:138, lanes] = ends[4:6, :]
    row_id = gx * depth_ref.shape[0] - 8 + iota(shape, 0)
    col_id = gy * depth_ref.shape[1] - 128 + iota(shape, 1)
    row_open = (row_id >= 0) & (row_id + 1 < rows_total)
    col_open = (col_id >= 0) & (col_id + 1 < cols_total)
    bed = bed_ext[...]
    rough = rough_ext[...]
    inverse = {
        0: jnp.where(row_open, 2.0 / (rough + pltpu.roll(rough, shape[0] - 1, 0)), 0.0),
        1: jnp.where(col_open, 2.0 / (rough + pltpu.roll(rough, shape[1] - 1, 1)), 0.0),
    }
    head = depth_ext[...]
    source = source_ext[...]
    for _ in range(3):
        wet = jnp.maximum(head, 0.0)
        section = head + bed
        net = jnp.zeros(shape, F32) - source
        for axis in range(2):
            back = shape[axis] - 1
            slope = pltpu.roll(section, back, axis) - section
            mean = 0.5 * (wet + pltpu.roll(wet, back, axis))
            flux = (
                jnp.exp2((5.0 / 3.0) * jnp.log2(mean))
                * inverse[axis]
                * slope
                * lax.rsqrt(jnp.abs(slope) + SLOPE_FLOOR)
            )
            net = net + flux - pltpu.roll(flux, 1, axis)
        head = head + SURF_STEP * net
    out_ref[...] = head[8:136, 128:384]
    low_lane = iota((32, 128), 1) < 64
    slots = packed.shape[1]
    for number in range(slots // 128):
        lanes = slice(128 * number, 128 * number + 128)
        stay, moved = back_ref[number, 0:32, :], back_ref[number, 32:64, :]
        high, low = split(jnp.where(low_lane, stay, pltpu.roll(moved, 64, 1)))
        packed[0:32, lanes] = high
        packed[64:96, lanes] = low
        high, low = split(jnp.where(low_lane, pltpu.roll(stay, 64, 1), moved))
        packed[32:64, lanes] = high
        packed[96:128, lanes] = low
    load.wait()
    factors = [(ref, at) for ref in (factor_0, factor_1, factor_2) for at in range(ref.shape[0])]
    turned[:, 0:64, :] = jnp.zeros((TILE // 128, 64, 128), F32)
    stores = []
    for tile in range(blocks // TILE):
        wanted = as_bf16(iota((slots, TILE), 0) == slot_ref[:, TILE * tile : TILE * tile + TILE])
        flux = jnp.dot(packed[...], wanted, preferred_element_type=F32)
        flux = flux[0:64] + flux[64:128]
        for half in range(TILE // 128):
            for i in range(8):
                turned[half, pl.ds(64 + i, 8, stride=8), :] = flux[8 * i : 8 * i + 8, 128 * half : 128 * half + 128]
            ref, at = factors[tile * (TILE // 128) + half]
            turned[half, 64:128, :] = turned[half, 64:128, :] * ref[at]
            rows = slice(TILE * tile + 128 * half, TILE * tile + 128 * half + 128)
            slab[rows, :] = slab[rows, :] + turned[half].T
        rows = pl.ds(TILE * tile, TILE)
        store = pltpu.make_async_copy(slab.at[rows, :], new_ref.at[rows, top_lanes], stored.at[tile])
        store.start()
        stores.append(store)
    for store in stores:
        store.wait()


def finish(place, water_depth, *rest):
    shape = (144, 512)
    head = rest[-1]
    blocks = head.shape[0]
    return pl.pallas_call(
        functools.partial(sweep_kernel, place),
        in_specs=[VMEM] * 14 + [ANY],
        out_specs=[VMEM, ANY],
        out_shape=[
            jax.ShapeDtypeStruct(water_depth.shape, F32),
            jax.ShapeDtypeStruct(head.shape, F32),
        ],
        input_output_aliases={14: 1},
        scratch_shapes=[pltpu.VMEM(shape, F32)] * 4
        + [
            pltpu.VMEM((128, 128), F32),
            pltpu.VMEM((blocks, 128), F32),
            pltpu.VMEM((128, place[1] * 128), BF16),
            pltpu.VMEM((TILE // 128, 128, 128), F32),
            pltpu.SemaphoreType.DMA,
            pltpu.SemaphoreType.DMA((blocks // TILE,)),
        ],
        compiler_params=pltpu.CompilerParams(vmem_limit_bytes=VMEM_LIMIT),
        name="finish",
    )(water_depth, *rest)


def halo_pieces(soil_ref, classes, source, slot, table, turned):
    pieces = []

    def turn(half):
        lanes = slice(128 * half, 128 * half + 128)
        turned[half] = source(lanes).T
        soil = soil_rows(soil_ref, classes(lanes))
        for face in range(6):
            late.append(functools.partial(part, half, face, soil))

    def part(half, face, soil):
        head = face_rows(turned, half, face)
        write_face(head, curve(head, soil)[0], half, face, slot, table)

    late = []
    for half in range(TILE // 128):
        turn(half)
    return pieces, late


def inner_pieces(soil_ref, classes, levels, source, slot, table, turned, cond, base_sc, factor_sc, top_ref):
    open_i = iota((8, 8, 128), 1) < 7
    nothing = jnp.zeros((1, 8, 128), F32)
    pieces, late = [], []

    def one(half):
        lanes = slice(128 * half, 128 * half + 128)
        at = 2 * (slot - 1) + half
        turned[half] = source(lanes).T
        soil = soil_rows(soil_ref, classes(lanes))
        width = cell_width(levels(lanes))
        half_over = 0.5 / width
        scaled = SUB_STEP / width
        state = {"below": None}

        def conduct(k):
            rows = slice(64 * k, 64 * k + 64)
            conductivity, base, ratio = curve(turned[half, rows, :], soil)
            cond[half, rows, :] = conductivity
            factor = scaled * base / (soil[4] * ratio + STORAGE * base)
            factor_sc[at, rows, :] = factor
            if k == 7:
                top_ref[at] = factor

        def flow(k):
            rows = slice(64 * k, 64 * k + 64)
            head = turned[half, rows, :].reshape(8, 8, 128)
            cnd = cond[half, rows, :].reshape(8, 8, 128)
            flux = (cnd + pltpu.roll(cnd, 7, 1)) * (pltpu.roll(head, 7, 1) - head) * half_over
            flux = jnp.where(open_i, flux, 0.0)
            inflow = flux - pltpu.roll(flux, 1, 1)
            flux = (cnd[1:] + cnd[:-1]) * (head[1:] - head[:-1]) * half_over
            inflow = inflow + jnp.concatenate([flux, nothing], 0) - jnp.concatenate([nothing, flux], 0)
            if k < 7:
                above = slice(64 * k + 64, 64 * k + 128)
                head_up = turned[half, above, :].reshape(8, 8, 128)
                cnd_up = cond[half, above, :].reshape(8, 8, 128)
                flux = (cnd + cnd_up) * ((head_up - head) * half_over + 0.5)
                inflow = inflow + flux
            if state["below"] is not None:
                inflow = inflow - state["below"]
            state["below"] = flux
            base_sc[at, rows, :] = (
                turned[half, rows, :] + factor_sc[at, rows, :] * inflow.reshape(64, 128)
            )

        pieces.append(functools.partial(conduct, 0))
        for k in range(8):
            if k < 7:
                pieces.append(functools.partial(conduct, k + 1))
            pieces.append(functools.partial(flow, k))
        for face in range(6):
            late.append(
                lambda face=face: write_face(
                    face_rows(turned, half, face), face_rows(cond, half, face), half, face, slot, table
                )
            )

    for half in range(TILE // 128):
        one(half)
    return pieces, late


def face_pieces(first_row, levels, near, slot, table, total, factor, out):
    halves = TILE // 128
    first = halves * (slot - 1)
    width = cell_width(levels)
    window = slice((slot - 1) * TILE, (slot + 2) * TILE)
    own = slice(slot * TILE, (slot + 1) * TILE)

    def one(face):
        neighbor = near(face)
        far_width = cell_width(near(6 + face))
        over_gap = 2.0 / (width + far_width)
        half = jnp.where(neighbor >= 0, 0.5, 0.0)
        row = jnp.where(neighbor >= 0, neighbor - first_row, -1)
        chosen = jnp.where(
            iota((3 * TILE, TILE), 0).astype(I16) == row.astype(I16), jnp.ones((), BF16), jnp.zeros((), BF16)
        )
        there = 256 * OPPOSITE[face]
        far = jnp.dot(table[there : there + 256, window], chosen, preferred_element_type=F32)
        here = table[256 * face : 256 * face + 256, own].astype(F32)
        head_diff = (far[0:64] - here[0:64]) + (far[64:128] - here[64:128])
        conds = (far[128:192] + here[128:192]) + (far[192:256] + here[192:256])
        flux = conds * half * (head_diff * over_gap + GRAVITY[face])
        for part in range(halves):
            at = first + part
            added = flux[:, 128 * part : 128 * part + 128]
            if face < 2:
                rows = pl.ds(7 * face, 64, stride=8)
                total[at, rows, :] += factor[at, rows, :] * added
            elif face < 4:
                for k in range(8):
                    rows = slice(64 * k + 56 * (face - 2), 64 * k + 56 * (face - 2) + 8)
                    total[at, rows, :] += factor[at, rows, :] * added[8 * k : 8 * k + 8]
            else:
                rows = slice(448 * (face - 4), 448 * (face - 4) + 64)
                total[at, rows, :] += factor[at, rows, :] * added

    def write():
        out([total[first + part].T for part in range(halves)])

    return [functools.partial(one, face) for face in range(6)] + [write]


def run_mixed(faces, pieces, late):
    done = 0
    for number, face in enumerate(faces):
        face()
        upto = -(-len(pieces) * (number + 1) // len(faces))
        for piece in pieces[done:upto]:
            piece()
        done = upto
    for piece in pieces[done:] + late:
        piece()


def cells_kernel(low, inner, tiles, width, has_edge, chained, *refs):
    soil_ref, class_any, level_any, near_any, pressure_ref, after_ref = refs[:6]
    edge_ref = refs[6] if has_edge else None
    (
        out_ref, top_any, table, turned, cond, base_sc, factor_sc, inbox, outbox, edge,
        class_ref, level_ref, near_ref, top_ref, arrived, stored, small,
    ) = refs[6 + has_edge + chained :]
    own, _, _ = position(width)
    loads, stores = [], []
    for number, (source, kept) in enumerate(((class_any, class_ref), (level_any, level_ref), (near_any, near_ref))):
        smalls = pltpu.make_async_copy(source, kept, small.at[number])
        smalls.start()
        loads.append(smalls)
    small_loads, loads = loads, []
    for slot in range(inner + 2):
        tile = low + slot - 1
        if 0 <= tile < tiles:
            rows = pl.ds(tile * TILE, TILE)
            load = pltpu.make_async_copy(pressure_ref.at[rows, :], inbox.at[slot], arrived.at[slot])
        else:
            load = pltpu.make_async_copy(edge_ref, edge, arrived.at[slot])
        load.start()
        loads.append(load)
    for load in small_loads:
        load.wait()

    def tile_lanes(ref, slot):
        start = (low + slot - 1) * TILE
        return lambda lanes: ref[:, start + lanes.start : start + lanes.stop]

    def around(slot):
        loads[slot].wait()
        if 0 <= low + slot - 1 < tiles:
            return halo_pieces(
                soil_ref, tile_lanes(class_ref, slot), lambda lanes: inbox[slot, lanes, :], slot, table,
                turned.at[slot % 2],
            )
        return halo_pieces(
            soil_ref,
            lambda lanes: edge[HB : HB + 8, lanes][0:1, :].astype(I32),
            lambda lanes: edge[lanes, :],
            slot, table, turned.at[slot % 2],
        )

    def within(slot):
        loads[slot].wait()
        return inner_pieces(
            soil_ref, tile_lanes(class_ref, slot), tile_lanes(level_ref, slot),
            lambda lanes: inbox[slot, lanes, :],
            slot, table, turned.at[slot % 2], cond.at[slot % 2], base_sc, factor_sc, top_ref,
        )

    def faces(slot):
        first_row = own * tiles * TILE + (low + slot - 2) * TILE
        start = (low + slot - 1) * TILE

        def near(row):
            return near_ref[row : row + 1, start : start + TILE]

        def out(halves):
            for number, value in enumerate(halves):
                outbox[slot - 1, 128 * number : 128 * number + 128, :] = value
            store = pltpu.make_async_copy(
                outbox.at[slot - 1], out_ref.at[pl.ds(start, TILE), :], stored.at[slot - 1]
            )
            store.start()
            stores.append(store)

        return face_pieces(
            first_row, level_ref[:, start : start + TILE], near, slot, table, base_sc, factor_sc, out
        )

    for step in range(inner + 3):
        if step == inner + 2:
            store = pltpu.make_async_copy(top_ref, top_any, small.at[3])
            store.start()
            stores.append(store)
        work = [], []
        if step in (0, inner + 1):
            work = around(step)
        elif step <= inner:
            work = within(step)
        run_mixed(faces(step - 2) if step >= 3 else [], *work)
    for store in stores:
        store.wait()


def cells(shape, soil, kinds, near, pressure, edge, after, part, head):
    tiles = pressure.shape[0] // TILE
    low, inner = PARTS[part]
    extra = [value for value in (edge, head) if value is not None]
    aliases = {} if head is None else {5 + len(extra): 0}
    return pl.pallas_call(
        functools.partial(
            cells_kernel, low, inner, tiles, shape[1], int(edge is not None), int(head is not None)
        ),
        in_specs=[SMEM] + [ANY] * (5 + len(extra)),
        out_specs=[ANY, ANY],
        out_shape=[
            jax.ShapeDtypeStruct(pressure.shape, F32),
            jax.ShapeDtypeStruct((2 * inner, 64, 128), F32),
        ],
        input_output_aliases=aliases,
        scratch_shapes=[
            pltpu.VMEM((1536, (inner + 2) * TILE), BF16),
            pltpu.VMEM((2, TILE // 128, 512, 128), F32),
            pltpu.VMEM((2, TILE // 128, 512, 128), F32),
            pltpu.VMEM((2 * inner, 512, 128), F32),
            pltpu.VMEM((2 * inner, 512, 128), F32),
            pltpu.VMEM((inner + 2, TILE, 512), F32),
            pltpu.VMEM((inner, TILE, 512), F32),
            pltpu.VMEM((HB + 8, 512), F32),
            pltpu.VMEM(kinds[0].shape, I32),
            pltpu.VMEM(kinds[1].shape, I32),
            pltpu.VMEM(near.shape, I32),
            pltpu.VMEM((2 * inner, 64, 128), F32),
            pltpu.SemaphoreType.DMA((inner + 2,)),
            pltpu.SemaphoreType.DMA((inner,)),
            pltpu.SemaphoreType.DMA((4,)),
        ],
        compiler_params=pltpu.CompilerParams(vmem_limit_bytes=VMEM_LIMIT),
        cost_estimate=pl.CostEstimate(
            flops=inner * 6 * 2 * 256 * 256 * 768,
            bytes_accessed=inner * TILE * 512 * 16,
            transcendentals=inner * TILE * 512 * 8,
        ),
        name="cells",
    )(soil, *kinds, near, pressure, after, *extra)


def shifted(value, axis, steps, wrap=True):
    count = lax.axis_size(axis)
    pairs = [(i, (i + steps) % count) for i in range(count) if wrap or 0 <= i + steps < count]
    return lax.ppermute(value, axis, pairs)


def per_device(pressure, soil_class, levels, neighbors, neighbor_levels, patch_of_block, soil_params,
               water_depth, bed_height, roughness):
    blocks = pressure.shape[0]
    rows, cols = water_depth.shape
    patches = rows // 8 * (cols // 8)
    shape = (lax.axis_size("gx"), lax.axis_size("gy"))
    width = shape[1]
    gy = lax.axis_index("gy")
    kinds = [value.reshape(1, blocks) for value in (soil_class, levels)]
    patch = patch_of_block.reshape(1, blocks)
    near = jnp.concatenate([neighbors.T, neighbor_levels.T], axis=0)

    send, slot, edge_rows = route(
        shape, kinds + [patch], pressure, water_depth, bed_height, roughness
    )
    later, class_later, send = lax.optimization_barrier((pressure, soil_class, send))

    def edge(part):
        classes = jnp.pad(class_later[part].astype(F32)[None], ((0, 7), (0, 512 - HB)))
        return jnp.concatenate([later[part], classes], axis=0)

    low_edge = shifted(edge(slice(blocks - HB, blocks)), ("gx", "gy"), 1, wrap=False)
    high_edge = shifted(edge(slice(0, HB)), ("gx", "gy"), -1, wrap=False)
    got = lax.all_to_all(send, "gy", 0, 0)
    halos = got[:, 72:88]
    west = lax.dynamic_index_in_dim(halos, jnp.maximum(gy - 1, 0), 0, keepdims=False)
    east = lax.dynamic_index_in_dim(halos, jnp.minimum(gy + 1, width - 1), 0, keepdims=False)
    moving = got[:, 32:72].reshape(40 * width, 128)
    up = jnp.concatenate([moving, edge_rows[1], west, east], axis=0)
    down = jnp.concatenate([moving, edge_rows[0], west, east], axis=0)
    from_low = shifted(up, "gx", 1)
    from_high = shifted(down, "gx", -1)
    head, top_1 = cells(shape, soil_params, kinds, near, pressure, None, up, 1, None)
    stay, back_high, back_low, tile, edge_cols = surface(
        shape, soil_params, got, from_low, from_high, water_depth, patches, top_1
    )
    back_high = shifted(back_high, "gx", -1)
    back_low = shifted(back_low, "gx", 1)
    head, top_0 = cells(shape, soil_params, kinds, near, pressure, low_edge, stay, 0, head)
    back_low, back_high, top_0 = lax.optimization_barrier((back_low, back_high, top_0))
    number = jnp.arange(width, dtype=I32)[:, None, None]
    answers = 32 * width
    moved = jnp.where(
        number >= gy,
        back_high[:answers].reshape(width, 32, 128),
        back_low[:answers].reshape(width, 32, 128),
    )

    def side(kind):
        lines = slice(answers + 2 * kind, answers + 2 * kind + 2)
        return jnp.concatenate(
            [edge_cols[kind, 0:2], back_low[lines], back_high[lines], jnp.zeros((2, 128), F32)], axis=0
        )

    sides = jnp.where(number == gy + 1, side(1)[None], side(0)[None])
    reply = jnp.concatenate([stay, moved, sides], axis=1)
    returned = lax.all_to_all(reply, "gy", 0, 0)
    head, top_2 = cells(shape, soil_params, kinds, near, pressure, high_edge, reply, 2, head)
    new_depth, new_pressure = finish(
        shape, water_depth, bed_height, roughness, got, from_low, from_high, tile,
        back_low, back_high, returned, slot, top_0, top_1, top_2, head,
    )
    return new_pressure, new_depth


def solution(mesh):
    blocks = P(("gx", "gy"))
    wide = P(("gx", "gy"), None)
    tile = P("gx", "gy")
    return jax.shard_map(
        per_device,
        mesh=mesh,
        in_specs=(wide, blocks, blocks, wide, wide, blocks, P(), tile, tile, tile),
        out_specs=(wide, tile),
        check_vma=False,
    )
```

```python
import functools

import jax
import jax.numpy as jnp
from jax import lax
from jax.experimental import pallas as pl
from jax.experimental.pallas import tpu as pltpu
from jax.sharding import PartitionSpec as P

F32 = jnp.float32
BF16 = jnp.bfloat16
I32 = jnp.int32
I16 = jnp.int16

HB = 256
TILE = 256
PARTS = ((0, 3), (3, 2), (5, 3))
SLOTS = 64
GROUPS = 16
STORAGE = 0.05
SUB_STEP = 0.02
SURF_STEP = 0.003
SLOPE_FLOOR = 0.01
OPPOSITE = (1, 0, 3, 2, 5, 4)
GRAVITY = (0.0, 0.0, 0.0, 0.0, -1.0, 1.0)
VMEM_LIMIT = 60 * 1024 * 1024
VMEM_SHARE = 32 * 1024 * 1024

VMEM = pl.BlockSpec(memory_space=pltpu.VMEM)
SMEM = pl.BlockSpec(memory_space=pltpu.SMEM)
ANY = pl.BlockSpec(memory_space=pl.ANY)
HBM = pl.BlockSpec(memory_space=pltpu.HBM)


def position(width):
    gx, gy = lax.axis_index("gx"), lax.axis_index("gy")
    return gx * width + gy, gx, gy


def split(value):
    high = value.astype(BF16)
    low = (value - high.astype(F32)).astype(BF16)
    return high, low


def iota(shape, dim):
    return lax.broadcasted_iota(I32, shape, dim)


def as_bf16(mask):
    return jnp.where(mask, 1.0, 0.0).astype(BF16)


def cell_width(levels):
    return jnp.where(levels == 0, 0.25, jnp.where(levels == 1, 0.5, 1.0)).astype(F32)


def soil_rows(soil_ref, classes):
    rows = []
    for row in range(5):
        value = jnp.full(classes.shape, soil_ref[row, 0], F32)
        for cls in range(1, soil_ref.shape[1]):
            value = jnp.where(classes == cls, soil_ref[row, cls], value)
        rows.append(value)
    residual, saturated, alpha, power, cond = rows
    exponent = 1.0 - 1.0 / power
    return alpha, power - 1.0, -0.5 * exponent, cond, (saturated - residual) * alpha * (exponent * power)


def curve(pressure, soil):
    alpha, lesser, half, _, _ = soil
    suction = alpha * jnp.maximum(-pressure, 0.0)
    powered = jnp.exp2(lesser * jnp.log2(suction))
    base = 1.0 + powered * suction
    root = jnp.exp2(half * jnp.log2(base))
    ratio = powered * (root * root)
    rest = 1.0 - ratio
    conductivity = soil[3] * root * (rest * rest)
    return conductivity, base, ratio


def face_rows(ref, half, face):
    if face < 2:
        return ref[half, pl.ds(7 * face, 64, stride=8), :]
    if face < 4:
        start = 56 * (face - 2)
        return jnp.concatenate([ref[half, 64 * k + start : 64 * k + start + 8, :] for k in range(8)], axis=0)
    start = 448 * (face - 4)
    return ref[half, start : start + 64, :]


def write_face(head, conductivity, half, face, slot, table):
    lanes = slice(slot * TILE + 128 * half, slot * TILE + 128 * half + 128)
    for part, value in enumerate(split(head) + split(conductivity)):
        row = 256 * face + 64 * part
        table[row : row + 64, lanes] = value


def route_kernel(shape, class_ref, level_ref, patch_ref, top_ref, depth_ref, bed_ref, rough_ref,
                 send_ref, slot_ref, rows_ref, turned, packed, edges):
    own, _, gy = position(shape[1])
    route_once(own, gy, shape, class_ref, level_ref, patch_ref, top_ref, depth_ref, bed_ref, rough_ref,
               slot_ref, rows_ref, turned, packed, edges)
    blocks = patch_ref.shape[1]
    low_lane = iota((32, 128), 1) < 64
    for number in range(send_ref.shape[0]):
        wanted = as_bf16(iota((128, blocks), 0) == slot_ref[...] - 128 * number)
        out = lax.dot_general(packed[...], wanted, (((1,), (1,)), ((), ())), preferred_element_type=F32)
        first = out[0:32] + out[64:96]
        second = out[32:64] + out[96:128]
        send_ref[number, 0:32, :] = jnp.where(low_lane, first, pltpu.roll(second, 64, 1))
        send_ref[number, 32:64, :] = jnp.where(low_lane, pltpu.roll(first, 64, 1), second)
        label = out[130:131] * (out[128:129] + 256.0 * out[129:130] + 1.0) - 1.0
        row = iota((8, 128), 0)
        send_ref[number, 64:72, :] = jnp.where(row == 0, label, jnp.where(row == 1, out[131:132], out[132:133]))
        send_ref[number, 72:88, :] = jnp.where(number == gy + 1, edges[1], edges[0])


def route_once(own, gy, shape, class_ref, level_ref, patch_ref, top_ref, depth_ref, bed_ref, rough_ref,
               slot_ref, rows_ref, turned, packed, edges):
    devices, width = shape[0] * shape[1], shape[1]
    blocks = patch_ref.shape[1]
    patch = patch_ref[...]
    is_top = patch >= 0
    safe = jnp.where(is_top, patch, 0)
    offset = lax.rem(lax.shift_right_logical(safe, 9) - own + (GROUPS // 2 - 1) + devices, devices) - (GROUPS // 2 - 1)
    column = gy + offset
    moved = (column < 0) | (column >= width)
    group = 2 * lax.rem(column + width, width) + moved.astype(I32)
    upper = as_bf16(iota((TILE, TILE), 0) < iota((TILE, TILE), 1))
    carry = jnp.zeros((GROUPS, 1), F32)
    for part in range(blocks // TILE):
        lanes = slice(part * TILE, (part + 1) * TILE)
        member = jnp.where(
            (iota((GROUPS, TILE), 0) == group[:, lanes]) & is_top[:, lanes], 1.0, 0.0
        )
        before = jnp.dot(member.astype(BF16), upper, preferred_element_type=F32) + carry
        rank = jnp.sum(member * before, axis=0, keepdims=True)
        carry = carry + jnp.sum(member, axis=1, keepdims=True)
        slot_ref[:, lanes] = jnp.where(
            is_top[:, lanes], group[:, lanes] * SLOTS + rank.astype(I32), -1
        )
        for half in (2 * part, 2 * part + 1):
            turned[half] = top_ref[128 * half : 128 * half + 128, :].T
    for half in range(blocks // 128):
        lanes = slice(128 * half, 128 * half + 128)
        heads = jnp.concatenate(
            [turned[half, pl.ds(64 + i, 8, stride=8), :] for i in range(8)], axis=0
        )
        high, low = split(heads)
        packed[0:64, lanes] = high
        packed[64:128, lanes] = low
    place = jnp.bitwise_and(safe, 511)
    row = iota((16, blocks), 0)
    tags = jnp.where(row == 0, jnp.bitwise_and(place, 255), 0)
    tags = jnp.where(row == 1, lax.shift_right_logical(place, 8), tags)
    tags = jnp.where(row == 2, 1, tags)
    tags = jnp.where(row == 3, class_ref[...], tags)
    tags = jnp.where(row == 4, level_ref[...], tags)
    packed[128:144, :] = tags.astype(F32).astype(BF16)
    for number, field in enumerate((depth_ref, bed_ref, rough_ref)):
        edges[0, 3 * number : 3 * number + 3, :] = field[:, 0:128].T[0:3, :]
        edges[1, 3 * number : 3 * number + 3, :] = field[:, 128:256].T[125:128, :]
        for half in range(2):
            at = 3 * (2 * number + half)
            lanes = slice(128 * half, 128 * half + 128)
            rows_ref[0, at : at + 3, :] = field[0:3, lanes]
            rows_ref[1, at : at + 3, :] = field[125:128, lanes]


def route(shape, kinds, pressure, water_depth, bed_height, roughness):
    blocks = pressure.shape[0]
    width = shape[1]
    row = pl.BlockSpec((1, blocks), lambda t: (0, 0))
    return pl.pallas_call(
        functools.partial(route_kernel, shape),
        grid=(1,),
        in_specs=[
            row,
            row,
            row,
            pl.BlockSpec((blocks, 128), lambda t: (0, 3)),
            pl.BlockSpec(water_depth.shape, lambda t: (0, 0)),
            pl.BlockSpec(water_depth.shape, lambda t: (0, 0)),
            pl.BlockSpec(water_depth.shape, lambda t: (0, 0)),
        ],
        out_specs=[
            pl.BlockSpec((width, 88, 128), lambda t: (0, 0, 0)),
            pl.BlockSpec((1, blocks), lambda t: (0, 0)),
            pl.BlockSpec((2, 24, 128), lambda t: (0, 0, 0)),
        ],
        out_shape=[
            jax.ShapeDtypeStruct((width, 88, 128), F32),
            jax.ShapeDtypeStruct((1, blocks), I32),
            jax.ShapeDtypeStruct((2, 24, 128), F32),
        ],
        scratch_shapes=[
            pltpu.VMEM((blocks // 128, 128, 128), F32),
            pltpu.VMEM((144, blocks), BF16),
            pltpu.VMEM((2, 16, 128), F32),
        ],
        compiler_params=pltpu.CompilerParams(vmem_limit_bytes=VMEM_LIMIT),
        name="route",
    )(*kinds, pressure, water_depth, bed_height, roughness)


def surface_kernel(shape, soil_ref, got_ref, up_ref, down_ref, depth_ref, after_ref,
                   stay_ref, back_high_ref, back_low_ref, tile_ref, cols_ref, packed, labels, match):
    _, _, gy = position(shape[1])
    low_lane = iota((32, 128), 1) < 64
    tag_low = iota((8, 128), 1) < 64
    width = got_ref.shape[0]
    slots = width * 128
    patches = match.shape[0]
    for source in range(width):
        lanes = slice(128 * source, 128 * source + 128)
        at = 40 * source
        from_up = source >= gy
        stay = got_ref[source, 0:32, :]
        moved = jnp.where(from_up, up_ref[at : at + 32, :], down_ref[at : at + 32, :])
        high, low = split(jnp.where(low_lane, stay, pltpu.roll(moved, 64, 1)))
        packed[0:32, lanes] = high
        packed[64:96, lanes] = low
        high, low = split(jnp.where(low_lane, pltpu.roll(stay, 64, 1), moved))
        packed[32:64, lanes] = high
        packed[96:128, lanes] = low
        tags = jnp.where(
            tag_low,
            got_ref[source, 64:72, :],
            jnp.where(from_up, up_ref[at + 32 : at + 40, :], down_ref[at + 32 : at + 40, :]),
        )
        labels[:, lanes] = (tags[0:1, :] + 0.5).astype(I32) - jnp.where(tags[0:1, :] < 0, 1, 0)
        row = iota((16, 128), 0)
        packed[128:144, lanes] = jnp.where(row == 0, tags[1:2, :], tags[2:3, :]).astype(BF16)
    for part in range(patches // 128):
        match[128 * part : 128 * part + 128, :] = as_bf16(
            iota((128, slots), 0) + 128 * part == labels[...]
        )
    placed = lax.dot_general(
        packed[...], match[...], (((1,), (1,)), ((), ())), preferred_element_type=F32
    )
    classes = (placed[128:129] + 0.5).astype(I32)
    levels = (placed[129:130] + 0.5).astype(I32)
    soil = soil_rows(soil_ref, classes)
    half_cell = 0.5 * cell_width(levels)
    head = placed[0:64] + placed[64:128]
    conductivity, _, _ = curve(head, soil)
    row_of = lax.shift_right_logical(iota((128, patches), 0), 3)
    own_row = row_of == lax.shift_right_logical(iota((128, patches), 1), 5)
    depth_high, depth_low = split(depth_ref[...])
    depth_both = jnp.concatenate([depth_high, depth_low], axis=0)
    cols = depth_ref.shape[1]
    pieces = []
    for i in range(8):
        pick = as_bf16(iota((cols, patches), 0) == 8 * jnp.bitwise_and(iota((cols, patches), 1), 31) + i)
        spread = jnp.dot(depth_both, pick, preferred_element_type=F32)
        spread = jnp.where(own_row, spread[0:128] + spread[128:256], 0.0)
        pieces.append(jnp.sum(spread.reshape(16, 8, patches), axis=0))
    depth = jnp.concatenate(pieces, axis=0)
    infiltration = jnp.minimum(
        conductivity / half_cell * (depth - (head - half_cell)), depth / (3.0 * SURF_STEP)
    )
    high, low = split(infiltration)
    both = jnp.concatenate([high, low], axis=0)
    answer = jnp.dot(both, match[...], preferred_element_type=F32)
    answer = answer[0:64] + answer[64:128]
    for source in range(width):
        lanes = slice(128 * source, 128 * source + 128)
        first, second = answer[0:32, lanes], answer[32:64, lanes]
        stay_ref[source] = jnp.where(low_lane, first, pltpu.roll(second, 64, 1))
        moved = jnp.where(low_lane, pltpu.roll(first, 64, 1), second)
        back_high_ref[32 * source : 32 * source + 32, :] = moved
        back_low_ref[32 * source : 32 * source + 32, :] = moved
    total = jnp.zeros(depth_ref.shape, F32)
    for i in range(8):
        pick = as_bf16(iota((patches, cols), 1) == 8 * jnp.bitwise_and(iota((patches, cols), 0), 31) + i)
        rows = jnp.concatenate([infiltration[8 * i : 8 * i + 8]] * 16, axis=0)
        high, low = split(jnp.where(own_row, rows, 0.0))
        spread = jnp.dot(jnp.concatenate([high, low], axis=0), pick, preferred_element_type=F32)
        total = total + (spread[0:128] + spread[128:256])
    tile_ref[...] = total
    base = 32 * width
    for half in range(2):
        lanes = slice(128 * half, 128 * half + 128)
        back_high_ref[base + 2 * half : base + 2 * half + 2, :] = total[0:2, lanes]
        back_low_ref[base + 2 * half : base + 2 * half + 2, :] = total[126:128, lanes]
    cols_ref[0, 0:2, :] = total[:, 0:128].T[0:2, :]
    cols_ref[1, 0:2, :] = total[:, 128:256].T[126:128, :]


def surface(shape, soil, got, up, down, water_depth, patches, after):
    width = got.shape[0]
    return pl.pallas_call(
        functools.partial(surface_kernel, shape),
        in_specs=[SMEM, VMEM, VMEM, VMEM, VMEM, ANY],
        out_specs=[VMEM] * 5,
        out_shape=[
            jax.ShapeDtypeStruct((width, 32, 128), F32),
            jax.ShapeDtypeStruct((32 * width + 8, 128), F32),
            jax.ShapeDtypeStruct((32 * width + 8, 128), F32),
            jax.ShapeDtypeStruct(water_depth.shape, F32),
            jax.ShapeDtypeStruct((2, 8, 128), F32),
        ],
        scratch_shapes=[
            pltpu.VMEM((144, width * 128), BF16),
            pltpu.VMEM((1, width * 128), I32),
            pltpu.VMEM((patches, width * 128), BF16),
        ],
        compiler_params=pltpu.CompilerParams(vmem_limit_bytes=VMEM_SHARE),
        name="surface",
    )(soil, got, up, down, water_depth, after)


def sweep_kernel(place, depth_ref, bed_ref, rough_ref, got_ref, up_ref, down_ref,
                 source_ref, low_ref, high_ref, back_ref, slot_ref, factor_0, factor_1, factor_2, head_ref,
                 out_ref, new_ref, depth_ext, bed_ext, rough_ext, source_ext, turn, slab, packed, turned, loaded, stored):
    blocks = slab.shape[0]
    top_lanes = pl.ds(384, 128)
    load = pltpu.make_async_copy(head_ref.at[:, top_lanes], slab, loaded)
    load.start()
    _, gx, gy = position(place[1])
    left_at, right_at = jnp.maximum(gy - 1, 0), jnp.minimum(gy + 1, place[1] - 1)
    rows_total, cols_total = depth_ref.shape[0] * place[0], depth_ref.shape[1] * place[1]
    shape = depth_ext.shape
    halo = 40 * got_ref.shape[0]
    edge = 32 * got_ref.shape[0]
    depth_ext[...] = jnp.zeros(shape, F32)
    bed_ext[...] = jnp.zeros(shape, F32)
    rough_ext[...] = jnp.ones(shape, F32)
    source_ext[...] = jnp.zeros(shape, F32)
    for number, (ext, field) in enumerate(
        ((depth_ext, depth_ref), (bed_ext, bed_ref), (rough_ext, rough_ref))
    ):
        ext[8:136, 128:384] = field[...]
        for half in range(2):
            at = 3 * (2 * number + half)
            lanes = slice(128 + 128 * half, 256 + 128 * half)
            ext[5:8, lanes] = up_ref[halo + at : halo + at + 3, :]
            ext[136:139, lanes] = down_ref[halo + at : halo + at + 3, :]
        col = 3 * number
        fill = 1.0 if number == 2 else 0.0
        for side, lanes in ((0, slice(0, 128)), (1, slice(384, 512))):
            to = slice(125, 128) if side == 0 else slice(0, 3)
            beside = left_at if side == 0 else right_at
            away = halo + 24 + 16 * side + col
            turn[...] = jnp.full((128, 128), fill, F32)
            turn[to, :] = got_ref[beside, 72:88, :][col : col + 3, :]
            ext[8:136, lanes] = turn[...].T
            turn[to, :] = up_ref[away : away + 3, :]
            ext[0:8, lanes] = turn[...].T[120:128, :]
            turn[to, :] = down_ref[away : away + 3, :]
            ext[136:144, lanes] = turn[...].T[0:8, :]
    source_ext[8:136, 128:384] = source_ref[...]
    for half in range(2):
        lanes = slice(128 + 128 * half, 256 + 128 * half)
        source_ext[6:8, lanes] = low_ref[edge + 2 * half : edge + 2 * half + 2, :]
        source_ext[136:138, lanes] = high_ref[edge + 2 * half : edge + 2 * half + 2, :]
    for side, lanes in ((0, slice(0, 128)), (1, slice(384, 512))):
        to = slice(126, 128) if side == 0 else slice(0, 2)
        ends = back_ref[left_at if side == 0 else right_at, 64:72, :]
        turn[...] = jnp.zeros((128, 128), F32)
        turn[to, :] = ends[0:2, :]
        source_ext[8:136, lanes] = turn[...].T
        source_ext[6:8, lanes] = ends[2:4, :]
        source_ext[136:138, lanes] = ends[4:6, :]
    row_id = gx * depth_ref.shape[0] - 8 + iota(shape, 0)
    col_id = gy * depth_ref.shape[1] - 128 + iota(shape, 1)
    row_open = (row_id >= 0) & (row_id + 1 < rows_total)
    col_open = (col_id >= 0) & (col_id + 1 < cols_total)
    bed = bed_ext[...]
    rough = rough_ext[...]
    inverse = {
        0: jnp.where(row_open, 2.0 / (rough + pltpu.roll(rough, shape[0] - 1, 0)), 0.0),
        1: jnp.where(col_open, 2.0 / (rough + pltpu.roll(rough, shape[1] - 1, 1)), 0.0),
    }
    head = depth_ext[...]
    source = source_ext[...]
    for _ in range(3):
        wet = jnp.maximum(head, 0.0)
        section = head + bed
        net = jnp.zeros(shape, F32) - source
        for axis in range(2):
            back = shape[axis] - 1
            slope = pltpu.roll(section, back, axis) - section
            mean = 0.5 * (wet + pltpu.roll(wet, back, axis))
            flux = (
                jnp.exp2((5.0 / 3.0) * jnp.log2(mean))
                * inverse[axis]
                * slope
                * lax.rsqrt(jnp.abs(slope) + SLOPE_FLOOR)
            )
            net = net + flux - pltpu.roll(flux, 1, axis)
        head = head + SURF_STEP * net
    out_ref[...] = head[8:136, 128:384]
    low_lane = iota((32, 128), 1) < 64
    slots = packed.shape[1]
    for number in range(slots // 128):
        lanes = slice(128 * number, 128 * number + 128)
        stay, moved = back_ref[number, 0:32, :], back_ref[number, 32:64, :]
        high, low = split(jnp.where(low_lane, stay, pltpu.roll(moved, 64, 1)))
        packed[0:32, lanes] = high
        packed[64:96, lanes] = low
        high, low = split(jnp.where(low_lane, pltpu.roll(stay, 64, 1), moved))
        packed[32:64, lanes] = high
        packed[96:128, lanes] = low
    load.wait()
    factors = [(ref, at) for ref in (factor_0, factor_1, factor_2) for at in range(ref.shape[0])]
    turned[:, 0:64, :] = jnp.zeros((TILE // 128, 64, 128), F32)
    stores = []
    for tile in range(blocks // TILE):
        wanted = as_bf16(iota((slots, TILE), 0) == slot_ref[:, TILE * tile : TILE * tile + TILE])
        flux = jnp.dot(packed[...], wanted, preferred_element_type=F32)
        flux = flux[0:64] + flux[64:128]
        for half in range(TILE // 128):
            for i in range(8):
                turned[half, pl.ds(64 + i, 8, stride=8), :] = flux[8 * i : 8 * i + 8, 128 * half : 128 * half + 128]
            ref, at = factors[tile * (TILE // 128) + half]
            turned[half, 64:128, :] = turned[half, 64:128, :] * ref[at]
            rows = slice(TILE * tile + 128 * half, TILE * tile + 128 * half + 128)
            slab[rows, :] = slab[rows, :] + turned[half].T
        rows = pl.ds(TILE * tile, TILE)
        store = pltpu.make_async_copy(slab.at[rows, :], new_ref.at[rows, top_lanes], stored.at[tile])
        store.start()
        stores.append(store)
    for store in stores:
        store.wait()


def finish(place, water_depth, *rest):
    shape = (144, 512)
    head = rest[-1]
    blocks = head.shape[0]
    return pl.pallas_call(
        functools.partial(sweep_kernel, place),
        in_specs=[VMEM] * 14 + [HBM],
        out_specs=[VMEM, HBM],
        out_shape=[
            jax.ShapeDtypeStruct(water_depth.shape, F32),
            pltpu.HBM(head.shape, F32),
        ],
        input_output_aliases={14: 1},
        scratch_shapes=[pltpu.VMEM(shape, F32)] * 4
        + [
            pltpu.VMEM((128, 128), F32),
            pltpu.VMEM((blocks, 128), F32),
            pltpu.VMEM((128, place[1] * 128), BF16),
            pltpu.VMEM((TILE // 128, 128, 128), F32),
            pltpu.SemaphoreType.DMA,
            pltpu.SemaphoreType.DMA((blocks // TILE,)),
        ],
        compiler_params=pltpu.CompilerParams(vmem_limit_bytes=VMEM_SHARE),
        name="finish",
    )(water_depth, *rest)


def halo_pieces(soil_ref, classes, source, slot, table, turned):
    pieces = []

    def turn(half):
        lanes = slice(128 * half, 128 * half + 128)
        turned[half] = source(lanes).T
        soil = soil_rows(soil_ref, classes(lanes))
        for face in range(6):
            late.append(functools.partial(part, half, face, soil))

    def part(half, face, soil):
        head = face_rows(turned, half, face)
        write_face(head, curve(head, soil)[0], half, face, slot, table)

    late = []
    for half in range(TILE // 128):
        turn(half)
    return pieces, late


def inner_pieces(soil_ref, classes, levels, source, slot, table, turned, cond, base_sc, factor_sc, top_ref):
    open_i = iota((8, 8, 128), 1) < 7
    nothing = jnp.zeros((1, 8, 128), F32)
    pieces, late = [], []

    def one(half):
        lanes = slice(128 * half, 128 * half + 128)
        at = 2 * (slot - 1) + half
        turned[half] = source(lanes).T
        soil = soil_rows(soil_ref, classes(lanes))
        width = cell_width(levels(lanes))
        half_over = 0.5 / width
        scaled = SUB_STEP / width
        state = {"below": None}

        def conduct(k):
            rows = slice(64 * k, 64 * k + 64)
            conductivity, base, ratio = curve(turned[half, rows, :], soil)
            cond[half, rows, :] = conductivity
            factor = scaled * base / (soil[4] * ratio + STORAGE * base)
            factor_sc[at, rows, :] = factor
            if k == 7:
                top_ref[at] = factor

        def flow(k):
            rows = slice(64 * k, 64 * k + 64)
            head = turned[half, rows, :].reshape(8, 8, 128)
            cnd = cond[half, rows, :].reshape(8, 8, 128)
            flux = (cnd + pltpu.roll(cnd, 7, 1)) * (pltpu.roll(head, 7, 1) - head) * half_over
            flux = jnp.where(open_i, flux, 0.0)
            inflow = flux - pltpu.roll(flux, 1, 1)
            flux = (cnd[1:] + cnd[:-1]) * (head[1:] - head[:-1]) * half_over
            inflow = inflow + jnp.concatenate([flux, nothing], 0) - jnp.concatenate([nothing, flux], 0)
            if k < 7:
                above = slice(64 * k + 64, 64 * k + 128)
                head_up = turned[half, above, :].reshape(8, 8, 128)
                cnd_up = cond[half, above, :].reshape(8, 8, 128)
                flux = (cnd + cnd_up) * ((head_up - head) * half_over + 0.5)
                inflow = inflow + flux
            if state["below"] is not None:
                inflow = inflow - state["below"]
            state["below"] = flux
            base_sc[at, rows, :] = (
                turned[half, rows, :] + factor_sc[at, rows, :] * inflow.reshape(64, 128)
            )

        pieces.append(functools.partial(conduct, 0))
        for k in range(8):
            if k < 7:
                pieces.append(functools.partial(conduct, k + 1))
            pieces.append(functools.partial(flow, k))
        for face in range(6):
            late.append(
                lambda face=face: write_face(
                    face_rows(turned, half, face), face_rows(cond, half, face), half, face, slot, table
                )
            )

    for half in range(TILE // 128):
        one(half)
    return pieces, late


def face_pieces(first_row, levels, near, slot, table, total, factor, out):
    halves = TILE // 128
    first = halves * (slot - 1)
    width = cell_width(levels)
    window = slice((slot - 1) * TILE, (slot + 2) * TILE)
    own = slice(slot * TILE, (slot + 1) * TILE)

    def one(face):
        neighbor = near(face)
        far_width = cell_width(near(6 + face))
        over_gap = 2.0 / (width + far_width)
        half = jnp.where(neighbor >= 0, 0.5, 0.0)
        row = jnp.where(neighbor >= 0, neighbor - first_row, -1)
        chosen = jnp.where(
            iota((3 * TILE, TILE), 0).astype(I16) == row.astype(I16), jnp.ones((), BF16), jnp.zeros((), BF16)
        )
        there = 256 * OPPOSITE[face]
        far = jnp.dot(table[there : there + 256, window], chosen, preferred_element_type=F32)
        here = table[256 * face : 256 * face + 256, own].astype(F32)
        head_diff = (far[0:64] - here[0:64]) + (far[64:128] - here[64:128])
        conds = (far[128:192] + here[128:192]) + (far[192:256] + here[192:256])
        flux = conds * half * (head_diff * over_gap + GRAVITY[face])
        for part in range(halves):
            at = first + part
            added = flux[:, 128 * part : 128 * part + 128]
            if face < 2:
                rows = pl.ds(7 * face, 64, stride=8)
                total[at, rows, :] += factor[at, rows, :] * added
            elif face < 4:
                for k in range(8):
                    rows = slice(64 * k + 56 * (face - 2), 64 * k + 56 * (face - 2) + 8)
                    total[at, rows, :] += factor[at, rows, :] * added[8 * k : 8 * k + 8]
            else:
                rows = slice(448 * (face - 4), 448 * (face - 4) + 64)
                total[at, rows, :] += factor[at, rows, :] * added

    def write():
        out([total[first + part].T for part in range(halves)])

    return [functools.partial(one, face) for face in range(6)] + [write]


def run_mixed(faces, pieces, late):
    done = 0
    for number, face in enumerate(faces):
        face()
        upto = -(-len(pieces) * (number + 1) // len(faces))
        for piece in pieces[done:upto]:
            piece()
        done = upto
    for piece in pieces[done:] + late:
        piece()


def cells_kernel(low, inner, tiles, width, has_edge, chained, *refs):
    soil_ref, class_any, level_any, near_any, pressure_ref, after_ref = refs[:6]
    edge_ref = refs[6] if has_edge else None
    (
        out_ref, top_any, table, turned, cond, base_sc, factor_sc, inbox, outbox, edge,
        class_ref, level_ref, near_ref, top_ref, arrived, stored, small,
    ) = refs[6 + has_edge + chained :]
    own, _, _ = position(width)
    loads, stores = [], []
    for number, (source, kept) in enumerate(((class_any, class_ref), (level_any, level_ref), (near_any, near_ref))):
        smalls = pltpu.make_async_copy(source, kept, small.at[number])
        smalls.start()
        loads.append(smalls)
    small_loads, loads = loads, []
    for slot in range(inner + 2):
        tile = low + slot - 1
        if 0 <= tile < tiles:
            rows = pl.ds(tile * TILE, TILE)
            load = pltpu.make_async_copy(pressure_ref.at[rows, :], inbox.at[slot], arrived.at[slot])
        else:
            load = pltpu.make_async_copy(edge_ref, edge, arrived.at[slot])
        load.start()
        loads.append(load)
    for load in small_loads:
        load.wait()

    def tile_lanes(ref, slot):
        start = (low + slot - 1) * TILE
        return lambda lanes: ref[:, start + lanes.start : start + lanes.stop]

    def around(slot):
        loads[slot].wait()
        if 0 <= low + slot - 1 < tiles:
            return halo_pieces(
                soil_ref, tile_lanes(class_ref, slot), lambda lanes: inbox[slot, lanes, :], slot, table,
                turned.at[slot % 2],
            )
        return halo_pieces(
            soil_ref,
            lambda lanes: edge[HB : HB + 8, lanes][0:1, :].astype(I32),
            lambda lanes: edge[lanes, :],
            slot, table, turned.at[slot % 2],
        )

    def within(slot):
        loads[slot].wait()
        return inner_pieces(
            soil_ref, tile_lanes(class_ref, slot), tile_lanes(level_ref, slot),
            lambda lanes: inbox[slot, lanes, :],
            slot, table, turned.at[slot % 2], cond.at[slot % 2], base_sc, factor_sc, top_ref,
        )

    def faces(slot):
        first_row = own * tiles * TILE + (low + slot - 2) * TILE
        start = (low + slot - 1) * TILE

        def near(row):
            return near_ref[row : row + 1, start : start + TILE]

        def out(halves):
            for number, value in enumerate(halves):
                outbox[slot - 1, 128 * number : 128 * number + 128, :] = value
            store = pltpu.make_async_copy(
                outbox.at[slot - 1], out_ref.at[pl.ds(start, TILE), :], stored.at[slot - 1]
            )
            store.start()
            stores.append(store)

        return face_pieces(
            first_row, level_ref[:, start : start + TILE], near, slot, table, base_sc, factor_sc, out
        )

    for step in range(inner + 3):
        if step == inner + 2:
            store = pltpu.make_async_copy(top_ref, top_any, small.at[3])
            store.start()
            stores.append(store)
        work = [], []
        if step in (0, inner + 1):
            work = around(step)
        elif step <= inner:
            work = within(step)
        run_mixed(faces(step - 2) if step >= 3 else [], *work)
    for store in stores:
        store.wait()


def cells(shape, soil, kinds, near, pressure, edge, after, part, head):
    tiles = pressure.shape[0] // TILE
    low, inner = PARTS[part]
    extra = [value for value in (edge, head) if value is not None]
    aliases = {} if head is None else {5 + len(extra): 0}
    return pl.pallas_call(
        functools.partial(
            cells_kernel, low, inner, tiles, shape[1], int(edge is not None), int(head is not None)
        ),
        in_specs=[SMEM, ANY, ANY, ANY, HBM, ANY] + [ANY] * (edge is not None) + [HBM] * (head is not None),
        out_specs=[HBM, ANY],
        out_shape=[
            pltpu.HBM(pressure.shape, F32),
            jax.ShapeDtypeStruct((2 * inner, 64, 128), F32),
        ],
        input_output_aliases=aliases,
        scratch_shapes=[
            pltpu.VMEM((1536, (inner + 2) * TILE), BF16),
            pltpu.VMEM((2, TILE // 128, 512, 128), F32),
            pltpu.VMEM((2, TILE // 128, 512, 128), F32),
            pltpu.VMEM((2 * inner, 512, 128), F32),
            pltpu.VMEM((2 * inner, 512, 128), F32),
            pltpu.VMEM((inner + 2, TILE, 512), F32),
            pltpu.VMEM((inner, TILE, 512), F32),
            pltpu.VMEM((HB + 8, 512), F32),
            pltpu.VMEM(kinds[0].shape, I32),
            pltpu.VMEM(kinds[1].shape, I32),
            pltpu.VMEM(near.shape, I32),
            pltpu.VMEM((2 * inner, 64, 128), F32),
            pltpu.SemaphoreType.DMA((inner + 2,)),
            pltpu.SemaphoreType.DMA((inner,)),
            pltpu.SemaphoreType.DMA((4,)),
        ],
        compiler_params=pltpu.CompilerParams(vmem_limit_bytes=VMEM_SHARE),
        cost_estimate=pl.CostEstimate(
            flops=inner * 6 * 2 * 256 * 256 * 768,
            bytes_accessed=inner * TILE * 512 * 16,
            transcendentals=inner * TILE * 512 * 8,
        ),
        name="cells",
    )(soil, *kinds, near, pressure, after, *extra)


def shifted(value, axis, steps, wrap=True):
    count = lax.axis_size(axis)
    pairs = [(i, (i + steps) % count) for i in range(count) if wrap or 0 <= i + steps < count]
    return lax.ppermute(value, axis, pairs)


def per_device(pressure, soil_class, levels, neighbors, neighbor_levels, patch_of_block, soil_params,
               water_depth, bed_height, roughness):
    blocks = pressure.shape[0]
    rows, cols = water_depth.shape
    patches = rows // 8 * (cols // 8)
    shape = (lax.axis_size("gx"), lax.axis_size("gy"))
    width = shape[1]
    gy = lax.axis_index("gy")
    kinds = [value.reshape(1, blocks) for value in (soil_class, levels)]
    patch = patch_of_block.reshape(1, blocks)
    near = jnp.concatenate([neighbors.T, neighbor_levels.T], axis=0)

    send, slot, edge_rows = route(
        shape, kinds + [patch], pressure, water_depth, bed_height, roughness
    )
    later, class_later, send = lax.optimization_barrier((pressure, soil_class, send))

    def edge(part):
        classes = jnp.pad(class_later[part].astype(F32)[None], ((0, 7), (0, 512 - HB)))
        return jnp.concatenate([later[part], classes], axis=0)

    low_edge = shifted(edge(slice(blocks - HB, blocks)), ("gx", "gy"), 1, wrap=False)
    high_edge = shifted(edge(slice(0, HB)), ("gx", "gy"), -1, wrap=False)
    got = lax.all_to_all(send, "gy", 0, 0)
    halos = got[:, 72:88]
    west = lax.dynamic_index_in_dim(halos, jnp.maximum(gy - 1, 0), 0, keepdims=False)
    east = lax.dynamic_index_in_dim(halos, jnp.minimum(gy + 1, width - 1), 0, keepdims=False)
    moving = got[:, 32:72].reshape(40 * width, 128)
    up = jnp.concatenate([moving, edge_rows[1], west, east], axis=0)
    down = jnp.concatenate([moving, edge_rows[0], west, east], axis=0)
    from_low = shifted(up, "gx", 1)
    from_high = shifted(down, "gx", -1)
    head, top_1 = cells(shape, soil_params, kinds, near, pressure, None, up, 1, None)
    stay, back_high, back_low, tile, edge_cols = surface(
        shape, soil_params, got, from_low, from_high, water_depth, patches, top_1
    )
    back_high = shifted(back_high, "gx", -1)
    back_low = shifted(back_low, "gx", 1)
    head, top_0 = cells(shape, soil_params, kinds, near, pressure, low_edge, stay, 0, head)
    back_low, back_high, top_0 = lax.optimization_barrier((back_low, back_high, top_0))
    number = jnp.arange(width, dtype=I32)[:, None, None]
    answers = 32 * width
    moved = jnp.where(
        number >= gy,
        back_high[:answers].reshape(width, 32, 128),
        back_low[:answers].reshape(width, 32, 128),
    )

    def side(kind):
        lines = slice(answers + 2 * kind, answers + 2 * kind + 2)
        return jnp.concatenate(
            [edge_cols[kind, 0:2], back_low[lines], back_high[lines], jnp.zeros((2, 128), F32)], axis=0
        )

    sides = jnp.where(number == gy + 1, side(1)[None], side(0)[None])
    reply = jnp.concatenate([stay, moved, sides], axis=1)
    returned = lax.all_to_all(reply, "gy", 0, 0)
    head, top_2 = cells(shape, soil_params, kinds, near, pressure, high_edge, reply, 2, head)
    new_depth, new_pressure = finish(
        shape, water_depth, bed_height, roughness, got, from_low, from_high, tile,
        back_low, back_high, returned, slot, top_0, top_1, top_2, head,
    )
    return new_pressure, new_depth


def solution(mesh):
    blocks = P(("gx", "gy"))
    wide = P(("gx", "gy"), None)
    tile = P("gx", "gy")
    return jax.shard_map(
        per_device,
        mesh=mesh,
        in_specs=(wide, blocks, blocks, wide, wide, blocks, P(), tile, tile, tile),
        out_specs=(wide, tile),
        check_vma=False,
    )
```

```python
import functools

import jax
import jax.numpy as jnp
from jax import lax
from jax.experimental import pallas as pl
from jax.experimental.pallas import tpu as pltpu
from jax.sharding import PartitionSpec as P

F32 = jnp.float32
BF16 = jnp.bfloat16
I32 = jnp.int32
I16 = jnp.int16

HB = 256
TILE = 256
PARTS = ((0, 3), (3, 2), (5, 3))
SLOTS = 64
GROUPS = 16
STORAGE = 0.05
SUB_STEP = 0.02
SURF_STEP = 0.003
SLOPE_FLOOR = 0.01
OPPOSITE = (1, 0, 3, 2, 5, 4)
GRAVITY = (0.0, 0.0, 0.0, 0.0, -1.0, 1.0)
VMEM_LIMIT = 60 * 1024 * 1024
VMEM_SHARE = 32 * 1024 * 1024

VMEM = pl.BlockSpec(memory_space=pltpu.VMEM)
SMEM = pl.BlockSpec(memory_space=pltpu.SMEM)
ANY = pl.BlockSpec(memory_space=pl.ANY)
HBM = pl.BlockSpec(memory_space=pltpu.HBM)


def position(width):
    gx, gy = lax.axis_index("gx"), lax.axis_index("gy")
    return gx * width + gy, gx, gy


def split(value):
    high = value.astype(BF16)
    low = (value - high.astype(F32)).astype(BF16)
    return high, low


def iota(shape, dim):
    return lax.broadcasted_iota(I32, shape, dim)


def as_bf16(mask):
    return jnp.where(mask, 1.0, 0.0).astype(BF16)


def cell_width(levels):
    return jnp.where(levels == 0, 0.25, jnp.where(levels == 1, 0.5, 1.0)).astype(F32)


def soil_rows(soil_ref, classes):
    rows = []
    for row in range(5):
        value = jnp.full(classes.shape, soil_ref[row, 0], F32)
        for cls in range(1, soil_ref.shape[1]):
            value = jnp.where(classes == cls, soil_ref[row, cls], value)
        rows.append(value)
    residual, saturated, alpha, power, cond = rows
    exponent = 1.0 - 1.0 / power
    return alpha, power - 1.0, -0.5 * exponent, cond, (saturated - residual) * alpha * (exponent * power)


def curve(pressure, soil):
    alpha, lesser, half, _, _ = soil
    suction = alpha * jnp.maximum(-pressure, 0.0)
    powered = jnp.exp2(lesser * jnp.log2(suction))
    base = 1.0 + powered * suction
    root = jnp.exp2(half * jnp.log2(base))
    ratio = powered * (root * root)
    rest = 1.0 - ratio
    conductivity = soil[3] * root * (rest * rest)
    return conductivity, base, ratio


def face_rows(ref, half, face):
    if face < 2:
        return ref[half, pl.ds(7 * face, 64, stride=8), :]
    if face < 4:
        start = 56 * (face - 2)
        return jnp.concatenate([ref[half, 64 * k + start : 64 * k + start + 8, :] for k in range(8)], axis=0)
    start = 448 * (face - 4)
    return ref[half, start : start + 64, :]


def write_face(head, conductivity, half, face, slot, table):
    lanes = slice(slot * TILE + 128 * half, slot * TILE + 128 * half + 128)
    for part, value in enumerate(split(head) + split(conductivity)):
        row = 256 * face + 64 * part
        table[row : row + 64, lanes] = value


def route_kernel(shape, class_ref, level_ref, patch_ref, top_ref, depth_ref, bed_ref, rough_ref,
                 send_ref, slot_ref, rows_ref, turned, packed, edges):
    own, _, gy = position(shape[1])
    route_once(own, gy, shape, class_ref, level_ref, patch_ref, top_ref, depth_ref, bed_ref, rough_ref,
               slot_ref, rows_ref, turned, packed, edges)
    blocks = patch_ref.shape[1]
    low_lane = iota((32, 128), 1) < 64
    for number in range(send_ref.shape[0]):
        wanted = as_bf16(iota((128, blocks), 0) == slot_ref[...] - 128 * number)
        out = lax.dot_general(packed[...], wanted, (((1,), (1,)), ((), ())), preferred_element_type=F32)
        first = out[0:32] + out[64:96]
        second = out[32:64] + out[96:128]
        send_ref[number, 0:32, :] = jnp.where(low_lane, first, pltpu.roll(second, 64, 1))
        send_ref[number, 32:64, :] = jnp.where(low_lane, pltpu.roll(first, 64, 1), second)
        label = out[130:131] * (out[128:129] + 256.0 * out[129:130] + 1.0) - 1.0
        row = iota((8, 128), 0)
        send_ref[number, 64:72, :] = jnp.where(row == 0, label, jnp.where(row == 1, out[131:132], out[132:133]))
        send_ref[number, 72:88, :] = jnp.where(number == gy + 1, edges[1], edges[0])


def route_once(own, gy, shape, class_ref, level_ref, patch_ref, top_ref, depth_ref, bed_ref, rough_ref,
               slot_ref, rows_ref, turned, packed, edges):
    devices, width = shape[0] * shape[1], shape[1]
    blocks = patch_ref.shape[1]
    patch = patch_ref[...]
    is_top = patch >= 0
    safe = jnp.where(is_top, patch, 0)
    offset = lax.rem(lax.shift_right_logical(safe, 9) - own + (GROUPS // 2 - 1) + devices, devices) - (GROUPS // 2 - 1)
    column = gy + offset
    moved = (column < 0) | (column >= width)
    group = 2 * lax.rem(column + width, width) + moved.astype(I32)
    upper = as_bf16(iota((TILE, TILE), 0) < iota((TILE, TILE), 1))
    carry = jnp.zeros((GROUPS, 1), F32)
    for part in range(blocks // TILE):
        lanes = slice(part * TILE, (part + 1) * TILE)
        member = jnp.where(
            (iota((GROUPS, TILE), 0) == group[:, lanes]) & is_top[:, lanes], 1.0, 0.0
        )
        before = jnp.dot(member.astype(BF16), upper, preferred_element_type=F32) + carry
        rank = jnp.sum(member * before, axis=0, keepdims=True)
        carry = carry + jnp.sum(member, axis=1, keepdims=True)
        slot_ref[:, lanes] = jnp.where(
            is_top[:, lanes], group[:, lanes] * SLOTS + rank.astype(I32), -1
        )
        for half in (2 * part, 2 * part + 1):
            turned[half] = top_ref[128 * half : 128 * half + 128, :].T
    for half in range(blocks // 128):
        lanes = slice(128 * half, 128 * half + 128)
        heads = jnp.concatenate(
            [turned[half, pl.ds(64 + i, 8, stride=8), :] for i in range(8)], axis=0
        )
        high, low = split(heads)
        packed[0:64, lanes] = high
        packed[64:128, lanes] = low
    place = jnp.bitwise_and(safe, 511)
    row = iota((16, blocks), 0)
    tags = jnp.where(row == 0, jnp.bitwise_and(place, 255), 0)
    tags = jnp.where(row == 1, lax.shift_right_logical(place, 8), tags)
    tags = jnp.where(row == 2, 1, tags)
    tags = jnp.where(row == 3, class_ref[...], tags)
    tags = jnp.where(row == 4, level_ref[...], tags)
    packed[128:144, :] = tags.astype(F32).astype(BF16)
    for number, field in enumerate((depth_ref, bed_ref, rough_ref)):
        edges[0, 3 * number : 3 * number + 3, :] = field[:, 0:128].T[0:3, :]
        edges[1, 3 * number : 3 * number + 3, :] = field[:, 128:256].T[125:128, :]
        for half in range(2):
            at = 3 * (2 * number + half)
            lanes = slice(128 * half, 128 * half + 128)
            rows_ref[0, at : at + 3, :] = field[0:3, lanes]
            rows_ref[1, at : at + 3, :] = field[125:128, lanes]


def route(shape, kinds, pressure, water_depth, bed_height, roughness):
    blocks = pressure.shape[0]
    width = shape[1]
    row = pl.BlockSpec((1, blocks), lambda t: (0, 0))
    return pl.pallas_call(
        functools.partial(route_kernel, shape),
        grid=(1,),
        in_specs=[
            row,
            row,
            row,
            pl.BlockSpec((blocks, 128), lambda t: (0, 3)),
            pl.BlockSpec(water_depth.shape, lambda t: (0, 0)),
            pl.BlockSpec(water_depth.shape, lambda t: (0, 0)),
            pl.BlockSpec(water_depth.shape, lambda t: (0, 0)),
        ],
        out_specs=[
            pl.BlockSpec((width, 88, 128), lambda t: (0, 0, 0)),
            pl.BlockSpec((1, blocks), lambda t: (0, 0)),
            pl.BlockSpec((2, 24, 128), lambda t: (0, 0, 0)),
        ],
        out_shape=[
            jax.ShapeDtypeStruct((width, 88, 128), F32),
            jax.ShapeDtypeStruct((1, blocks), I32),
            jax.ShapeDtypeStruct((2, 24, 128), F32),
        ],
        scratch_shapes=[
            pltpu.VMEM((blocks // 128, 128, 128), F32),
            pltpu.VMEM((144, blocks), BF16),
            pltpu.VMEM((2, 16, 128), F32),
        ],
        compiler_params=pltpu.CompilerParams(vmem_limit_bytes=VMEM_LIMIT),
        name="route",
    )(*kinds, pressure, water_depth, bed_height, roughness)


def surface_kernel(shape, soil_ref, got_ref, up_ref, down_ref, depth_ref, after_ref,
                   stay_ref, back_high_ref, back_low_ref, tile_ref, cols_ref, packed, labels, match):
    _, _, gy = position(shape[1])
    low_lane = iota((32, 128), 1) < 64
    tag_low = iota((8, 128), 1) < 64
    width = got_ref.shape[0]
    slots = width * 128
    patches = match.shape[0]
    for source in range(width):
        lanes = slice(128 * source, 128 * source + 128)
        at = 40 * source
        from_up = source >= gy
        stay = got_ref[source, 0:32, :]
        moved = jnp.where(from_up, up_ref[at : at + 32, :], down_ref[at : at + 32, :])
        high, low = split(jnp.where(low_lane, stay, pltpu.roll(moved, 64, 1)))
        packed[0:32, lanes] = high
        packed[64:96, lanes] = low
        high, low = split(jnp.where(low_lane, pltpu.roll(stay, 64, 1), moved))
        packed[32:64, lanes] = high
        packed[96:128, lanes] = low
        tags = jnp.where(
            tag_low,
            got_ref[source, 64:72, :],
            jnp.where(from_up, up_ref[at + 32 : at + 40, :], down_ref[at + 32 : at + 40, :]),
        )
        labels[:, lanes] = (tags[0:1, :] + 0.5).astype(I32) - jnp.where(tags[0:1, :] < 0, 1, 0)
        row = iota((16, 128), 0)
        packed[128:144, lanes] = jnp.where(row == 0, tags[1:2, :], tags[2:3, :]).astype(BF16)
    for part in range(patches // 128):
        match[128 * part : 128 * part + 128, :] = as_bf16(
            iota((128, slots), 0) + 128 * part == labels[...]
        )
    placed = lax.dot_general(
        packed[...], match[...], (((1,), (1,)), ((), ())), preferred_element_type=F32
    )
    classes = (placed[128:129] + 0.5).astype(I32)
    levels = (placed[129:130] + 0.5).astype(I32)
    soil = soil_rows(soil_ref, classes)
    half_cell = 0.5 * cell_width(levels)
    head = placed[0:64] + placed[64:128]
    conductivity, _, _ = curve(head, soil)
    row_of = lax.shift_right_logical(iota((128, patches), 0), 3)
    own_row = row_of == lax.shift_right_logical(iota((128, patches), 1), 5)
    depth_high, depth_low = split(depth_ref[...])
    depth_both = jnp.concatenate([depth_high, depth_low], axis=0)
    cols = depth_ref.shape[1]
    pieces = []
    for i in range(8):
        pick = as_bf16(iota((cols, patches), 0) == 8 * jnp.bitwise_and(iota((cols, patches), 1), 31) + i)
        spread = jnp.dot(depth_both, pick, preferred_element_type=F32)
        spread = jnp.where(own_row, spread[0:128] + spread[128:256], 0.0)
        pieces.append(jnp.sum(spread.reshape(16, 8, patches), axis=0))
    depth = jnp.concatenate(pieces, axis=0)
    infiltration = jnp.minimum(
        conductivity / half_cell * (depth - (head - half_cell)), depth / (3.0 * SURF_STEP)
    )
    high, low = split(infiltration)
    both = jnp.concatenate([high, low], axis=0)
    answer = jnp.dot(both, match[...], preferred_element_type=F32)
    answer = answer[0:64] + answer[64:128]
    for source in range(width):
        lanes = slice(128 * source, 128 * source + 128)
        first, second = answer[0:32, lanes], answer[32:64, lanes]
        stay_ref[source] = jnp.where(low_lane, first, pltpu.roll(second, 64, 1))
        moved = jnp.where(low_lane, pltpu.roll(first, 64, 1), second)
        back_high_ref[32 * source : 32 * source + 32, :] = moved
        back_low_ref[32 * source : 32 * source + 32, :] = moved
    total = jnp.zeros(depth_ref.shape, F32)
    for i in range(8):
        pick = as_bf16(iota((patches, cols), 1) == 8 * jnp.bitwise_and(iota((patches, cols), 0), 31) + i)
        rows = jnp.concatenate([infiltration[8 * i : 8 * i + 8]] * 16, axis=0)
        high, low = split(jnp.where(own_row, rows, 0.0))
        spread = jnp.dot(jnp.concatenate([high, low], axis=0), pick, preferred_element_type=F32)
        total = total + (spread[0:128] + spread[128:256])
    tile_ref[...] = total
    base = 32 * width
    for half in range(2):
        lanes = slice(128 * half, 128 * half + 128)
        back_high_ref[base + 2 * half : base + 2 * half + 2, :] = total[0:2, lanes]
        back_low_ref[base + 2 * half : base + 2 * half + 2, :] = total[126:128, lanes]
    cols_ref[0, 0:2, :] = total[:, 0:128].T[0:2, :]
    cols_ref[1, 0:2, :] = total[:, 128:256].T[126:128, :]


def surface(shape, soil, got, up, down, water_depth, patches, after):
    width = got.shape[0]
    return pl.pallas_call(
        functools.partial(surface_kernel, shape),
        in_specs=[SMEM, VMEM, VMEM, VMEM, VMEM, ANY],
        out_specs=[VMEM] * 5,
        out_shape=[
            jax.ShapeDtypeStruct((width, 32, 128), F32),
            jax.ShapeDtypeStruct((32 * width + 8, 128), F32),
            jax.ShapeDtypeStruct((32 * width + 8, 128), F32),
            jax.ShapeDtypeStruct(water_depth.shape, F32),
            jax.ShapeDtypeStruct((2, 8, 128), F32),
        ],
        scratch_shapes=[
            pltpu.VMEM((144, width * 128), BF16),
            pltpu.VMEM((1, width * 128), I32),
            pltpu.VMEM((patches, width * 128), BF16),
        ],
        compiler_params=pltpu.CompilerParams(vmem_limit_bytes=VMEM_SHARE),
        name="surface",
    )(soil, got, up, down, water_depth, after)


def sweep_kernel(place, depth_ref, bed_ref, rough_ref, got_ref, up_ref, down_ref,
                 source_ref, low_ref, high_ref, back_ref, slot_ref, factor_0, factor_1, factor_2, head_ref,
                 out_ref, new_ref, depth_ext, bed_ext, rough_ext, source_ext, turn, slab, packed, turned, loaded, stored):
    blocks = slab.shape[0]
    top_lanes = pl.ds(384, 128)
    load = pltpu.make_async_copy(head_ref.at[:, top_lanes], slab, loaded)
    load.start()
    _, gx, gy = position(place[1])
    left_at, right_at = jnp.maximum(gy - 1, 0), jnp.minimum(gy + 1, place[1] - 1)
    rows_total, cols_total = depth_ref.shape[0] * place[0], depth_ref.shape[1] * place[1]
    shape = depth_ext.shape
    halo = 40 * got_ref.shape[0]
    edge = 32 * got_ref.shape[0]
    depth_ext[...] = jnp.zeros(shape, F32)
    bed_ext[...] = jnp.zeros(shape, F32)
    rough_ext[...] = jnp.ones(shape, F32)
    source_ext[...] = jnp.zeros(shape, F32)
    for number, (ext, field) in enumerate(
        ((depth_ext, depth_ref), (bed_ext, bed_ref), (rough_ext, rough_ref))
    ):
        ext[8:136, 128:384] = field[...]
        for half in range(2):
            at = 3 * (2 * number + half)
            lanes = slice(128 + 128 * half, 256 + 128 * half)
            ext[5:8, lanes] = up_ref[halo + at : halo + at + 3, :]
            ext[136:139, lanes] = down_ref[halo + at : halo + at + 3, :]
        col = 3 * number
        fill = 1.0 if number == 2 else 0.0
        for side, lanes in ((0, slice(0, 128)), (1, slice(384, 512))):
            to = slice(125, 128) if side == 0 else slice(0, 3)
            beside = left_at if side == 0 else right_at
            away = halo + 24 + 16 * side + col
            turn[...] = jnp.full((128, 128), fill, F32)
            turn[to, :] = got_ref[beside, 72:88, :][col : col + 3, :]
            ext[8:136, lanes] = turn[...].T
            turn[to, :] = up_ref[away : away + 3, :]
            ext[0:8, lanes] = turn[...].T[120:128, :]
            turn[to, :] = down_ref[away : away + 3, :]
            ext[136:144, lanes] = turn[...].T[0:8, :]
    source_ext[8:136, 128:384] = source_ref[...]
    for half in range(2):
        lanes = slice(128 + 128 * half, 256 + 128 * half)
        source_ext[6:8, lanes] = low_ref[edge + 2 * half : edge + 2 * half + 2, :]
        source_ext[136:138, lanes] = high_ref[edge + 2 * half : edge + 2 * half + 2, :]
    for side, lanes in ((0, slice(0, 128)), (1, slice(384, 512))):
        to = slice(126, 128) if side == 0 else slice(0, 2)
        ends = back_ref[left_at if side == 0 else right_at, 64:72, :]
        turn[...] = jnp.zeros((128, 128), F32)
        turn[to, :] = ends[0:2, :]
        source_ext[8:136, lanes] = turn[...].T
        source_ext[6:8, lanes] = ends[2:4, :]
        source_ext[136:138, lanes] = ends[4:6, :]
    row_id = gx * depth_ref.shape[0] - 8 + iota(shape, 0)
    col_id = gy * depth_ref.shape[1] - 128 + iota(shape, 1)
    row_open = (row_id >= 0) & (row_id + 1 < rows_total)
    col_open = (col_id >= 0) & (col_id + 1 < cols_total)
    bed = bed_ext[...]
    rough = rough_ext[...]
    inverse = {
        0: jnp.where(row_open, 2.0 / (rough + pltpu.roll(rough, shape[0] - 1, 0)), 0.0),
        1: jnp.where(col_open, 2.0 / (rough + pltpu.roll(rough, shape[1] - 1, 1)), 0.0),
    }
    head = depth_ext[...]
    source = source_ext[...]
    for _ in range(3):
        wet = jnp.maximum(head, 0.0)
        section = head + bed
        net = jnp.zeros(shape, F32) - source
        for axis in range(2):
            back = shape[axis] - 1
            slope = pltpu.roll(section, back, axis) - section
            mean = 0.5 * (wet + pltpu.roll(wet, back, axis))
            flux = (
                jnp.exp2((5.0 / 3.0) * jnp.log2(mean))
                * inverse[axis]
                * slope
                * lax.rsqrt(jnp.abs(slope) + SLOPE_FLOOR)
            )
            net = net + flux - pltpu.roll(flux, 1, axis)
        head = head + SURF_STEP * net
    out_ref[...] = head[8:136, 128:384]
    low_lane = iota((32, 128), 1) < 64
    slots = packed.shape[1]
    for number in range(slots // 128):
        lanes = slice(128 * number, 128 * number + 128)
        stay, moved = back_ref[number, 0:32, :], back_ref[number, 32:64, :]
        high, low = split(jnp.where(low_lane, stay, pltpu.roll(moved, 64, 1)))
        packed[0:32, lanes] = high
        packed[64:96, lanes] = low
        high, low = split(jnp.where(low_lane, pltpu.roll(stay, 64, 1), moved))
        packed[32:64, lanes] = high
        packed[96:128, lanes] = low
    load.wait()
    factors = [(ref, at) for ref in (factor_0, factor_1, factor_2) for at in range(ref.shape[0])]
    turned[:, 0:64, :] = jnp.zeros((TILE // 128, 64, 128), F32)
    stores = []
    for tile in range(blocks // TILE):
        wanted = as_bf16(iota((slots, TILE), 0) == slot_ref[:, TILE * tile : TILE * tile + TILE])
        flux = jnp.dot(packed[...], wanted, preferred_element_type=F32)
        flux = flux[0:64] + flux[64:128]
        for half in range(TILE // 128):
            for i in range(8):
                turned[half, pl.ds(64 + i, 8, stride=8), :] = flux[8 * i : 8 * i + 8, 128 * half : 128 * half + 128]
            ref, at = factors[tile * (TILE // 128) + half]
            turned[half, 64:128, :] = turned[half, 64:128, :] * ref[at]
            rows = slice(TILE * tile + 128 * half, TILE * tile + 128 * half + 128)
            slab[rows, :] = slab[rows, :] + turned[half].T
        rows = pl.ds(TILE * tile, TILE)
        store = pltpu.make_async_copy(slab.at[rows, :], new_ref.at[rows, top_lanes], stored.at[tile])
        store.start()
        stores.append(store)
    for store in stores:
        store.wait()


def finish(place, water_depth, *rest):
    shape = (144, 512)
    head = rest[-1]
    blocks = head.shape[0]
    return pl.pallas_call(
        functools.partial(sweep_kernel, place),
        in_specs=[VMEM] * 14 + [HBM],
        out_specs=[VMEM, HBM],
        out_shape=[
            jax.ShapeDtypeStruct(water_depth.shape, F32),
            pltpu.HBM(head.shape, F32),
        ],
        input_output_aliases={14: 1},
        scratch_shapes=[pltpu.VMEM(shape, F32)] * 4
        + [
            pltpu.VMEM((128, 128), F32),
            pltpu.VMEM((blocks, 128), F32),
            pltpu.VMEM((128, place[1] * 128), BF16),
            pltpu.VMEM((TILE // 128, 128, 128), F32),
            pltpu.SemaphoreType.DMA,
            pltpu.SemaphoreType.DMA((blocks // TILE,)),
        ],
        compiler_params=pltpu.CompilerParams(vmem_limit_bytes=VMEM_SHARE),
        name="finish",
    )(water_depth, *rest)


def halo_pieces(soil_ref, classes, source, slot, table, turned):
    pieces = []

    def turn(half):
        lanes = slice(128 * half, 128 * half + 128)
        turned[half] = source(lanes).T
        soil = soil_rows(soil_ref, classes(lanes))
        for face in range(6):
            late.append(functools.partial(part, half, face, soil))

    def part(half, face, soil):
        head = face_rows(turned, half, face)
        write_face(head, curve(head, soil)[0], half, face, slot, table)

    late = []
    for half in range(TILE // 128):
        turn(half)
    return pieces, late


def inner_pieces(soil_ref, classes, levels, source, slot, table, turned, cond, base_sc, factor_sc, top_ref):
    open_i = iota((8, 8, 128), 1) < 7
    nothing = jnp.zeros((1, 8, 128), F32)
    pieces, late = [], []

    def one(half):
        lanes = slice(128 * half, 128 * half + 128)
        at = 2 * (slot - 1) + half
        turned[half] = source(lanes).T
        soil = soil_rows(soil_ref, classes(lanes))
        width = cell_width(levels(lanes))
        half_over = 0.5 / width
        scaled = SUB_STEP / width
        state = {"below": None}

        def conduct(k):
            rows = slice(64 * k, 64 * k + 64)
            conductivity, base, ratio = curve(turned[half, rows, :], soil)
            cond[half, rows, :] = conductivity
            factor = scaled * base / (soil[4] * ratio + STORAGE * base)
            factor_sc[at, rows, :] = factor
            if k == 7:
                top_ref[at] = factor

        def flow(k):
            rows = slice(64 * k, 64 * k + 64)
            head = turned[half, rows, :].reshape(8, 8, 128)
            cnd = cond[half, rows, :].reshape(8, 8, 128)
            flux = (cnd + pltpu.roll(cnd, 7, 1)) * (pltpu.roll(head, 7, 1) - head) * half_over
            flux = jnp.where(open_i, flux, 0.0)
            inflow = flux - pltpu.roll(flux, 1, 1)
            flux = (cnd[1:] + cnd[:-1]) * (head[1:] - head[:-1]) * half_over
            inflow = inflow + jnp.concatenate([flux, nothing], 0) - jnp.concatenate([nothing, flux], 0)
            if k < 7:
                above = slice(64 * k + 64, 64 * k + 128)
                head_up = turned[half, above, :].reshape(8, 8, 128)
                cnd_up = cond[half, above, :].reshape(8, 8, 128)
                flux = (cnd + cnd_up) * ((head_up - head) * half_over + 0.5)
                inflow = inflow + flux
            if state["below"] is not None:
                inflow = inflow - state["below"]
            state["below"] = flux
            base_sc[at, rows, :] = (
                turned[half, rows, :] + factor_sc[at, rows, :] * inflow.reshape(64, 128)
            )

        pieces.append(functools.partial(conduct, 0))
        for k in range(8):
            if k < 7:
                pieces.append(functools.partial(conduct, k + 1))
            pieces.append(functools.partial(flow, k))
        for face in range(6):
            late.append(
                lambda face=face: write_face(
                    face_rows(turned, half, face), face_rows(cond, half, face), half, face, slot, table
                )
            )

    for half in range(TILE // 128):
        one(half)
    return pieces, late


def face_pieces(first_row, levels, near, slot, table, total, factor, out):
    halves = TILE // 128
    first = halves * (slot - 1)
    width = cell_width(levels)
    window = slice((slot - 1) * TILE, (slot + 2) * TILE)
    own = slice(slot * TILE, (slot + 1) * TILE)

    def one(face):
        neighbor = near(face)
        far_width = cell_width(near(6 + face))
        over_gap = 2.0 / (width + far_width)
        half = jnp.where(neighbor >= 0, 0.5, 0.0)
        row = jnp.where(neighbor >= 0, neighbor - first_row, -1)
        chosen = jnp.where(
            iota((3 * TILE, TILE), 0).astype(I16) == row.astype(I16), jnp.ones((), BF16), jnp.zeros((), BF16)
        )
        there = 256 * OPPOSITE[face]
        far = jnp.dot(table[there : there + 256, window], chosen, preferred_element_type=F32)
        here = table[256 * face : 256 * face + 256, own].astype(F32)
        head_diff = (far[0:64] - here[0:64]) + (far[64:128] - here[64:128])
        conds = (far[128:192] + here[128:192]) + (far[192:256] + here[192:256])
        flux = conds * half * (head_diff * over_gap + GRAVITY[face])
        for part in range(halves):
            at = first + part
            added = flux[:, 128 * part : 128 * part + 128]
            if face < 2:
                rows = pl.ds(7 * face, 64, stride=8)
                total[at, rows, :] += factor[at, rows, :] * added
            elif face < 4:
                for k in range(8):
                    rows = slice(64 * k + 56 * (face - 2), 64 * k + 56 * (face - 2) + 8)
                    total[at, rows, :] += factor[at, rows, :] * added[8 * k : 8 * k + 8]
            else:
                rows = slice(448 * (face - 4), 448 * (face - 4) + 64)
                total[at, rows, :] += factor[at, rows, :] * added

    def write():
        out([total[first + part].T for part in range(halves)])

    return [functools.partial(one, face) for face in range(6)] + [write]


def run_mixed(faces, pieces, late):
    done = 0
    for number, face in enumerate(faces):
        face()
        upto = -(-len(pieces) * (number + 1) // len(faces))
        for piece in pieces[done:upto]:
            piece()
        done = upto
    for piece in pieces[done:] + late:
        piece()


def cells_kernel(low, inner, tiles, width, has_edge, chained, *refs):
    soil_ref, class_any, level_any, near_any, pressure_ref, after_ref = refs[:6]
    edge_ref = refs[6] if has_edge else None
    (
        out_ref, top_any, table, turned, cond, base_sc, factor_sc, inbox, outbox, edge,
        class_ref, level_ref, near_ref, top_ref, arrived, stored, small,
    ) = refs[6 + has_edge + chained :]
    own, _, _ = position(width)
    loads, stores = [], []
    for number, (source, kept) in enumerate(((class_any, class_ref), (level_any, level_ref), (near_any, near_ref))):
        smalls = pltpu.make_async_copy(source, kept, small.at[number])
        smalls.start()
        loads.append(smalls)
    small_loads, loads = loads, []
    for slot in range(inner + 2):
        tile = low + slot - 1
        if 0 <= tile < tiles:
            rows = pl.ds(tile * TILE, TILE)
            load = pltpu.make_async_copy(pressure_ref.at[rows, :], inbox.at[slot], arrived.at[slot])
        else:
            load = pltpu.make_async_copy(edge_ref, edge, arrived.at[slot])
        load.start()
        loads.append(load)
    for load in small_loads:
        load.wait()

    def tile_lanes(ref, slot):
        start = (low + slot - 1) * TILE
        return lambda lanes: ref[:, start + lanes.start : start + lanes.stop]

    def around(slot):
        loads[slot].wait()
        if 0 <= low + slot - 1 < tiles:
            return halo_pieces(
                soil_ref, tile_lanes(class_ref, slot), lambda lanes: inbox[slot, lanes, :], slot, table,
                turned.at[slot % 2],
            )
        return halo_pieces(
            soil_ref,
            lambda lanes: edge[HB : HB + 8, lanes][0:1, :].astype(I32),
            lambda lanes: edge[lanes, :],
            slot, table, turned.at[slot % 2],
        )

    def within(slot):
        loads[slot].wait()
        return inner_pieces(
            soil_ref, tile_lanes(class_ref, slot), tile_lanes(level_ref, slot),
            lambda lanes: inbox[slot, lanes, :],
            slot, table, turned.at[slot % 2], cond.at[slot % 2], base_sc, factor_sc, top_ref,
        )

    def faces(slot):
        first_row = own * tiles * TILE + (low + slot - 2) * TILE
        start = (low + slot - 1) * TILE

        def near(row):
            return near_ref[row : row + 1, start : start + TILE]

        def out(halves):
            for number, value in enumerate(halves):
                outbox[slot - 1, 128 * number : 128 * number + 128, :] = value
            store = pltpu.make_async_copy(
                outbox.at[slot - 1], out_ref.at[pl.ds(start, TILE), :], stored.at[slot - 1]
            )
            store.start()
            stores.append(store)

        return face_pieces(
            first_row, level_ref[:, start : start + TILE], near, slot, table, base_sc, factor_sc, out
        )

    for step in range(inner + 3):
        if step == inner + 2:
            store = pltpu.make_async_copy(top_ref, top_any, small.at[3])
            store.start()
            stores.append(store)
        work = [], []
        if step in (0, inner + 1):
            work = around(step)
        elif step <= inner:
            work = within(step)
        run_mixed(faces(step - 2) if step >= 3 else [], *work)
    for store in stores:
        store.wait()


def cells(shape, soil, kinds, near, pressure, edge, after, part, head):
    tiles = pressure.shape[0] // TILE
    low, inner = PARTS[part]
    extra = [value for value in (edge, head) if value is not None]
    aliases = {} if head is None else {5 + len(extra): 0}
    return pl.pallas_call(
        functools.partial(
            cells_kernel, low, inner, tiles, shape[1], int(edge is not None), int(head is not None)
        ),
        in_specs=[SMEM, ANY, ANY, ANY, HBM, ANY] + [ANY] * (edge is not None) + [HBM] * (head is not None),
        out_specs=[HBM, ANY],
        out_shape=[
            pltpu.HBM(pressure.shape, F32),
            jax.ShapeDtypeStruct((2 * inner, 64, 128), F32),
        ],
        input_output_aliases=aliases,
        scratch_shapes=[
            pltpu.VMEM((1536, (inner + 2) * TILE), BF16),
            pltpu.VMEM((2, TILE // 128, 512, 128), F32),
            pltpu.VMEM((2, TILE // 128, 512, 128), F32),
            pltpu.VMEM((2 * inner, 512, 128), F32),
            pltpu.VMEM((2 * inner, 512, 128), F32),
            pltpu.VMEM((inner + 2, TILE, 512), F32),
            pltpu.VMEM((inner, TILE, 512), F32),
            pltpu.VMEM((HB + 8, 512), F32),
            pltpu.VMEM(kinds[0].shape, I32),
            pltpu.VMEM(kinds[1].shape, I32),
            pltpu.VMEM(near.shape, I32),
            pltpu.VMEM((2 * inner, 64, 128), F32),
            pltpu.SemaphoreType.DMA((inner + 2,)),
            pltpu.SemaphoreType.DMA((inner,)),
            pltpu.SemaphoreType.DMA((4,)),
        ],
        compiler_params=pltpu.CompilerParams(vmem_limit_bytes=VMEM_SHARE),
        cost_estimate=pl.CostEstimate(
            flops=inner * 6 * 2 * 256 * 256 * 768,
            bytes_accessed=inner * TILE * 512 * 16,
            transcendentals=inner * TILE * 512 * 8,
        ),
        name="cells",
    )(soil, *kinds, near, pltpu.with_memory_space_constraint(pressure, pltpu.HBM), after, *extra)


def shifted(value, axis, steps, wrap=True):
    count = lax.axis_size(axis)
    pairs = [(i, (i + steps) % count) for i in range(count) if wrap or 0 <= i + steps < count]
    return lax.ppermute(value, axis, pairs)


def per_device(pressure, soil_class, levels, neighbors, neighbor_levels, patch_of_block, soil_params,
               water_depth, bed_height, roughness):
    blocks = pressure.shape[0]
    rows, cols = water_depth.shape
    patches = rows // 8 * (cols // 8)
    shape = (lax.axis_size("gx"), lax.axis_size("gy"))
    width = shape[1]
    gy = lax.axis_index("gy")
    kinds = [value.reshape(1, blocks) for value in (soil_class, levels)]
    patch = patch_of_block.reshape(1, blocks)
    near = jnp.concatenate([neighbors.T, neighbor_levels.T], axis=0)

    send, slot, edge_rows = route(
        shape, kinds + [patch], pressure, water_depth, bed_height, roughness
    )
    later, class_later, send = lax.optimization_barrier((pressure, soil_class, send))

    def edge(part):
        classes = jnp.pad(class_later[part].astype(F32)[None], ((0, 7), (0, 512 - HB)))
        return jnp.concatenate([later[part], classes], axis=0)

    low_edge = shifted(edge(slice(blocks - HB, blocks)), ("gx", "gy"), 1, wrap=False)
    high_edge = shifted(edge(slice(0, HB)), ("gx", "gy"), -1, wrap=False)
    got = lax.all_to_all(send, "gy", 0, 0)
    halos = got[:, 72:88]
    west = lax.dynamic_index_in_dim(halos, jnp.maximum(gy - 1, 0), 0, keepdims=False)
    east = lax.dynamic_index_in_dim(halos, jnp.minimum(gy + 1, width - 1), 0, keepdims=False)
    moving = got[:, 32:72].reshape(40 * width, 128)
    up = jnp.concatenate([moving, edge_rows[1], west, east], axis=0)
    down = jnp.concatenate([moving, edge_rows[0], west, east], axis=0)
    from_low = shifted(up, "gx", 1)
    from_high = shifted(down, "gx", -1)
    head, top_1 = cells(shape, soil_params, kinds, near, pressure, None, up, 1, None)
    stay, back_high, back_low, tile, edge_cols = surface(
        shape, soil_params, got, from_low, from_high, water_depth, patches, top_1
    )
    back_high = shifted(back_high, "gx", -1)
    back_low = shifted(back_low, "gx", 1)
    head, top_0 = cells(shape, soil_params, kinds, near, pressure, low_edge, stay, 0, head)
    back_low, back_high, top_0 = lax.optimization_barrier((back_low, back_high, top_0))
    number = jnp.arange(width, dtype=I32)[:, None, None]
    answers = 32 * width
    moved = jnp.where(
        number >= gy,
        back_high[:answers].reshape(width, 32, 128),
        back_low[:answers].reshape(width, 32, 128),
    )

    def side(kind):
        lines = slice(answers + 2 * kind, answers + 2 * kind + 2)
        return jnp.concatenate(
            [edge_cols[kind, 0:2], back_low[lines], back_high[lines], jnp.zeros((2, 128), F32)], axis=0
        )

    sides = jnp.where(number == gy + 1, side(1)[None], side(0)[None])
    reply = jnp.concatenate([stay, moved, sides], axis=1)
    returned = lax.all_to_all(reply, "gy", 0, 0)
    head, top_2 = cells(shape, soil_params, kinds, near, pressure, high_edge, reply, 2, head)
    new_depth, new_pressure = finish(
        shape, water_depth, bed_height, roughness, got, from_low, from_high, tile,
        back_low, back_high, returned, slot, top_0, top_1, top_2, head,
    )
    return new_pressure, new_depth


def solution(mesh):
    blocks = P(("gx", "gy"))
    wide = P(("gx", "gy"), None)
    tile = P("gx", "gy")
    return jax.shard_map(
        per_device,
        mesh=mesh,
        in_specs=(wide, blocks, blocks, wide, wide, blocks, P(), tile, tile, tile),
        out_specs=(wide, tile),
        check_vma=False,
    )
```

```python
import functools

import jax
import jax.numpy as jnp
from jax import lax
from jax.experimental import pallas as pl
from jax.experimental.pallas import tpu as pltpu
from jax.sharding import PartitionSpec as P

F32 = jnp.float32
BF16 = jnp.bfloat16
I32 = jnp.int32
I16 = jnp.int16

HB = 256
TILE = 256
PARTS = ((0, 2), (2, 3), (5, 3))
SLOTS = 64
GROUPS = 16
STORAGE = 0.05
SUB_STEP = 0.02
SURF_STEP = 0.003
SLOPE_FLOOR = 0.01
OPPOSITE = (1, 0, 3, 2, 5, 4)
GRAVITY = (0.0, 0.0, 0.0, 0.0, -1.0, 1.0)
VMEM_LIMIT = 60 * 1024 * 1024
VMEM_SHARE = 32 * 1024 * 1024

VMEM = pl.BlockSpec(memory_space=pltpu.VMEM)
SMEM = pl.BlockSpec(memory_space=pltpu.SMEM)
ANY = pl.BlockSpec(memory_space=pl.ANY)
HBM = pl.BlockSpec(memory_space=pltpu.HBM)


def position(width):
    gx, gy = lax.axis_index("gx"), lax.axis_index("gy")
    return gx * width + gy, gx, gy


def split(value):
    high = value.astype(BF16)
    low = (value - high.astype(F32)).astype(BF16)
    return high, low


def iota(shape, dim):
    return lax.broadcasted_iota(I32, shape, dim)


def as_bf16(mask):
    return jnp.where(mask, 1.0, 0.0).astype(BF16)


def cell_width(levels):
    return jnp.where(levels == 0, 0.25, jnp.where(levels == 1, 0.5, 1.0)).astype(F32)


def soil_rows(soil_ref, classes):
    rows = []
    for row in range(5):
        value = jnp.full(classes.shape, soil_ref[row, 0], F32)
        for cls in range(1, soil_ref.shape[1]):
            value = jnp.where(classes == cls, soil_ref[row, cls], value)
        rows.append(value)
    residual, saturated, alpha, power, cond = rows
    exponent = 1.0 - 1.0 / power
    return alpha, power - 1.0, -0.5 * exponent, cond, (saturated - residual) * alpha * (exponent * power)


def curve(pressure, soil):
    alpha, lesser, half, _, _ = soil
    suction = alpha * jnp.maximum(-pressure, 0.0)
    powered = jnp.exp2(lesser * jnp.log2(suction))
    base = 1.0 + powered * suction
    root = jnp.exp2(half * jnp.log2(base))
    ratio = powered * (root * root)
    rest = 1.0 - ratio
    conductivity = soil[3] * root * (rest * rest)
    return conductivity, base, ratio


def face_rows(ref, half, face):
    if face < 2:
        return ref[half, pl.ds(7 * face, 64, stride=8), :]
    if face < 4:
        start = 56 * (face - 2)
        return jnp.concatenate([ref[half, 64 * k + start : 64 * k + start + 8, :] for k in range(8)], axis=0)
    start = 448 * (face - 4)
    return ref[half, start : start + 64, :]


def write_face(head, conductivity, half, face, slot, table):
    lanes = slice(slot * TILE + 128 * half, slot * TILE + 128 * half + 128)
    for part, value in enumerate(split(head) + split(conductivity)):
        row = 256 * face + 64 * part
        table[row : row + 64, lanes] = value


def route_kernel(shape, class_ref, level_ref, patch_ref, top_ref, depth_ref, bed_ref, rough_ref,
                 send_ref, slot_ref, rows_ref, turned, packed, edges):
    own, _, gy = position(shape[1])
    route_once(own, gy, shape, class_ref, level_ref, patch_ref, top_ref, depth_ref, bed_ref, rough_ref,
               slot_ref, rows_ref, turned, packed, edges)
    blocks = patch_ref.shape[1]
    low_lane = iota((32, 128), 1) < 64
    for number in range(send_ref.shape[0]):
        wanted = as_bf16(iota((128, blocks), 0) == slot_ref[...] - 128 * number)
        out = lax.dot_general(packed[...], wanted, (((1,), (1,)), ((), ())), preferred_element_type=F32)
        first = out[0:32] + out[64:96]
        second = out[32:64] + out[96:128]
        send_ref[number, 0:32, :] = jnp.where(low_lane, first, pltpu.roll(second, 64, 1))
        send_ref[number, 32:64, :] = jnp.where(low_lane, pltpu.roll(first, 64, 1), second)
        label = out[130:131] * (out[128:129] + 256.0 * out[129:130] + 1.0) - 1.0
        row = iota((8, 128), 0)
        send_ref[number, 64:72, :] = jnp.where(row == 0, label, jnp.where(row == 1, out[131:132], out[132:133]))
        send_ref[number, 72:88, :] = jnp.where(number == gy + 1, edges[1], edges[0])


def route_once(own, gy, shape, class_ref, level_ref, patch_ref, top_ref, depth_ref, bed_ref, rough_ref,
               slot_ref, rows_ref, turned, packed, edges):
    devices, width = shape[0] * shape[1], shape[1]
    blocks = patch_ref.shape[1]
    patch = patch_ref[...]
    is_top = patch >= 0
    safe = jnp.where(is_top, patch, 0)
    offset = lax.rem(lax.shift_right_logical(safe, 9) - own + (GROUPS // 2 - 1) + devices, devices) - (GROUPS // 2 - 1)
    column = gy + offset
    moved = (column < 0) | (column >= width)
    group = 2 * lax.rem(column + width, width) + moved.astype(I32)
    upper = as_bf16(iota((TILE, TILE), 0) < iota((TILE, TILE), 1))
    carry = jnp.zeros((GROUPS, 1), F32)
    for part in range(blocks // TILE):
        lanes = slice(part * TILE, (part + 1) * TILE)
        member = jnp.where(
            (iota((GROUPS, TILE), 0) == group[:, lanes]) & is_top[:, lanes], 1.0, 0.0
        )
        before = jnp.dot(member.astype(BF16), upper, preferred_element_type=F32) + carry
        rank = jnp.sum(member * before, axis=0, keepdims=True)
        carry = carry + jnp.sum(member, axis=1, keepdims=True)
        slot_ref[:, lanes] = jnp.where(
            is_top[:, lanes], group[:, lanes] * SLOTS + rank.astype(I32), -1
        )
        for half in (2 * part, 2 * part + 1):
            turned[half] = top_ref[128 * half : 128 * half + 128, :].T
    for half in range(blocks // 128):
        lanes = slice(128 * half, 128 * half + 128)
        heads = jnp.concatenate(
            [turned[half, pl.ds(64 + i, 8, stride=8), :] for i in range(8)], axis=0
        )
        high, low = split(heads)
        packed[0:64, lanes] = high
        packed[64:128, lanes] = low
    place = jnp.bitwise_and(safe, 511)
    row = iota((16, blocks), 0)
    tags = jnp.where(row == 0, jnp.bitwise_and(place, 255), 0)
    tags = jnp.where(row == 1, lax.shift_right_logical(place, 8), tags)
    tags = jnp.where(row == 2, 1, tags)
    tags = jnp.where(row == 3, class_ref[...], tags)
    tags = jnp.where(row == 4, level_ref[...], tags)
    packed[128:144, :] = tags.astype(F32).astype(BF16)
    for number, field in enumerate((depth_ref, bed_ref, rough_ref)):
        edges[0, 3 * number : 3 * number + 3, :] = field[:, 0:128].T[0:3, :]
        edges[1, 3 * number : 3 * number + 3, :] = field[:, 128:256].T[125:128, :]
        for half in range(2):
            at = 3 * (2 * number + half)
            lanes = slice(128 * half, 128 * half + 128)
            rows_ref[0, at : at + 3, :] = field[0:3, lanes]
            rows_ref[1, at : at + 3, :] = field[125:128, lanes]


def route(shape, kinds, pressure, water_depth, bed_height, roughness):
    blocks = pressure.shape[0]
    width = shape[1]
    row = pl.BlockSpec((1, blocks), lambda t: (0, 0))
    return pl.pallas_call(
        functools.partial(route_kernel, shape),
        grid=(1,),
        in_specs=[
            row,
            row,
            row,
            pl.BlockSpec((blocks, 128), lambda t: (0, 3)),
            pl.BlockSpec(water_depth.shape, lambda t: (0, 0)),
            pl.BlockSpec(water_depth.shape, lambda t: (0, 0)),
            pl.BlockSpec(water_depth.shape, lambda t: (0, 0)),
        ],
        out_specs=[
            pl.BlockSpec((width, 88, 128), lambda t: (0, 0, 0)),
            pl.BlockSpec((1, blocks), lambda t: (0, 0)),
            pl.BlockSpec((2, 24, 128), lambda t: (0, 0, 0)),
        ],
        out_shape=[
            jax.ShapeDtypeStruct((width, 88, 128), F32),
            jax.ShapeDtypeStruct((1, blocks), I32),
            jax.ShapeDtypeStruct((2, 24, 128), F32),
        ],
        scratch_shapes=[
            pltpu.VMEM((blocks // 128, 128, 128), F32),
            pltpu.VMEM((144, blocks), BF16),
            pltpu.VMEM((2, 16, 128), F32),
        ],
        compiler_params=pltpu.CompilerParams(vmem_limit_bytes=VMEM_LIMIT),
        name="route",
    )(*kinds, pressure, water_depth, bed_height, roughness)


def surface_kernel(shape, soil_ref, got_ref, up_ref, down_ref, depth_ref, after_ref,
                   stay_ref, back_high_ref, back_low_ref, tile_ref, cols_ref, packed, labels, match):
    _, _, gy = position(shape[1])
    low_lane = iota((32, 128), 1) < 64
    tag_low = iota((8, 128), 1) < 64
    width = got_ref.shape[0]
    slots = width * 128
    patches = match.shape[0]
    for source in range(width):
        lanes = slice(128 * source, 128 * source + 128)
        at = 40 * source
        from_up = source >= gy
        stay = got_ref[source, 0:32, :]
        moved = jnp.where(from_up, up_ref[at : at + 32, :], down_ref[at : at + 32, :])
        high, low = split(jnp.where(low_lane, stay, pltpu.roll(moved, 64, 1)))
        packed[0:32, lanes] = high
        packed[64:96, lanes] = low
        high, low = split(jnp.where(low_lane, pltpu.roll(stay, 64, 1), moved))
        packed[32:64, lanes] = high
        packed[96:128, lanes] = low
        tags = jnp.where(
            tag_low,
            got_ref[source, 64:72, :],
            jnp.where(from_up, up_ref[at + 32 : at + 40, :], down_ref[at + 32 : at + 40, :]),
        )
        labels[:, lanes] = (tags[0:1, :] + 0.5).astype(I32) - jnp.where(tags[0:1, :] < 0, 1, 0)
        row = iota((16, 128), 0)
        packed[128:144, lanes] = jnp.where(row == 0, tags[1:2, :], tags[2:3, :]).astype(BF16)
    for part in range(patches // 128):
        match[128 * part : 128 * part + 128, :] = as_bf16(
            iota((128, slots), 0) + 128 * part == labels[...]
        )
    placed = lax.dot_general(
        packed[...], match[...], (((1,), (1,)), ((), ())), preferred_element_type=F32
    )
    classes = (placed[128:129] + 0.5).astype(I32)
    levels = (placed[129:130] + 0.5).astype(I32)
    soil = soil_rows(soil_ref, classes)
    half_cell = 0.5 * cell_width(levels)
    head = placed[0:64] + placed[64:128]
    conductivity, _, _ = curve(head, soil)
    row_of = lax.shift_right_logical(iota((128, patches), 0), 3)
    own_row = row_of == lax.shift_right_logical(iota((128, patches), 1), 5)
    depth_high, depth_low = split(depth_ref[...])
    depth_both = jnp.concatenate([depth_high, depth_low], axis=0)
    cols = depth_ref.shape[1]
    pieces = []
    for i in range(8):
        pick = as_bf16(iota((cols, patches), 0) == 8 * jnp.bitwise_and(iota((cols, patches), 1), 31) + i)
        spread = jnp.dot(depth_both, pick, preferred_element_type=F32)
        spread = jnp.where(own_row, spread[0:128] + spread[128:256], 0.0)
        pieces.append(jnp.sum(spread.reshape(16, 8, patches), axis=0))
    depth = jnp.concatenate(pieces, axis=0)
    infiltration = jnp.minimum(
        conductivity / half_cell * (depth - (head - half_cell)), depth / (3.0 * SURF_STEP)
    )
    high, low = split(infiltration)
    both = jnp.concatenate([high, low], axis=0)
    answer = jnp.dot(both, match[...], preferred_element_type=F32)
    answer = answer[0:64] + answer[64:128]
    for source in range(width):
        lanes = slice(128 * source, 128 * source + 128)
        first, second = answer[0:32, lanes], answer[32:64, lanes]
        stay_ref[source] = jnp.where(low_lane, first, pltpu.roll(second, 64, 1))
        moved = jnp.where(low_lane, pltpu.roll(first, 64, 1), second)
        back_high_ref[32 * source : 32 * source + 32, :] = moved
        back_low_ref[32 * source : 32 * source + 32, :] = moved
    total = jnp.zeros(depth_ref.shape, F32)
    for i in range(8):
        pick = as_bf16(iota((patches, cols), 1) == 8 * jnp.bitwise_and(iota((patches, cols), 0), 31) + i)
        rows = jnp.concatenate([infiltration[8 * i : 8 * i + 8]] * 16, axis=0)
        high, low = split(jnp.where(own_row, rows, 0.0))
        spread = jnp.dot(jnp.concatenate([high, low], axis=0), pick, preferred_element_type=F32)
        total = total + (spread[0:128] + spread[128:256])
    tile_ref[...] = total
    base = 32 * width
    for half in range(2):
        lanes = slice(128 * half, 128 * half + 128)
        back_high_ref[base + 2 * half : base + 2 * half + 2, :] = total[0:2, lanes]
        back_low_ref[base + 2 * half : base + 2 * half + 2, :] = total[126:128, lanes]
    cols_ref[0, 0:2, :] = total[:, 0:128].T[0:2, :]
    cols_ref[1, 0:2, :] = total[:, 128:256].T[126:128, :]


def surface(shape, soil, got, up, down, water_depth, patches, after):
    width = got.shape[0]
    return pl.pallas_call(
        functools.partial(surface_kernel, shape),
        in_specs=[SMEM, VMEM, VMEM, VMEM, VMEM, ANY],
        out_specs=[VMEM] * 5,
        out_shape=[
            jax.ShapeDtypeStruct((width, 32, 128), F32),
            jax.ShapeDtypeStruct((32 * width + 8, 128), F32),
            jax.ShapeDtypeStruct((32 * width + 8, 128), F32),
            jax.ShapeDtypeStruct(water_depth.shape, F32),
            jax.ShapeDtypeStruct((2, 8, 128), F32),
        ],
        scratch_shapes=[
            pltpu.VMEM((144, width * 128), BF16),
            pltpu.VMEM((1, width * 128), I32),
            pltpu.VMEM((patches, width * 128), BF16),
        ],
        compiler_params=pltpu.CompilerParams(vmem_limit_bytes=VMEM_SHARE),
        name="surface",
    )(soil, got, up, down, water_depth, after)


def sweep_kernel(place, depth_ref, bed_ref, rough_ref, got_ref, up_ref, down_ref,
                 source_ref, low_ref, high_ref, back_ref, slot_ref, factor_0, factor_1, factor_2, head_ref,
                 out_ref, new_ref, depth_ext, bed_ext, rough_ext, source_ext, turn, slab, packed, turned, loaded, stored):
    blocks = slab.shape[0]
    top_lanes = pl.ds(384, 128)
    load = pltpu.make_async_copy(head_ref.at[:, top_lanes], slab, loaded)
    load.start()
    _, gx, gy = position(place[1])
    left_at, right_at = jnp.maximum(gy - 1, 0), jnp.minimum(gy + 1, place[1] - 1)
    rows_total, cols_total = depth_ref.shape[0] * place[0], depth_ref.shape[1] * place[1]
    shape = depth_ext.shape
    halo = 40 * got_ref.shape[0]
    edge = 32 * got_ref.shape[0]
    depth_ext[...] = jnp.zeros(shape, F32)
    bed_ext[...] = jnp.zeros(shape, F32)
    rough_ext[...] = jnp.ones(shape, F32)
    source_ext[...] = jnp.zeros(shape, F32)
    for number, (ext, field) in enumerate(
        ((depth_ext, depth_ref), (bed_ext, bed_ref), (rough_ext, rough_ref))
    ):
        ext[8:136, 128:384] = field[...]
        for half in range(2):
            at = 3 * (2 * number + half)
            lanes = slice(128 + 128 * half, 256 + 128 * half)
            ext[5:8, lanes] = up_ref[halo + at : halo + at + 3, :]
            ext[136:139, lanes] = down_ref[halo + at : halo + at + 3, :]
        col = 3 * number
        fill = 1.0 if number == 2 else 0.0
        for side, lanes in ((0, slice(0, 128)), (1, slice(384, 512))):
            to = slice(125, 128) if side == 0 else slice(0, 3)
            beside = left_at if side == 0 else right_at
            away = halo + 24 + 16 * side + col
            turn[...] = jnp.full((128, 128), fill, F32)
            turn[to, :] = got_ref[beside, 72:88, :][col : col + 3, :]
            ext[8:136, lanes] = turn[...].T
            turn[to, :] = up_ref[away : away + 3, :]
            ext[0:8, lanes] = turn[...].T[120:128, :]
            turn[to, :] = down_ref[away : away + 3, :]
            ext[136:144, lanes] = turn[...].T[0:8, :]
    source_ext[8:136, 128:384] = source_ref[...]
    for half in range(2):
        lanes = slice(128 + 128 * half, 256 + 128 * half)
        source_ext[6:8, lanes] = low_ref[edge + 2 * half : edge + 2 * half + 2, :]
        source_ext[136:138, lanes] = high_ref[edge + 2 * half : edge + 2 * half + 2, :]
    for side, lanes in ((0, slice(0, 128)), (1, slice(384, 512))):
        to = slice(126, 128) if side == 0 else slice(0, 2)
        ends = back_ref[left_at if side == 0 else right_at, 64:72, :]
        turn[...] = jnp.zeros((128, 128), F32)
        turn[to, :] = ends[0:2, :]
        source_ext[8:136, lanes] = turn[...].T
        source_ext[6:8, lanes] = ends[2:4, :]
        source_ext[136:138, lanes] = ends[4:6, :]
    row_id = gx * depth_ref.shape[0] - 8 + iota(shape, 0)
    col_id = gy * depth_ref.shape[1] - 128 + iota(shape, 1)
    row_open = (row_id >= 0) & (row_id + 1 < rows_total)
    col_open = (col_id >= 0) & (col_id + 1 < cols_total)
    bed = bed_ext[...]
    rough = rough_ext[...]
    inverse = {
        0: jnp.where(row_open, 2.0 / (rough + pltpu.roll(rough, shape[0] - 1, 0)), 0.0),
        1: jnp.where(col_open, 2.0 / (rough + pltpu.roll(rough, shape[1] - 1, 1)), 0.0),
    }
    head = depth_ext[...]
    source = source_ext[...]
    for _ in range(3):
        wet = jnp.maximum(head, 0.0)
        section = head + bed
        net = jnp.zeros(shape, F32) - source
        for axis in range(2):
            back = shape[axis] - 1
            slope = pltpu.roll(section, back, axis) - section
            mean = 0.5 * (wet + pltpu.roll(wet, back, axis))
            flux = (
                jnp.exp2((5.0 / 3.0) * jnp.log2(mean))
                * inverse[axis]
                * slope
                * lax.rsqrt(jnp.abs(slope) + SLOPE_FLOOR)
            )
            net = net + flux - pltpu.roll(flux, 1, axis)
        head = head + SURF_STEP * net
    out_ref[...] = head[8:136, 128:384]
    low_lane = iota((32, 128), 1) < 64
    slots = packed.shape[1]
    for number in range(slots // 128):
        lanes = slice(128 * number, 128 * number + 128)
        stay, moved = back_ref[number, 0:32, :], back_ref[number, 32:64, :]
        high, low = split(jnp.where(low_lane, stay, pltpu.roll(moved, 64, 1)))
        packed[0:32, lanes] = high
        packed[64:96, lanes] = low
        high, low = split(jnp.where(low_lane, pltpu.roll(stay, 64, 1), moved))
        packed[32:64, lanes] = high
        packed[96:128, lanes] = low
    load.wait()
    factors = [(ref, at) for ref in (factor_0, factor_1, factor_2) for at in range(ref.shape[0])]
    turned[:, 0:64, :] = jnp.zeros((TILE // 128, 64, 128), F32)
    stores = []
    for tile in range(blocks // TILE):
        wanted = as_bf16(iota((slots, TILE), 0) == slot_ref[:, TILE * tile : TILE * tile + TILE])
        flux = jnp.dot(packed[...], wanted, preferred_element_type=F32)
        flux = flux[0:64] + flux[64:128]
        for half in range(TILE // 128):
            for i in range(8):
                turned[half, pl.ds(64 + i, 8, stride=8), :] = flux[8 * i : 8 * i + 8, 128 * half : 128 * half + 128]
            ref, at = factors[tile * (TILE // 128) + half]
            turned[half, 64:128, :] = turned[half, 64:128, :] * ref[at]
            rows = slice(TILE * tile + 128 * half, TILE * tile + 128 * half + 128)
            slab[rows, :] = slab[rows, :] + turned[half].T
        rows = pl.ds(TILE * tile, TILE)
        store = pltpu.make_async_copy(slab.at[rows, :], new_ref.at[rows, top_lanes], stored.at[tile])
        store.start()
        stores.append(store)
    for store in stores:
        store.wait()


def finish(place, water_depth, *rest):
    shape = (144, 512)
    head = rest[-1]
    blocks = head.shape[0]
    return pl.pallas_call(
        functools.partial(sweep_kernel, place),
        in_specs=[VMEM] * 14 + [HBM],
        out_specs=[VMEM, HBM],
        out_shape=[
            jax.ShapeDtypeStruct(water_depth.shape, F32),
            pltpu.HBM(head.shape, F32),
        ],
        input_output_aliases={14: 1},
        scratch_shapes=[pltpu.VMEM(shape, F32)] * 4
        + [
            pltpu.VMEM((128, 128), F32),
            pltpu.VMEM((blocks, 128), F32),
            pltpu.VMEM((128, place[1] * 128), BF16),
            pltpu.VMEM((TILE // 128, 128, 128), F32),
            pltpu.SemaphoreType.DMA,
            pltpu.SemaphoreType.DMA((blocks // TILE,)),
        ],
        compiler_params=pltpu.CompilerParams(vmem_limit_bytes=VMEM_SHARE),
        name="finish",
    )(water_depth, *rest)


def halo_pieces(soil_ref, classes, source, slot, table, turned):
    pieces = []

    def turn(half):
        lanes = slice(128 * half, 128 * half + 128)
        turned[half] = source(lanes).T
        soil = soil_rows(soil_ref, classes(lanes))
        for face in range(6):
            late.append(functools.partial(part, half, face, soil))

    def part(half, face, soil):
        head = face_rows(turned, half, face)
        write_face(head, curve(head, soil)[0], half, face, slot, table)

    late = []
    for half in range(TILE // 128):
        turn(half)
    return pieces, late


def inner_pieces(soil_ref, classes, levels, source, slot, table, turned, cond, base_sc, factor_sc, top_ref):
    open_i = iota((8, 8, 128), 1) < 7
    nothing = jnp.zeros((1, 8, 128), F32)
    pieces, late = [], []

    def one(half):
        lanes = slice(128 * half, 128 * half + 128)
        at = 2 * (slot - 1) + half
        turned[half] = source(lanes).T
        soil = soil_rows(soil_ref, classes(lanes))
        width = cell_width(levels(lanes))
        half_over = 0.5 / width
        scaled = SUB_STEP / width
        state = {"below": None}

        def conduct(k):
            rows = slice(64 * k, 64 * k + 64)
            conductivity, base, ratio = curve(turned[half, rows, :], soil)
            cond[half, rows, :] = conductivity
            factor = scaled * base / (soil[4] * ratio + STORAGE * base)
            factor_sc[at, rows, :] = factor
            if k == 7:
                top_ref[at] = factor

        def flow(k):
            rows = slice(64 * k, 64 * k + 64)
            head = turned[half, rows, :].reshape(8, 8, 128)
            cnd = cond[half, rows, :].reshape(8, 8, 128)
            flux = (cnd + pltpu.roll(cnd, 7, 1)) * (pltpu.roll(head, 7, 1) - head) * half_over
            flux = jnp.where(open_i, flux, 0.0)
            inflow = flux - pltpu.roll(flux, 1, 1)
            flux = (cnd[1:] + cnd[:-1]) * (head[1:] - head[:-1]) * half_over
            inflow = inflow + jnp.concatenate([flux, nothing], 0) - jnp.concatenate([nothing, flux], 0)
            if k < 7:
                above = slice(64 * k + 64, 64 * k + 128)
                head_up = turned[half, above, :].reshape(8, 8, 128)
                cnd_up = cond[half, above, :].reshape(8, 8, 128)
                flux = (cnd + cnd_up) * ((head_up - head) * half_over + 0.5)
                inflow = inflow + flux
            if state["below"] is not None:
                inflow = inflow - state["below"]
            state["below"] = flux
            base_sc[at, rows, :] = (
                turned[half, rows, :] + factor_sc[at, rows, :] * inflow.reshape(64, 128)
            )

        pieces.append(functools.partial(conduct, 0))
        for k in range(8):
            if k < 7:
                pieces.append(functools.partial(conduct, k + 1))
            pieces.append(functools.partial(flow, k))
        for face in range(6):
            late.append(
                lambda face=face: write_face(
                    face_rows(turned, half, face), face_rows(cond, half, face), half, face, slot, table
                )
            )

    for half in range(TILE // 128):
        one(half)
    return pieces, late


def face_pieces(first_row, levels, near, slot, table, total, factor, out):
    halves = TILE // 128
    first = halves * (slot - 1)
    width = cell_width(levels)
    window = slice((slot - 1) * TILE, (slot + 2) * TILE)
    own = slice(slot * TILE, (slot + 1) * TILE)

    def one(face):
        neighbor = near(face)
        far_width = cell_width(near(6 + face))
        over_gap = 2.0 / (width + far_width)
        half = jnp.where(neighbor >= 0, 0.5, 0.0)
        row = jnp.where(neighbor >= 0, neighbor - first_row, -1)
        chosen = jnp.where(
            iota((3 * TILE, TILE), 0).astype(I16) == row.astype(I16), jnp.ones((), BF16), jnp.zeros((), BF16)
        )
        there = 256 * OPPOSITE[face]
        far = jnp.dot(table[there : there + 256, window], chosen, preferred_element_type=F32)
        here = table[256 * face : 256 * face + 256, own].astype(F32)
        head_diff = (far[0:64] - here[0:64]) + (far[64:128] - here[64:128])
        conds = (far[128:192] + here[128:192]) + (far[192:256] + here[192:256])
        flux = conds * half * (head_diff * over_gap + GRAVITY[face])
        for part in range(halves):
            at = first + part
            added = flux[:, 128 * part : 128 * part + 128]
            if face < 2:
                rows = pl.ds(7 * face, 64, stride=8)
                total[at, rows, :] += factor[at, rows, :] * added
            elif face < 4:
                for k in range(8):
                    rows = slice(64 * k + 56 * (face - 2), 64 * k + 56 * (face - 2) + 8)
                    total[at, rows, :] += factor[at, rows, :] * added[8 * k : 8 * k + 8]
            else:
                rows = slice(448 * (face - 4), 448 * (face - 4) + 64)
                total[at, rows, :] += factor[at, rows, :] * added

    def write():
        out([total[first + part].T for part in range(halves)])

    return [functools.partial(one, face) for face in range(6)] + [write]


def run_mixed(faces, pieces, late):
    done = 0
    for number, face in enumerate(faces):
        face()
        upto = -(-len(pieces) * (number + 1) // len(faces))
        for piece in pieces[done:upto]:
            piece()
        done = upto
    for piece in pieces[done:] + late:
        piece()


def cells_kernel(low, inner, tiles, width, has_edge, chained, *refs):
    soil_ref, class_any, level_any, near_any, pressure_ref, after_ref = refs[:6]
    edge_ref = refs[6] if has_edge else None
    (
        out_ref, top_any, table, turned, cond, base_sc, factor_sc, inbox, outbox, edge,
        class_ref, level_ref, near_ref, top_ref, arrived, stored, small,
    ) = refs[6 + has_edge + chained :]
    own, _, _ = position(width)
    loads, stores = [], []
    for number, (source, kept) in enumerate(((class_any, class_ref), (level_any, level_ref), (near_any, near_ref))):
        smalls = pltpu.make_async_copy(source, kept, small.at[number])
        smalls.start()
        loads.append(smalls)
    small_loads, loads = loads, []
    for slot in range(inner + 2):
        tile = low + slot - 1
        if 0 <= tile < tiles:
            rows = pl.ds(tile * TILE, TILE)
            load = pltpu.make_async_copy(pressure_ref.at[rows, :], inbox.at[slot], arrived.at[slot])
        else:
            load = pltpu.make_async_copy(edge_ref, edge, arrived.at[slot])
        load.start()
        loads.append(load)
    for load in small_loads:
        load.wait()

    def tile_lanes(ref, slot):
        start = (low + slot - 1) * TILE
        return lambda lanes: ref[:, start + lanes.start : start + lanes.stop]

    def around(slot):
        loads[slot].wait()
        if 0 <= low + slot - 1 < tiles:
            return halo_pieces(
                soil_ref, tile_lanes(class_ref, slot), lambda lanes: inbox[slot, lanes, :], slot, table,
                turned.at[slot % 2],
            )
        return halo_pieces(
            soil_ref,
            lambda lanes: edge[HB : HB + 8, lanes][0:1, :].astype(I32),
            lambda lanes: edge[lanes, :],
            slot, table, turned.at[slot % 2],
        )

    def within(slot):
        loads[slot].wait()
        return inner_pieces(
            soil_ref, tile_lanes(class_ref, slot), tile_lanes(level_ref, slot),
            lambda lanes: inbox[slot, lanes, :],
            slot, table, turned.at[slot % 2], cond.at[slot % 2], base_sc, factor_sc, top_ref,
        )

    def faces(slot):
        first_row = own * tiles * TILE + (low + slot - 2) * TILE
        start = (low + slot - 1) * TILE

        def near(row):
            return near_ref[row : row + 1, start : start + TILE]

        def out(halves):
            for number, value in enumerate(halves):
                outbox[slot - 1, 128 * number : 128 * number + 128, :] = value
            store = pltpu.make_async_copy(
                outbox.at[slot - 1], out_ref.at[pl.ds(start, TILE), :], stored.at[slot - 1]
            )
            store.start()
            stores.append(store)

        return face_pieces(
            first_row, level_ref[:, start : start + TILE], near, slot, table, base_sc, factor_sc, out
        )

    for step in range(inner + 3):
        if step == inner + 2:
            store = pltpu.make_async_copy(top_ref, top_any, small.at[3])
            store.start()
            stores.append(store)
        work = [], []
        if step in (0, inner + 1):
            work = around(step)
        elif step <= inner:
            work = within(step)
        run_mixed(faces(step - 2) if step >= 3 else [], *work)
    for store in stores:
        store.wait()


def cells(shape, soil, kinds, near, pressure, edge, after, part, head):
    tiles = pressure.shape[0] // TILE
    low, inner = PARTS[part]
    extra = [value for value in (edge, head) if value is not None]
    aliases = {} if head is None else {5 + len(extra): 0}
    return pl.pallas_call(
        functools.partial(
            cells_kernel, low, inner, tiles, shape[1], int(edge is not None), int(head is not None)
        ),
        in_specs=[SMEM, ANY, ANY, ANY, HBM, ANY] + [ANY] * (edge is not None) + [HBM] * (head is not None),
        out_specs=[HBM, ANY],
        out_shape=[
            pltpu.HBM(pressure.shape, F32),
            jax.ShapeDtypeStruct((2 * inner, 64, 128), F32),
        ],
        input_output_aliases=aliases,
        scratch_shapes=[
            pltpu.VMEM((1536, (inner + 2) * TILE), BF16),
            pltpu.VMEM((2, TILE // 128, 512, 128), F32),
            pltpu.VMEM((2, TILE // 128, 512, 128), F32),
            pltpu.VMEM((2 * inner, 512, 128), F32),
            pltpu.VMEM((2 * inner, 512, 128), F32),
            pltpu.VMEM((inner + 2, TILE, 512), F32),
            pltpu.VMEM((inner, TILE, 512), F32),
            pltpu.VMEM((HB + 8, 512), F32),
            pltpu.VMEM(kinds[0].shape, I32),
            pltpu.VMEM(kinds[1].shape, I32),
            pltpu.VMEM(near.shape, I32),
            pltpu.VMEM((2 * inner, 64, 128), F32),
            pltpu.SemaphoreType.DMA((inner + 2,)),
            pltpu.SemaphoreType.DMA((inner,)),
            pltpu.SemaphoreType.DMA((4,)),
        ],
        compiler_params=pltpu.CompilerParams(vmem_limit_bytes=VMEM_SHARE),
        cost_estimate=pl.CostEstimate(
            flops=inner * 6 * 2 * 256 * 256 * 768,
            bytes_accessed=inner * TILE * 512 * 16,
            transcendentals=inner * TILE * 512 * 8,
        ),
        name="cells",
    )(soil, *kinds, near, pltpu.with_memory_space_constraint(pressure, pltpu.HBM), after, *extra)


def shifted(value, axis, steps, wrap=True):
    count = lax.axis_size(axis)
    pairs = [(i, (i + steps) % count) for i in range(count) if wrap or 0 <= i + steps < count]
    return lax.ppermute(value, axis, pairs)


def per_device(pressure, soil_class, levels, neighbors, neighbor_levels, patch_of_block, soil_params,
               water_depth, bed_height, roughness):
    blocks = pressure.shape[0]
    rows, cols = water_depth.shape
    patches = rows // 8 * (cols // 8)
    shape = (lax.axis_size("gx"), lax.axis_size("gy"))
    width = shape[1]
    gy = lax.axis_index("gy")
    kinds = [value.reshape(1, blocks) for value in (soil_class, levels)]
    patch = patch_of_block.reshape(1, blocks)
    near = jnp.concatenate([neighbors.T, neighbor_levels.T], axis=0)

    send, slot, edge_rows = route(
        shape, kinds + [patch], pressure, water_depth, bed_height, roughness
    )
    later, class_later, send = lax.optimization_barrier((pressure, soil_class, send))

    def edge(part):
        classes = jnp.pad(class_later[part].astype(F32)[None], ((0, 7), (0, 512 - HB)))
        return jnp.concatenate([later[part], classes], axis=0)

    low_edge = shifted(edge(slice(blocks - HB, blocks)), ("gx", "gy"), 1, wrap=False)
    high_edge = shifted(edge(slice(0, HB)), ("gx", "gy"), -1, wrap=False)
    got = lax.all_to_all(send, "gy", 0, 0)
    halos = got[:, 72:88]
    west = lax.dynamic_index_in_dim(halos, jnp.maximum(gy - 1, 0), 0, keepdims=False)
    east = lax.dynamic_index_in_dim(halos, jnp.minimum(gy + 1, width - 1), 0, keepdims=False)
    moving = got[:, 32:72].reshape(40 * width, 128)
    up = jnp.concatenate([moving, edge_rows[1], west, east], axis=0)
    down = jnp.concatenate([moving, edge_rows[0], west, east], axis=0)
    from_low = shifted(up, "gx", 1)
    from_high = shifted(down, "gx", -1)
    head, top_1 = cells(shape, soil_params, kinds, near, pressure, None, up, 1, None)
    stay, back_high, back_low, tile, edge_cols = surface(
        shape, soil_params, got, from_low, from_high, water_depth, patches, top_1
    )
    back_high = shifted(back_high, "gx", -1)
    back_low = shifted(back_low, "gx", 1)
    head, top_0 = cells(shape, soil_params, kinds, near, pressure, low_edge, stay, 0, head)
    back_low, back_high, top_0 = lax.optimization_barrier((back_low, back_high, top_0))
    number = jnp.arange(width, dtype=I32)[:, None, None]
    answers = 32 * width
    moved = jnp.where(
        number >= gy,
        back_high[:answers].reshape(width, 32, 128),
        back_low[:answers].reshape(width, 32, 128),
    )

    def side(kind):
        lines = slice(answers + 2 * kind, answers + 2 * kind + 2)
        return jnp.concatenate(
            [edge_cols[kind, 0:2], back_low[lines], back_high[lines], jnp.zeros((2, 128), F32)], axis=0
        )

    sides = jnp.where(number == gy + 1, side(1)[None], side(0)[None])
    reply = jnp.concatenate([stay, moved, sides], axis=1)
    returned = lax.all_to_all(reply, "gy", 0, 0)
    head, top_2 = cells(shape, soil_params, kinds, near, pressure, high_edge, reply, 2, head)
    new_depth, new_pressure = finish(
        shape, water_depth, bed_height, roughness, got, from_low, from_high, tile,
        back_low, back_high, returned, slot, top_0, top_1, top_2, head,
    )
    return new_pressure, new_depth


def solution(mesh):
    blocks = P(("gx", "gy"))
    wide = P(("gx", "gy"), None)
    tile = P("gx", "gy")
    return jax.shard_map(
        per_device,
        mesh=mesh,
        in_specs=(wide, blocks, blocks, wide, wide, blocks, P(), tile, tile, tile),
        out_specs=(wide, tile),
        check_vma=False,
    )
```
